32 devices in a mesh: groups: 2 (over x), latent: 16 (over z, y, core).
Axes of the slice: x: 2, y: 2, z: 4, core: 2. Of those that a mesh axis runs over, the one named last changes fastest.
Arguments:
- x_rows: bfloat16 [32768, 3584], P(('groups', 'latent')), parts along dimension 0, may hold values from -6 to 6
- out_grad: bfloat16 [32768, 3584], P(('groups', 'latent')), parts along dimension 0, may hold values from -0.046875 to 0.046875
- enc_coef: bfloat16 [32768, 512], P(('groups', 'latent')), parts along dimension 0, may hold values from -0.0625 to 0.0625
- latent_act: bfloat16 [32768, 512], P(('groups', 'latent')), parts along dimension 0, may hold values from 0 to 1
- enc_w: float32 [1024, 3584], P(('groups', 'latent')), parts along dimension 0, may hold values from -0.036 to 0.036
- enc_m: float32 [1024, 3584], P(('groups', 'latent')), parts along dimension 0, may hold values from -0.18 to 0.18
- enc_v: float32 [1024, 3584], P(('groups', 'latent')), parts along dimension 0, may hold values from 0.0005 to 0.05
- dec_w: float32 [1024, 3584], P(('groups', 'latent')), parts along dimension 0, may hold values from -0.036 to 0.036
- dec_m: float32 [1024, 3584], P(('groups', 'latent')), parts along dimension 0, may hold values from -0.18 to 0.18
- dec_v: float32 [1024, 3584], P(('groups', 'latent')), parts along dimension 0, may hold values from 0.0005 to 0.05
- dead_order: int32 [32, 32], P(('groups', 'latent')), parts along dimension 0, may hold values from 0 to 31, each once within a row
- pick_rows: int32 [32, 16, 2], P(('groups', 'latent')), parts along dimension 0, may hold values from 0 to 1023
- send_count: int32 [32, 16], P(('groups', 'latent')), parts along dimension 0, may hold values from 0 to 2, as said below
Outputs:
- enc_w_out: float32 [1024, 3584], P(('groups', 'latent')), parts along dimension 0
- enc_m_out: float32 [1024, 3584], P(('groups', 'latent')), parts along dimension 0
- enc_v_out: float32 [1024, 3584], P(('groups', 'latent')), parts along dimension 0
- dec_w_out: float32 [1024, 3584], P(('groups', 'latent')), parts along dimension 0
- dec_m_out: float32 [1024, 3584], P(('groups', 'latent')), parts along dimension 0
- dec_v_out: float32 [1024, 3584], P(('groups', 'latent')), parts along dimension 0
- enc_full: bfloat16 [1024, 3584], P('groups'), parts along dimension 0
- dec_full: bfloat16 [1024, 3584], P('groups'), parts along dimension 0
The draws below stay inside these ranges and needn't reach their ends.
There are 2 independent parts, one for each index of `groups`. The reference program is written for one: setup_inputs(seed, part) draws one part's arguments, and reference() takes and returns one part's arrays. A program takes and returns all parts, laid end to end along the dimension named above; each array names one. Nothing has to cross between parts.
Inputs may be any that keep to these rules, and one draw needn't show every extreme that they name: `send_count`: column d counts the rows that owner d receives; each column sums to at most 32, and some column reaches 32 in every draw.
All inputs are finite; a program needn't handle non-finite values.
Results may differ from the reference program's by a relative error of at most 0.015.
Values may be sent and summed in bfloat16 or wider, within the bound.
No kernel may reach another device: no remote copies, remote signals or barrier semaphores. Data moves between devices by JAX's collectives and lax.ppermute only.
A program may use at most 128 MiB of HBM per device.

```python
import math
import jax
import jax.numpy as jnp
from jax import lax

D = 3584
L_DEV = 32
CAP = 2
TOK_DEV = 1024
LAT = 512
TOKENS = 16384
N_LATENT = 16


def draw_send_count(key, part):
    key = jax.random.fold_in(key, 11)
    key_raw, key_busy, key_quota, key_begin = jax.random.split(key, 4)
    owners = N_LATENT
    raw_counts = jax.random.randint(key_raw, (owners, owners), 0, CAP + 1)
    busiest = jax.random.randint(key_busy, (), 0, owners)
    columns = jnp.arange(owners)
    raw_counts = jnp.where(columns[None, :] == busiest, CAP, raw_counts)
    quota = jax.random.randint(key_quota, (owners,), L_DEV // 4, 3 * L_DEV // 4 + 1)
    quota = jnp.where(columns == busiest, L_DEV, quota)
    begins = jax.random.randint(key_begin, (owners,), 0, owners)
    order_pos = (columns[:, None] - begins[None, :]) % owners
    earlier = (order_pos[:, None, :] <= order_pos[None, :, :]).astype(jnp.int32)
    upto = jnp.sum(raw_counts[:, None, :] * earlier, axis=0)
    before = upto - raw_counts
    counts = jnp.minimum(upto, quota[None, :]) - jnp.minimum(before, quota[None, :])
    return counts.astype(jnp.int32)


def touch_ends(values, own_key, smallest, largest):
    spot = [jax.random.randint(jax.random.fold_in(own_key, axis), (), 0, length) for axis, length in enumerate(values.shape)]
    main_axis = values.shape.index(max(values.shape))
    beside = spot[:main_axis] + [(spot[main_axis] + 1) % values.shape[main_axis]] + spot[main_axis + 1:]
    return values.at[tuple(spot)].set(smallest).at[tuple(beside)].set(largest)


def raised(drawn, rng, source, target, shards_of, factor):
    def block_of(position):
        return (jnp.arange(drawn.shape[position]) // (drawn.shape[position] // shards_of)).reshape((-1,) + (1,) * (drawn.ndim - 1 - position))

    near = jax.random.permutation(rng, shards_of)[block_of(target)]
    second = (block_of(target) + shards_of // 2) % shards_of
    return jnp.where((block_of(source) == near) | (block_of(source) == second), factor * drawn, drawn)


def shard_levels(rng, extent, cuts, least, high):
    loudness, own = 1.0, jax.random.fold_in(rng, 6)
    for axis_at, parts in cuts:
        draws = jnp.exp(jax.random.uniform(jax.random.fold_in(own, axis_at), (parts,), jnp.float32, least / len(cuts), high / len(cuts)))
        loudness = loudness * jnp.repeat(draws, extent[axis_at] // parts).reshape([-1 if axis == axis_at else 1 for axis in range(len(extent))])
    return loudness


def gaussian(stream_key, dims, scale, limit, cuts=(), dtype=jnp.bfloat16):
    result = jax.random.normal(stream_key, dims, jnp.float32) * scale
    if len(cuts) > 0:
        result = shard_levels(stream_key, dims, cuts, -0.22, 0.18) * result
    return jnp.clip(result, min=-limit, max=limit).astype(dtype)


def bell_draw_with(stream_key, shape, deviation, bound, pieces, heavy, dtype=jnp.bfloat16):
    entries = deviation * jax.random.normal(stream_key, shape, jnp.float32)
    if pieces:
        entries = entries * shard_levels(stream_key, shape, pieces, -0.22, 0.18)
    return jnp.clip(raised(entries, jax.random.fold_in(stream_key, 3), *heavy), -bound, bound).astype(dtype)


def setup_inputs(seed: int = 0, part: int = 0) -> dict:
    keys = jax.random.split(jax.random.key(seed), 14)
    part_splits = jax.random.split(jax.random.fold_in(keys[13], part), 14)
    return {
        "x_rows": gaussian(part_splits[0], (TOKENS, D), 1.0, 6.0, ((0, 16),)),
        "out_grad": gaussian(part_splits[1], (TOKENS, D), TOKENS ** -0.5, 0.046875, ((0, 16),)),
        "enc_coef": bell_draw_with(part_splits[2], (TOKENS, LAT), TOKENS ** -0.5, 0.0625, ((0, 16),), (0, 1, 16, 2.0)),
        "latent_act": jnp.clip(1.0 * jax.random.uniform(part_splits[3], (TOKENS, LAT), jnp.float32) ** shard_levels(part_splits[3], (TOKENS, LAT), ((0, 16),), -0.2, 0.2), 0.0, 1.0).astype(jnp.bfloat16),
        "enc_w": gaussian(part_splits[4], (LAT, D), 0.006, 0.036, ((0, 16),), jnp.float32),
        "enc_m": gaussian(part_splits[5], (LAT, D), 0.03, 0.18, ((0, 16),), jnp.float32),
        "enc_v": jnp.clip(jnp.exp(math.log(0.05) - 4.6051702 * jax.random.uniform(part_splits[6], (LAT, D), jnp.float32) ** shard_levels(part_splits[6], (LAT, D), ((0, 16),), -0.2, 0.2)), 0.0005, 0.05),
        "dec_w": gaussian(part_splits[7], (LAT, D), 0.006, 0.036, ((0, 16),), jnp.float32),
        "dec_m": gaussian(part_splits[8], (LAT, D), 0.03, 0.18, ((0, 16),), jnp.float32),
        "dec_v": jnp.clip(jnp.exp(math.log(0.05) - 4.6051702 * jax.random.uniform(part_splits[9], (LAT, D), jnp.float32) ** shard_levels(part_splits[9], (LAT, D), ((0, 16),), -0.2, 0.2)), 0.0005, 0.05),
        "dead_order": jax.vmap(lambda own: jax.random.permutation(own, L_DEV))(jax.random.split(part_splits[10], N_LATENT)).reshape((N_LATENT, L_DEV)).astype(jnp.int32),
        "pick_rows": touch_ends(jax.random.randint(part_splits[11], (N_LATENT, N_LATENT, CAP), 0, TOK_DEV), jax.random.fold_in(part_splits[11], 1), 0, TOK_DEV - 1).astype(jnp.int32),
        "send_count": draw_send_count(jax.random.fold_in(jax.random.fold_in(keys[13], part), 71), part),
    }


beta_one = 0.9
beta_two = 0.99
first_fix = 1.0 - 0.9 ** 4
second_fix = 1.0 - 0.99 ** 4
learn_rate = 0.02
adam_eps = 1e-08
reset_gain = 0.01
norm_eps = 1e-06

def adam_update(weight, moment, second, gradient):
    moment_new = beta_one * moment + (1.0 - beta_one) * gradient
    second_new = beta_two * second + (1.0 - beta_two) * gradient * gradient
    weight_new = weight - learn_rate * (moment_new / first_fix) / (jnp.sqrt(second_new / second_fix) + adam_eps)
    return (weight_new, moment_new, second_new)

def reset_shard(arrived, arrived_counts, dead_list, states):
    enc_weight, enc_moment, enc_second, dec_weight, dec_moment, dec_second = states
    sources = arrived_counts.shape[0]
    per_source = arrived.shape[0] // sources
    latents = enc_weight.shape[0]
    offsets = jnp.cumsum(arrived_counts) - arrived_counts
    within = jnp.tile(jnp.arange(per_source), sources)
    slot_rank = jnp.repeat(offsets, per_source) + within
    slot_live = within < jnp.repeat(arrived_counts, per_source)
    dead_total = jnp.sum(arrived_counts)
    positions = jnp.arange(latents)
    in_use = positions < dead_total
    chooser = ((slot_rank[None, :] == positions[:, None]) & slot_live[None, :] & in_use[:, None]).astype(jnp.float32)
    fresh_rows = jnp.dot(chooser, arrived.astype(jnp.float32), precision=lax.Precision.HIGHEST)
    placing = ((dead_list[:, None] == positions[None, :]) & in_use[:, None]).astype(jnp.float32)
    is_reset = (lax.optimization_barrier(jnp.sum(placing, axis=0)) > 0.5)[:, None]
    placed = jnp.dot(placing.T, fresh_rows, precision=lax.Precision.HIGHEST)
    enc_fresh = reset_gain * placed * lax.rsqrt(lax.optimization_barrier(jnp.mean(placed * placed, axis=1, keepdims=True)) + norm_eps)
    enc_weight = jnp.where(is_reset, enc_fresh, enc_weight)
    enc_moment = jnp.where(is_reset, 0.0, enc_moment)
    enc_second = jnp.where(is_reset, 0.0, enc_second)
    dec_weight = jnp.where(is_reset, placed, dec_weight)
    dec_moment = jnp.where(is_reset, 0.0, dec_moment)
    dec_second = jnp.where(is_reset, 0.0, dec_second)
    dec_weight = dec_weight * lax.rsqrt(lax.optimization_barrier(jnp.mean(dec_weight * dec_weight, axis=1, keepdims=True)) + norm_eps)
    return (enc_weight, enc_moment, enc_second, dec_weight, dec_moment, dec_second)

def reference(x_rows, out_grad, enc_coef, latent_act, enc_w, enc_m, enc_v, dec_w, dec_m, dec_v, dead_order, pick_rows, send_count):
    x_blocks = x_rows.reshape(N_LATENT, TOK_DEV, D)
    grad_blocks = out_grad.reshape(N_LATENT, TOK_DEV, D)
    coef_blocks = enc_coef.reshape(N_LATENT, TOK_DEV, LAT)
    act_blocks = latent_act.reshape(N_LATENT, TOK_DEV, LAT)

    def add_block(running, blocks):
        coef_block, x_block, act_block, grad_block = blocks
        enc_part = jnp.dot(coef_block.T, x_block, preferred_element_type=jnp.float32).astype(jnp.bfloat16)
        dec_part = jnp.dot(act_block.T, grad_block, preferred_element_type=jnp.float32).astype(jnp.bfloat16)
        enc_part, dec_part = lax.optimization_barrier((enc_part, dec_part))
        return ((running[0] + enc_part.astype(jnp.float32), running[1] + dec_part.astype(jnp.float32)), None)
    empty = jnp.zeros((LAT, D), jnp.float32)
    sums, unused = lax.scan(add_block, (empty, empty), (coef_blocks, x_blocks, act_blocks, grad_blocks))
    enc_grad, dec_grad = sums
    enc_new = adam_update(enc_w, enc_m, enc_v, enc_grad)
    dec_new = adam_update(dec_w, dec_m, dec_v, dec_grad)
    chosen = x_blocks[jnp.arange(N_LATENT)[:, None, None], pick_rows]
    arrived = jnp.transpose(chosen, (1, 0, 2, 3)).reshape(N_LATENT, N_LATENT * CAP, D)
    states = tuple((item.reshape(N_LATENT, L_DEV, D) for item in enc_new + dec_new))
    results = jax.vmap(reset_shard)(arrived, send_count.T, dead_order, states)
    outputs = tuple((item.reshape(LAT, D) for item in results))
    enc_out, enc_mo, enc_vo, dec_out, dec_mo, dec_vo = outputs
    return (enc_out, enc_mo, enc_vo, dec_out, dec_mo, dec_vo, enc_out.astype(jnp.bfloat16), dec_out.astype(jnp.bfloat16))
```

```python
import functools

import jax
import jax.numpy as jnp
from jax import lax
from jax.experimental import pallas as pl
from jax.experimental.pallas import tpu as pltpu
from jax.sharding import PartitionSpec as P

beta_one = 0.9
beta_two = 0.99
first_fix = 1.0 - 0.9**4
second_fix = 1.0 - 0.99**4
learn_rate = 0.02
adam_eps = 1e-08
reset_gain = 0.01
norm_eps = 1e-06


def adam_update(weight, moment, second, gradient):
    moment_new = beta_one * moment + (1.0 - beta_one) * gradient
    second_new = beta_two * second + (1.0 - beta_two) * gradient * gradient
    weight_new = weight - learn_rate * (moment_new / first_fix) / (
        jnp.sqrt(second_new / second_fix) + adam_eps
    )
    return (weight_new, moment_new, second_new)


def reset_shard(arrived, arrived_counts, dead_list, states):
    enc_weight, enc_moment, enc_second, dec_weight, dec_moment, dec_second = states
    sources = arrived_counts.shape[0]
    per_source = arrived.shape[0] // sources
    latents = enc_weight.shape[0]
    offsets = jnp.cumsum(arrived_counts) - arrived_counts
    within = jnp.tile(jnp.arange(per_source), sources)
    slot_rank = jnp.repeat(offsets, per_source) + within
    slot_live = within < jnp.repeat(arrived_counts, per_source)
    dead_total = jnp.sum(arrived_counts)
    positions = jnp.arange(latents)
    in_use = positions < dead_total
    chooser = (
        (slot_rank[None, :] == positions[:, None]) & slot_live[None, :] & in_use[:, None]
    ).astype(jnp.float32)
    fresh_rows = jnp.dot(chooser, arrived.astype(jnp.float32), precision=lax.Precision.HIGHEST)
    placing = ((dead_list[:, None] == positions[None, :]) & in_use[:, None]).astype(jnp.float32)
    is_reset = (jnp.sum(placing, axis=0) > 0.5)[:, None]
    placed = jnp.dot(placing.T, fresh_rows, precision=lax.Precision.HIGHEST)
    enc_fresh = (
        reset_gain * placed * lax.rsqrt(jnp.mean(placed * placed, axis=1, keepdims=True) + norm_eps)
    )
    enc_weight = jnp.where(is_reset, enc_fresh, enc_weight)
    enc_moment = jnp.where(is_reset, 0.0, enc_moment)
    enc_second = jnp.where(is_reset, 0.0, enc_second)
    dec_weight = jnp.where(is_reset, placed, dec_weight)
    dec_moment = jnp.where(is_reset, 0.0, dec_moment)
    dec_second = jnp.where(is_reset, 0.0, dec_second)
    dec_weight = dec_weight * lax.rsqrt(
        jnp.mean(dec_weight * dec_weight, axis=1, keepdims=True) + norm_eps
    )
    return (enc_weight, enc_moment, enc_second, dec_weight, dec_moment, dec_second)


def swap(value, bits, size):
    return lax.ppermute(value, "latent", [(i, i ^ bits) for i in range(size)])


def relative_rows(coef, owners, rows):
    latents = coef.shape[1]
    wanted = (owners[:, None] * rows + jnp.arange(rows)[None, :]).reshape(-1)
    pick = (wanted[:, None] == jnp.arange(latents)[None, :]).astype(coef.dtype)
    return lax.dot_general(
        pick, coef, (((1,), (1,)), ((), ())), preferred_element_type=jnp.float32
    ).astype(coef.dtype)


def owned_gradient(left, right, rows, size):
    depth = size // 4
    half, quarter = depth * 2 * rows, depth * rows

    def part(begin, count):
        return jnp.dot(
            left[begin : begin + count], right, preferred_element_type=jnp.float32
        )

    from_core = swap(part(0, half).astype(jnp.bfloat16), 1, size)
    to_y = part(half, quarter) + from_core[:quarter].astype(jnp.float32)
    from_y = swap(to_y.astype(jnp.bfloat16), 2, size)
    mine = (
        part(half + quarter, quarter)
        + from_core[quarter:].astype(jnp.float32)
    ).astype(jnp.bfloat16)
    total = mine.astype(jnp.float32) + from_y.astype(jnp.float32)
    sent = total.astype(jnp.bfloat16)
    gradient = total[:rows]
    for k in range(1, depth):
        gradient = gradient + swap(sent[k * rows : (k + 1) * rows], 4 * k, size).astype(
            jnp.float32
        )
    return gradient


def place_kernel(plan, rows, *refs):
    pieces, whole, sems = refs[: len(plan)], refs[len(plan)], refs[len(plan) + 1]
    me = lax.axis_index("latent")
    copies = []
    for piece, keys in zip(pieces, plan):
        for i, key in enumerate(keys):
            start = pl.multiple_of((me ^ key) * rows, rows)
            copies.append(
                pltpu.make_async_copy(
                    piece.at[pl.ds(i * rows, rows)],
                    whole.at[pl.ds(start, rows)],
                    sems.at[len(copies)],
                )
            )
    for copy in copies:
        copy.start()
    for copy in copies:
        copy.wait()


def gathered(block, size):
    rows, width = block.shape
    depth = size // 4
    z_keys = [4 * k for k in range(1, depth)]
    near = jnp.concatenate([swap(block, key, size) for key in z_keys], axis=0)
    pieces = [(block, [0]), (near, z_keys)]
    pieces += [(swap(value, 2, size), [key ^ 2 for key in keys]) for value, keys in pieces]
    pieces += [(swap(value, 1, size), [key ^ 1 for key in keys]) for value, keys in pieces]
    plan = [keys for _, keys in pieces]
    return pl.pallas_call(
        functools.partial(place_kernel, plan, rows),
        out_shape=jax.ShapeDtypeStruct((size * rows, width), block.dtype),
        in_specs=[pl.BlockSpec(memory_space=pl.ANY)] * len(pieces),
        out_specs=pl.BlockSpec(memory_space=pl.ANY),
        scratch_shapes=[pltpu.SemaphoreType.DMA((size,))],
        name="place",
    )(*[value for value, _ in pieces])


def shards(
    x_rows,
    out_grad,
    enc_coef,
    latent_act,
    enc_w,
    enc_m,
    enc_v,
    dec_w,
    dec_m,
    dec_v,
    dead_order,
    pick_rows,
    send_count,
):
    width = x_rows.shape[1]
    rows = enc_w.shape[0]
    size = lax.axis_size("latent")
    depth = size // 4
    me = lax.axis_index("latent")
    keys = jnp.array(
        [4 * kz + 2 * ky + kc for kc in (1, 0) for ky in (1, 0) for kz in range(depth)],
        jnp.int32,
    )
    owners = me ^ keys
    enc_grad = owned_gradient(relative_rows(enc_coef, owners, rows), x_rows, rows, size)
    dec_grad = owned_gradient(relative_rows(latent_act, owners, rows), out_grad, rows, size)
    enc_new = adam_update(enc_w, enc_m, enc_v, enc_grad)
    dec_new = adam_update(dec_w, dec_m, dec_v, dec_grad)
    chosen = x_rows[pick_rows[0]]
    arrived = lax.all_to_all(chosen, "latent", split_axis=0, concat_axis=0, tiled=True)
    arrived_counts = lax.all_to_all(
        send_count[0], "latent", split_axis=0, concat_axis=0, tiled=True
    )
    results = reset_shard(
        arrived.reshape(-1, width), arrived_counts, dead_order[0], enc_new + dec_new
    )
    enc_out, enc_mo, enc_vo, dec_out, dec_mo, dec_vo = results
    enc_full = gathered(enc_out.astype(jnp.bfloat16), size)
    dec_full = gathered(dec_out.astype(jnp.bfloat16), size)
    return (enc_out, enc_mo, enc_vo, dec_out, dec_mo, dec_vo, enc_full, dec_full)


def solution(mesh):
    split = P(("groups", "latent"), None)
    placed = (split,) * 11 + (P(("groups", "latent"), None, None), split)
    return jax.shard_map(
        shards,
        mesh=mesh,
        in_specs=placed,
        out_specs=(split,) * 6 + (P("groups", None),) * 2,
        check_vma=False,
    )
```

```python
import functools

import jax
import jax.numpy as jnp
from jax import lax
from jax.experimental import pallas as pl
from jax.experimental.pallas import tpu as pltpu
from jax.sharding import PartitionSpec as P

beta_one = 0.9
beta_two = 0.99
first_fix = 1.0 - 0.9**4
second_fix = 1.0 - 0.99**4
learn_rate = 0.02
adam_eps = 1e-08
reset_gain = 0.01
norm_eps = 1e-06

KEPT = -1
ABSENT = -2


def adam_update(weight, moment, second, gradient):
    moment_new = beta_one * moment + (1.0 - beta_one) * gradient
    second_new = beta_two * second + (1.0 - beta_two) * gradient * gradient
    weight_new = weight - learn_rate * (moment_new / first_fix) / (
        jnp.sqrt(second_new / second_fix) + adam_eps
    )
    return (weight_new, moment_new, second_new)


def inverse_rms(value):
    return lax.rsqrt(jnp.mean(value * value, axis=1, keepdims=True) + norm_eps)


def swap(value, bits, size):
    return lax.ppermute(value, "latent", [(i, i ^ bits) for i in range(size)])


def cost(flops, moved):
    return pl.CostEstimate(flops=int(flops), bytes_accessed=int(moved), transcendentals=0)


def slot_key(slot, depth):
    core = 1 - slot // (2 * depth)
    y = 1 - (slot // depth) % 2
    return 4 * (slot % depth) + 2 * y + core


def gather_table(row, size):
    table = row
    step = 1
    while step < size:
        near = [table]
        for k in range(1, 4 if step * 2 < size else 2):
            near.append(swap(table, step * k, size))
        table = jnp.concatenate(near, axis=0)
        step *= len(near)
    return table


def ordered_coef(coef, wanted):
    latents = coef.shape[1]
    columns = lax.broadcasted_iota(jnp.int32, (latents, latents), 1)
    pick = (wanted == columns).astype(coef.dtype)
    return lax.dot_general(
        pick, coef, (((1,), (1,)), ((), ())), preferred_element_type=jnp.float32
    ).astype(coef.dtype)


def slot_rows(size, rows):
    row = lax.broadcasted_iota(jnp.int32, (size * rows, 1), 0)
    return slot_key(row // rows, size // 4), row % rows


def order_kernel(size, rows, coef_ref, out_ref):
    key, local = slot_rows(size, rows)
    owner = lax.axis_index("latent") ^ key
    out_ref[...] = ordered_coef(coef_ref[...], owner * rows + local)


def select_kernel(size, rows, table_ref, picks_ref, coef_ref, out_ref, code_ref):
    me = lax.axis_index("latent")
    cap = picks_ref.shape[0]
    key, local = slot_rows(size, rows)
    counts = table_ref[:, :size]
    order = table_ref[:, size:]
    source = me ^ lax.broadcasted_iota(jnp.int32, (size, 1), 0)
    before = jnp.sum(jnp.where(source < me, counts, 0), axis=0, keepdims=True)
    total = jnp.sum(counts, axis=0, keepdims=True)
    owners = lax.broadcasted_iota(jnp.int32, (size, size), 1) == source

    def by_key(row):
        return jnp.sum(jnp.where(owners, row, 0), axis=1, keepdims=True)

    begin, here = by_key(before), by_key(counts[:1])
    place = lax.broadcasted_iota(jnp.int32, (size, rows), 1)
    token = jnp.full((size, rows), ABSENT, jnp.int32)
    for c in range(cap):
        own = (place == begin + c) & (here > c)
        token = jnp.where(own, by_key(picks_ref[c : c + 1]), token)
    token = jnp.where(place < by_key(total), token, KEPT)
    spread = (lax.broadcasted_iota(jnp.int32, (size * rows, size), 1) == key).astype(jnp.float32)

    def by_row(table):
        return jnp.dot(
            spread, table.astype(jnp.float32), precision=lax.Precision.HIGHEST
        )

    is_latent = by_row(order) == local.astype(jnp.float32)
    code = jnp.sum(jnp.where(is_latent, by_row(token), 0.0), axis=1, keepdims=True)
    code = (code + jnp.where(code < 0, -0.5, 0.5)).astype(jnp.int32)
    code_ref[...] = code
    ordered = ordered_coef(coef_ref[...], (me ^ key) * rows + local)
    tokens = lax.broadcasted_iota(jnp.int32, ordered.shape, 1)
    out_ref[...] = jnp.where(code == KEPT, ordered, (tokens == code).astype(ordered.dtype))


def order_call(coef, size, rows):
    tokens, latents = coef.shape
    return pl.pallas_call(
        functools.partial(order_kernel, size, rows),
        out_shape=jax.ShapeDtypeStruct((latents, tokens), coef.dtype),
        cost_estimate=cost(2 * latents * latents * tokens, 4 * latents * tokens),
        name="order",
    )(coef)


def select_call(table, picks, coef, size, rows):
    tokens, latents = coef.shape
    return pl.pallas_call(
        functools.partial(select_kernel, size, rows),
        out_shape=(
            jax.ShapeDtypeStruct((latents, tokens), coef.dtype),
            jax.ShapeDtypeStruct((latents, 1), jnp.int32),
        ),
        cost_estimate=cost(4 * latents * latents * tokens, 4 * latents * tokens),
        name="select",
    )(table, picks, coef)


def product_kernel(left_ref, right_ref, sent_ref, kept_ref):
    half = sent_ref.shape[0]
    right = right_ref[...]
    for ref, begin in ((sent_ref, 0), (kept_ref, half)):
        ref[...] = jnp.dot(
            left_ref[begin : begin + half], right, preferred_element_type=jnp.float32
        ).astype(ref.dtype)


def product(left, right, begin, width):
    latents, tokens = left.shape
    tile = 256
    half = latents // 2
    out = jax.ShapeDtypeStruct((half, width), left.dtype)
    return pl.pallas_call(
        product_kernel,
        grid=(width // tile,),
        in_specs=[
            pl.BlockSpec((latents, tokens), lambda j: (0, 0)),
            pl.BlockSpec((tokens, tile), lambda j: (0, j + begin // tile)),
        ],
        out_specs=(pl.BlockSpec((half, tile), lambda j: (0, j)),) * 2,
        out_shape=(out, out),
        cost_estimate=cost(
            2 * latents * tokens * width, 2 * (latents * tokens + (latents + tokens) * width)
        ),
        name="product",
    )(left, right)


def chunk_parts(left, right, begin, width, rows, size):
    depth = size // 4
    quarter = depth * rows
    sent, kept = product(left, right, begin, width)
    from_core = swap(sent, 1, size)
    wide = jnp.float32
    to_y = (kept[:quarter].astype(wide) + from_core[:quarter].astype(wide)).astype(kept.dtype)
    from_y = swap(to_y, 2, size)
    total = (
        kept[quarter:].astype(wide) + from_core[quarter:].astype(wide) + from_y.astype(wide)
    ).astype(kept.dtype)
    parts = [total[k * rows : (k + 1) * rows] for k in range(depth)]
    return [parts[0]] + [swap(parts[k], 4 * k, size) for k in range(1, depth)]


def read_gradient(refs, depth):
    sums = []
    for begin in range(0, len(refs), depth):
        total = refs[begin][...].astype(jnp.float32)
        for ref in refs[begin + 1 : begin + depth]:
            total = total + ref[...].astype(jnp.float32)
        sums.append(total)
    return jnp.concatenate(sums, axis=1)


def enc_kernel(depth, code_ref, w_ref, m_ref, v_ref, *refs):
    parts, (w_out, m_out, v_out, block, fresh) = refs[:-5], refs[-5:]
    gradient = read_gradient(parts, depth)
    reset = code_ref[...] != KEPT
    w, m, v = adam_update(w_ref[...], m_ref[...], v_ref[...], gradient)
    w = jnp.where(reset, reset_gain * gradient * inverse_rms(gradient), w)
    w_out[...] = w
    m_out[...] = jnp.where(reset, 0.0, m)
    v_out[...] = jnp.where(reset, 0.0, v)
    block[...] = w.astype(block.dtype)
    fresh[...] = gradient.astype(fresh.dtype)


def dec_kernel(depth, code_ref, w_ref, m_ref, v_ref, fresh_ref, *refs):
    parts, (w_out, m_out, v_out, block) = refs[:-4], refs[-4:]
    reset = code_ref[...] != KEPT
    w, m, v = adam_update(w_ref[...], m_ref[...], v_ref[...], read_gradient(parts, depth))
    w = jnp.where(reset, fresh_ref[...].astype(jnp.float32), w)
    w = w * inverse_rms(w)
    w_out[...] = w
    m_out[...] = jnp.where(reset, 0.0, m)
    v_out[...] = jnp.where(reset, 0.0, v)
    block[...] = w.astype(block.dtype)


def update(kernel, code, states, fresh, parts, size, extra, name):
    rows, width = states[0].shape
    depth = size // 4
    tile = 16
    own_slot = 3 * depth

    def row_block(columns):
        return pl.BlockSpec((tile, columns), lambda i: (i, 0))

    code_spec = pl.BlockSpec((tile, 1), lambda i: (i + own_slot * rows // tile, 0))
    operands = list(states) + list(fresh) + list(parts)
    wide = jax.ShapeDtypeStruct((rows, width), jnp.float32)
    narrow = jax.ShapeDtypeStruct((rows, width), jnp.bfloat16)
    return pl.pallas_call(
        functools.partial(kernel, depth),
        grid=(rows // tile,),
        in_specs=[code_spec] + [row_block(value.shape[1]) for value in operands],
        out_specs=(row_block(width),) * (3 + extra),
        out_shape=(wide,) * 3 + (narrow,) * extra,
        cost_estimate=cost(40 * rows * width, 40 * rows * width),
        name=name,
    )(code, *operands)


def place_kernel(keys, rows, *refs):
    count = len(keys)
    whole, stage, sems_in, sems_out = refs[-4:]
    pieces = refs[:count]
    me = lax.axis_index("latent")
    first = [
        pltpu.make_async_copy(piece, stage.at[i], sems_in.at[i])
        for i, piece in enumerate(pieces)
    ]
    second = []
    for i, key in enumerate(keys):
        start = pl.multiple_of((me ^ key) * rows, rows)
        second.append(
            pltpu.make_async_copy(stage.at[i], whole.at[pl.ds(start, rows)], sems_out.at[i])
        )
    for copy in first:
        copy.start()
    for before, after in zip(first, second):
        before.wait()
        after.start()
    for copy in second:
        copy.wait()


def place(pieces, size, prior=None):
    keys = [key for key, _ in pieces]
    blocks = [block for _, block in pieces]
    rows, width = blocks[0].shape
    dtype = blocks[0].dtype
    count = len(keys)
    operands = blocks + ([] if prior is None else [prior])
    return pl.pallas_call(
        functools.partial(place_kernel, keys, rows),
        out_shape=jax.ShapeDtypeStruct((size * rows, width), dtype),
        in_specs=[pl.BlockSpec(memory_space=pl.ANY)] * len(operands),
        out_specs=pl.BlockSpec(memory_space=pl.ANY),
        scratch_shapes=[
            pltpu.VMEM((count, rows, width), dtype),
            pltpu.SemaphoreType.DMA((count,)),
            pltpu.SemaphoreType.DMA((count,)),
        ],
        input_output_aliases={} if prior is None else {count: 0},
        cost_estimate=cost(0, 4 * count * rows * width),
        name="place",
    )(*operands)


def gathered(block, size):
    depth = size // 4
    near = [(0, block)] + [(4 * k, swap(block, 4 * k, size)) for k in range(1, depth)]
    near += [(key ^ 2, swap(value, 2, size)) for key, value in near]
    far = [(key ^ 1, swap(value, 1, size)) for key, value in near]
    return place(far, size, place(near, size))


def shards(
    x_rows,
    out_grad,
    enc_coef,
    latent_act,
    enc_w,
    enc_m,
    enc_v,
    dec_w,
    dec_m,
    dec_v,
    dead_order,
    pick_rows,
    send_count,
):
    width = x_rows.shape[1]
    rows = enc_w.shape[0]
    size = lax.axis_size("latent")
    half = width // 2
    table = gather_table(jnp.concatenate([send_count, dead_order], axis=1), size)
    dec_left = order_call(latent_act, size, rows)
    dec_parts = chunk_parts(dec_left, out_grad, 0, half, rows, size)
    enc_left, code = select_call(table, pick_rows[0].T, enc_coef, size, rows)
    enc_parts = chunk_parts(enc_left, x_rows, 0, half, rows, size)
    enc_parts += chunk_parts(enc_left, x_rows, half, half, rows, size)
    dec_parts += chunk_parts(dec_left, out_grad, half, half, rows, size)
    enc_out, enc_mo, enc_vo, enc_block, fresh = update(
        enc_kernel, code, (enc_w, enc_m, enc_v), (), enc_parts, size, 2, "enc_update"
    )
    enc_full = gathered(enc_block, size)
    dec_out, dec_mo, dec_vo, dec_block = update(
        dec_kernel, code, (dec_w, dec_m, dec_v), (fresh,), dec_parts, size, 1, "dec_update"
    )
    dec_full = gathered(dec_block, size)
    return (enc_out, enc_mo, enc_vo, dec_out, dec_mo, dec_vo, enc_full, dec_full)


def solution(mesh):
    split = P(("groups", "latent"), None)
    placed = (split,) * 11 + (P(("groups", "latent"), None, None), split)
    return jax.shard_map(
        shards,
        mesh=mesh,
        in_specs=placed,
        out_specs=(split,) * 6 + (P("groups", None),) * 2,
        check_vma=False,
    )
```

```python
import functools

import jax
import jax.numpy as jnp
from jax import lax
from jax.experimental import pallas as pl
from jax.experimental.pallas import tpu as pltpu
from jax.sharding import PartitionSpec as P

beta_one = 0.9
beta_two = 0.99
first_fix = 1.0 - 0.9**4
second_fix = 1.0 - 0.99**4
learn_rate = 0.02
adam_eps = 1e-08
reset_gain = 0.01
norm_eps = 1e-06

KEPT = -1
ABSENT = -2


def adam_update(weight, moment, second, gradient):
    moment_new = beta_one * moment + (1.0 - beta_one) * gradient
    second_new = beta_two * second + (1.0 - beta_two) * gradient * gradient
    weight_new = weight - learn_rate * (moment_new / first_fix) / (
        jnp.sqrt(second_new / second_fix) + adam_eps
    )
    return (weight_new, moment_new, second_new)


def inverse_rms(value):
    return lax.rsqrt(jnp.mean(value * value, axis=1, keepdims=True) + norm_eps)


def swap(value, bits, size):
    return lax.ppermute(value, "latent", [(i, i ^ bits) for i in range(size)])


def cost(flops, moved):
    return pl.CostEstimate(flops=int(flops), bytes_accessed=int(moved), transcendentals=0)


def chip_at(position, chips):
    return jnp.where(position < chips // 2, 2 * position, 2 * (chips - 1 - position) + 1)


def position_of(chip, chips):
    return jnp.where(chip % 2 == 0, chip // 2, chips - 1 - chip // 2)


def owner_at(offset, other_core, size):
    me = lax.axis_index("latent")
    chips = size // 2
    position = lax.rem(position_of(me // 2, chips) + offset + chips, chips)
    return 2 * chip_at(position, chips) + ((me % 2) ^ other_core)


def shift(value, step, size):
    chips = size // 2
    ring = [2 * q for q in range(chips // 2)] + [2 * q + 1 for q in reversed(range(chips // 2))]
    pairs = [
        (2 * ring[p] + core, 2 * ring[(p + step) % chips] + core)
        for p in range(chips)
        for core in range(2)
    ]
    return lax.ppermute(value, "latent", pairs)


def slot_offset(slot, chips):
    far = chips // 2 - slot // 2
    return jnp.where(slot % 2 == 0, far, 1 - far)


def gather_table(row, size):
    table = row
    step = 1
    while step < size:
        near = [table]
        for k in range(1, 4 if step * 2 < size else 2):
            near.append(swap(table, step * k, size))
        table = jnp.concatenate(near, axis=0)
        step *= len(near)
    return table


def ordered_coef(coef, wanted):
    latents = coef.shape[1]
    columns = lax.broadcasted_iota(jnp.int32, (latents, latents), 1)
    pick = (wanted == columns).astype(coef.dtype)
    return lax.dot_general(
        pick, coef, (((1,), (1,)), ((), ())), preferred_element_type=jnp.float32
    ).astype(coef.dtype)


def slot_rows(size, rows):
    chips = size // 2
    row = lax.broadcasted_iota(jnp.int32, (size * rows, 1), 0)
    block = row // rows
    group, inside = block // chips, block % chips
    slot = group * (chips // 2) + inside % (chips // 2)
    other_core = 1 - inside // (chips // 2)
    return owner_at(slot_offset(slot, chips), other_core, size), row % rows


def order_kernel(size, rows, coef_ref, out_ref):
    owner, local = slot_rows(size, rows)
    out_ref[...] = ordered_coef(coef_ref[...], owner * rows + local)


def select_kernel(size, rows, table_ref, picks_ref, coef_ref, out_ref, code_ref):
    me = lax.axis_index("latent")
    cap = picks_ref.shape[0]
    owner, local = slot_rows(size, rows)
    counts = table_ref[:, :size]
    order = table_ref[:, size:]
    source = me ^ lax.broadcasted_iota(jnp.int32, (size, 1), 0)
    before = jnp.sum(jnp.where(source < me, counts, 0), axis=0, keepdims=True)
    total = jnp.sum(counts, axis=0, keepdims=True)
    owners = lax.broadcasted_iota(jnp.int32, (size, size), 1) == source

    def by_key(row):
        return jnp.sum(jnp.where(owners, row, 0), axis=1, keepdims=True)

    begin, here = by_key(before), by_key(counts[:1])
    place = lax.broadcasted_iota(jnp.int32, (size, rows), 1)
    token = jnp.full((size, rows), ABSENT, jnp.int32)
    for c in range(cap):
        own = (place == begin + c) & (here > c)
        token = jnp.where(own, by_key(picks_ref[c : c + 1]), token)
    token = jnp.where(place < by_key(total), token, KEPT)
    spread = (lax.broadcasted_iota(jnp.int32, (size * rows, size), 1) == (owner ^ me)).astype(jnp.float32)

    def by_row(table):
        return jnp.dot(
            spread, table.astype(jnp.float32), precision=lax.Precision.HIGHEST
        )

    is_latent = by_row(order) == local.astype(jnp.float32)
    code = jnp.sum(jnp.where(is_latent, by_row(token), 0.0), axis=1, keepdims=True)
    code = (code + jnp.where(code < 0, -0.5, 0.5)).astype(jnp.int32)
    code_ref[...] = code
    ordered = ordered_coef(coef_ref[...], owner * rows + local)
    tokens = lax.broadcasted_iota(jnp.int32, ordered.shape, 1)
    out_ref[...] = jnp.where(code == KEPT, ordered, (tokens == code).astype(ordered.dtype))


def order_call(coef, size, rows):
    tokens, latents = coef.shape
    return pl.pallas_call(
        functools.partial(order_kernel, size, rows),
        out_shape=jax.ShapeDtypeStruct((latents, tokens), coef.dtype),
        cost_estimate=cost(2 * latents * latents * tokens, 4 * latents * tokens),
        name="order",
    )(coef)


def select_call(table, picks, coef, size, rows):
    tokens, latents = coef.shape
    return pl.pallas_call(
        functools.partial(select_kernel, size, rows),
        out_shape=(
            jax.ShapeDtypeStruct((latents, tokens), coef.dtype),
            jax.ShapeDtypeStruct((latents, 1), jnp.int32),
        ),
        cost_estimate=cost(4 * latents * latents * tokens, 4 * latents * tokens),
        name="select",
    )(table, picks, coef)


def product_kernel(left_ref, right_ref, sent_ref, kept_ref):
    half = sent_ref.shape[0]
    out = jnp.dot(left_ref[...], right_ref[...], preferred_element_type=jnp.float32)
    sent_ref[...] = out[:half].astype(sent_ref.dtype)
    kept_ref[...] = out[half:].astype(kept_ref.dtype)


def product(left, right, group):
    latents, tokens = left.shape
    width = right.shape[1]
    tile = 896
    half = latents // 4
    out = jax.ShapeDtypeStruct((half, width), left.dtype)
    return pl.pallas_call(
        product_kernel,
        grid=(width // tile,),
        in_specs=[
            pl.BlockSpec((2 * half, tokens), lambda j: (group, 0)),
            pl.BlockSpec((tokens, tile), lambda j: (0, j)),
        ],
        out_specs=(pl.BlockSpec((half, tile), lambda j: (0, j)),) * 2,
        out_shape=(out, out),
        cost_estimate=cost(
            latents * tokens * width, 2 * tokens * width + latents * (tokens + width)
        ),
        name="product",
    )(left, right)


def owned_parts(left, right, rows, size):
    chips = size // 2
    slots = chips // 2
    kept, from_core = [], []
    for group in range(2):
        sent, own = product(left, right, group)
        kept.append(own)
        from_core.append(swap(sent, 1, size))

    def term(slot):
        begin = slot % slots * rows
        return sum(
            half[slot // slots][begin : begin + rows].astype(jnp.float32)
            for half in (kept, from_core)
        )

    def travel(first, step):
        moving = term(first).astype(jnp.bfloat16)
        for slot in range(first + 2, chips - 1, 2):
            came = shift(moving, step, size).astype(jnp.float32)
            moving = (came + term(slot)).astype(jnp.bfloat16)
        return shift(moving, step, size)

    return [kept[1], from_core[1], travel(0, 1), travel(1, -1)]


def read_gradient(refs):
    return sum(ref[...].astype(jnp.float32) for ref in refs)


def enc_kernel(code_ref, w_ref, m_ref, v_ref, *refs):
    parts, (w_out, m_out, v_out, block, fresh) = refs[:-5], refs[-5:]
    gradient = read_gradient(parts)
    reset = code_ref[...] != KEPT
    w, m, v = adam_update(w_ref[...], m_ref[...], v_ref[...], gradient)
    w = jnp.where(reset, reset_gain * gradient * inverse_rms(gradient), w)
    w_out[...] = w
    m_out[...] = jnp.where(reset, 0.0, m)
    v_out[...] = jnp.where(reset, 0.0, v)
    block[...] = w.astype(block.dtype)
    fresh[...] = gradient.astype(fresh.dtype)


def dec_kernel(code_ref, w_ref, m_ref, v_ref, fresh_ref, *refs):
    parts, (w_out, m_out, v_out, block) = refs[:-4], refs[-4:]
    reset = code_ref[...] != KEPT
    w, m, v = adam_update(w_ref[...], m_ref[...], v_ref[...], read_gradient(parts))
    w = jnp.where(reset, fresh_ref[...].astype(jnp.float32), w)
    w = w * inverse_rms(w)
    w_out[...] = w
    m_out[...] = jnp.where(reset, 0.0, m)
    v_out[...] = jnp.where(reset, 0.0, v)
    block[...] = w.astype(block.dtype)


def update(kernel, code, states, fresh, parts, extra, name):
    rows, width = states[0].shape
    tile = 16

    def last_rows(value):
        skipped = (value.shape[0] - rows) // tile
        return pl.BlockSpec((tile, value.shape[1]), lambda i: (i + skipped, 0))

    operands = [code] + list(states) + list(fresh) + list(parts)
    out_spec = pl.BlockSpec((tile, width), lambda i: (i, 0))
    wide = jax.ShapeDtypeStruct((rows, width), jnp.float32)
    narrow = jax.ShapeDtypeStruct((rows, width), jnp.bfloat16)
    return pl.pallas_call(
        kernel,
        grid=(rows // tile,),
        in_specs=[last_rows(value) for value in operands],
        out_specs=(out_spec,) * (3 + extra),
        out_shape=(wide,) * 3 + (narrow,) * extra,
        cost_estimate=cost(40 * rows * width, 40 * rows * width),
        name=name,
    )(*operands)


def place_kernel(owners, size, rows, *refs):
    count = len(owners)
    pieces, (whole, sems) = refs[:count], refs[-2:]
    copies = []
    for i, (offset, other_core) in enumerate(owners):
        start = pl.multiple_of(owner_at(offset, other_core, size) * rows, rows)
        copies.append(
            pltpu.make_async_copy(pieces[i], whole.at[pl.ds(start, rows)], sems.at[i])
        )
    for copy in copies:
        copy.start()
    for copy in copies:
        copy.wait()


def place(pieces, other_core, size, prior=None):
    owners = [(offset, other_core) for offset, _ in pieces]
    blocks = [block for _, block in pieces]
    rows, width = blocks[0].shape
    dtype = blocks[0].dtype
    count = len(blocks)
    in_specs = [pl.BlockSpec(memory_space=pltpu.VMEM)] * count
    if prior is not None:
        in_specs.append(pl.BlockSpec(memory_space=pl.ANY))
    return pl.pallas_call(
        functools.partial(place_kernel, owners, size, rows),
        out_shape=jax.ShapeDtypeStruct((size * rows, width), dtype),
        in_specs=in_specs,
        out_specs=pl.BlockSpec(memory_space=pl.ANY),
        scratch_shapes=[pltpu.SemaphoreType.DMA((count,))],
        input_output_aliases={} if prior is None else {count: 0},
        cost_estimate=cost(0, 4 * count * rows * width),
        name="place",
    )(*blocks, *([] if prior is None else [prior]))


def gathered(block, size):
    chips = size // 2
    near = [(0, block)]
    for step, hops in ((1, chips // 2), (-1, (chips - 1) // 2)):
        moving = block
        for hop in range(1, hops + 1):
            moving = shift(moving, step, size)
            near.append((-step * hop, moving))
    far = [(offset, swap(value, 1, size)) for offset, value in near]
    return place(far, 1, size, place(near, 0, size))


def shards(
    x_rows,
    out_grad,
    enc_coef,
    latent_act,
    enc_w,
    enc_m,
    enc_v,
    dec_w,
    dec_m,
    dec_v,
    dead_order,
    pick_rows,
    send_count,
):
    rows = enc_w.shape[0]
    size = lax.axis_size("latent")
    table = gather_table(jnp.concatenate([send_count, dead_order], axis=1), size)
    dec_parts = owned_parts(order_call(latent_act, size, rows), out_grad, rows, size)
    enc_left, code = select_call(table, pick_rows[0].T, enc_coef, size, rows)
    enc_parts = owned_parts(enc_left, x_rows, rows, size)
    enc_out, enc_mo, enc_vo, enc_block, fresh = update(
        enc_kernel, code, (enc_w, enc_m, enc_v), (), enc_parts, 2, "enc_update"
    )
    enc_full = gathered(enc_block, size)
    dec_out, dec_mo, dec_vo, dec_block = update(
        dec_kernel, code, (dec_w, dec_m, dec_v), (fresh,), dec_parts, 1, "dec_update"
    )
    dec_full = gathered(dec_block, size)
    return (enc_out, enc_mo, enc_vo, dec_out, dec_mo, dec_vo, enc_full, dec_full)


def solution(mesh):
    split = P(("groups", "latent"), None)
    placed = (split,) * 11 + (P(("groups", "latent"), None, None), split)
    return jax.shard_map(
        shards,
        mesh=mesh,
        in_specs=placed,
        out_specs=(split,) * 6 + (P("groups", None),) * 2,
        check_vma=False,
    )
```

```python
import functools

import jax
import jax.numpy as jnp
from jax import lax
from jax.experimental import pallas as pl
from jax.experimental.pallas import tpu as pltpu
from jax.sharding import PartitionSpec as P

beta_one = 0.9
beta_two = 0.99
first_fix = 1.0 - 0.9**4
second_fix = 1.0 - 0.99**4
learn_rate = 0.02
adam_eps = 1e-08
reset_gain = 0.01
norm_eps = 1e-06

KEPT = -1
ABSENT = -2


def adam_update(weight, moment, second, gradient):
    moment_new = beta_one * moment + (1.0 - beta_one) * gradient
    second_new = beta_two * second + (1.0 - beta_two) * gradient * gradient
    weight_new = weight - learn_rate * (moment_new / first_fix) / (
        jnp.sqrt(second_new / second_fix) + adam_eps
    )
    return (weight_new, moment_new, second_new)


def inverse_rms(value):
    return lax.rsqrt(jnp.mean(value * value, axis=1, keepdims=True) + norm_eps)


def swap(value, bits, size):
    return lax.ppermute(value, "latent", [(i, i ^ bits) for i in range(size)])


def after(value, *others):
    return lax.optimization_barrier((value,) + others)[0]


def params(mebibytes):
    return pltpu.CompilerParams(vmem_limit_bytes=mebibytes * 2**20)


def cost(flops, moved):
    return pl.CostEstimate(flops=int(flops), bytes_accessed=int(moved), transcendentals=0)


def chip_at(position, chips):
    return jnp.where(position < chips // 2, 2 * position, 2 * (chips - 1 - position) + 1)


def position_of(chip, chips):
    return jnp.where(chip % 2 == 0, chip // 2, chips - 1 - chip // 2)


def owner_at(offset, other_core, size):
    me = lax.axis_index("latent")
    chips = size // 2
    position = lax.rem(position_of(me // 2, chips) + offset + chips, chips)
    return 2 * chip_at(position, chips) + ((me % 2) ^ other_core)


def shift(value, step, size):
    chips = size // 2
    ring = [2 * q for q in range(chips // 2)] + [2 * q + 1 for q in reversed(range(chips // 2))]
    pairs = [
        (2 * ring[p] + core, 2 * ring[(p + step) % chips] + core)
        for p in range(chips)
        for core in range(2)
    ]
    return lax.ppermute(value, "latent", pairs)


def gather_table(row, size, late):
    pieces, step = [row], 1
    while step < size:
        if step > 1:
            pieces = [jnp.concatenate([after(piece, late) for piece in pieces], axis=0)]
        pieces += [swap(pieces[0], step * k, size) for k in range(1, min(4, size // step))]
        step *= len(pieces)
    return pieces


def ordered_rows(size, rows, by_latent, by_slot):
    chips = size // 2
    for block in range(size):
        group, inside = block // chips, block % chips
        slot = group * (chips // 2) + inside % (chips // 2)
        far = chips // 2 - slot // 2
        offset = far if slot % 2 == 0 else 1 - far
        owner = owner_at(offset, 1 - inside // (chips // 2), size)
        begin = pl.multiple_of(owner * rows, rows)
        by_slot[block * rows : (block + 1) * rows] = by_latent[pl.ds(begin, rows)]


def row_codes(size, rows, table, picks_ref):
    me = lax.axis_index("latent")
    counts = table[:, :size]
    order = table[:, size:]
    source = me ^ lax.broadcasted_iota(jnp.int32, (size, 1), 0)
    before = jnp.sum(jnp.where(source < me, counts, 0), axis=0, keepdims=True)
    total = jnp.sum(counts, axis=0, keepdims=True)
    owners = lax.broadcasted_iota(jnp.int32, (size, size), 1) == source

    def by_key(row):
        return jnp.sum(jnp.where(owners, row, 0), axis=1, keepdims=True)

    begin, here = by_key(before), by_key(counts[:1])
    place = lax.broadcasted_iota(jnp.int32, (size, rows), 1)
    token = jnp.full((size, rows), ABSENT, jnp.int32)
    for c in range(picks_ref.shape[0]):
        own = (place == begin + c) & (here > c)
        token = jnp.where(own, by_key(picks_ref[c : c + 1]), token)
    token = jnp.where(place < by_key(total), token, KEPT)
    latent = lax.broadcasted_iota(jnp.int32, (size * rows, 1), 0)
    keys = lax.broadcasted_iota(jnp.int32, (size * rows, size), 1)
    spread = (keys == (me ^ (latent // rows))).astype(jnp.float32)

    def by_row(values):
        return jnp.dot(spread, values.astype(jnp.float32), precision=lax.Precision.HIGHEST)

    is_latent = by_row(order) == (latent % rows).astype(jnp.float32)
    code = jnp.sum(jnp.where(is_latent, by_row(token), 0.0), axis=1, keepdims=True)
    return (code + jnp.where(code < 0, -0.5, 0.5)).astype(jnp.int32)


def multiply(by_slot, right_ref, outs):
    out = jnp.dot(by_slot[...], right_ref[...], preferred_element_type=jnp.float32)
    part = outs[0].shape[0]
    for i, ref in enumerate(outs):
        ref[...] = out[i * part : (i + 1) * part].astype(ref.dtype)


def product_kernel(size, rows, coef_ref, right_ref, *refs):
    outs, (by_latent, by_slot) = refs[:4], refs[4:]

    @pl.when(pl.program_id(0) == 0)
    def _():
        by_latent[...] = coef_ref[...].T
        ordered_rows(size, rows, by_latent, by_slot)

    multiply(by_slot, right_ref, outs)


def select_kernel(size, rows, count, coef_ref, right_ref, picks_ref, *refs):
    pieces, refs = refs[:count], refs[count:]
    outs, own_code, (by_latent, by_slot, table, codes) = refs[:4], refs[4], refs[5:]

    @pl.when(pl.program_id(0) == 0)
    def _():
        height = size // count
        for i, piece in enumerate(pieces):
            table[i * height : (i + 1) * height] = piece[...]
        code = row_codes(size, rows, table[...], picks_ref)
        codes[...] = code
        own_code[...] = codes[pl.ds(pl.multiple_of(lax.axis_index("latent") * rows, rows), rows)]
        tokens = lax.broadcasted_iota(jnp.int32, by_latent.shape, 1)
        by_latent[...] = jnp.where(
            code == KEPT, coef_ref[...].T, (tokens == code).astype(by_latent.dtype)
        )
        ordered_rows(size, rows, by_latent, by_slot)

    multiply(by_slot, right_ref, outs)


def product(coef, right, size, rows, picks=None, table=()):
    tokens, latents = coef.shape
    width = right.shape[1]
    tile = 512
    part = latents // 4
    fixed = lambda j: (0, 0)
    in_specs = [pl.BlockSpec((tokens, latents), fixed), pl.BlockSpec((tokens, tile), lambda j: (0, j))]
    out_specs = [pl.BlockSpec((part, tile), lambda j: (0, j))] * 4
    out_shape = [jax.ShapeDtypeStruct((part, width), coef.dtype)] * 4
    scratch = [pltpu.VMEM((latents, tokens), coef.dtype)] * 2
    kernel = functools.partial(product_kernel, size, rows)
    operands = [coef, right]
    if picks is not None:
        kernel = functools.partial(select_kernel, size, rows, len(table))
        operands += [picks] + list(table)
        in_specs += [pl.BlockSpec(value.shape, fixed) for value in operands[2:]]
        out_specs.append(pl.BlockSpec((rows, 1), fixed))
        out_shape.append(jax.ShapeDtypeStruct((rows, 1), jnp.int32))
        scratch += [
            pltpu.VMEM((size, table[0].shape[1]), jnp.int32),
            pltpu.VMEM((latents, 1), jnp.int32),
        ]
    return pl.pallas_call(
        kernel,
        grid=(width // tile,),
        in_specs=in_specs,
        out_specs=out_specs,
        out_shape=out_shape,
        scratch_shapes=scratch,
        compiler_params=params(24),
        cost_estimate=cost(
            2 * latents * tokens * width, 2 * (tokens * width + latents * (tokens + width))
        ),
        name="product" if picks is None else "select_product",
    )(*operands)


def term(kept, from_core, slot, rows):
    slots = kept[0].shape[0] // rows
    group, begin = slot // slots, slot % slots * rows
    pair = (kept[group], from_core[group])
    return sum(value[begin : begin + rows].astype(jnp.float32) for value in pair)


def read_gradient(refs):
    return sum(ref[...].astype(jnp.float32) for ref in refs)


def enc_kernel(code_ref, w_ref, m_ref, v_ref, *refs):
    parts, (w_out, m_out, v_out, block, fresh) = refs[:-5], refs[-5:]
    gradient = read_gradient(parts)
    reset = code_ref[...] != KEPT
    w, m, v = adam_update(w_ref[...], m_ref[...], v_ref[...], gradient)
    w = jnp.where(reset, reset_gain * gradient * inverse_rms(gradient), w)
    w_out[...] = w
    m_out[...] = jnp.where(reset, 0.0, m)
    v_out[...] = jnp.where(reset, 0.0, v)
    block[...] = w.astype(block.dtype)
    fresh[...] = gradient.astype(fresh.dtype)


def dec_kernel(code_ref, w_ref, m_ref, v_ref, fresh_ref, *refs):
    parts, (w_out, m_out, v_out, block) = refs[:-4], refs[-4:]
    reset = code_ref[...] != KEPT
    w, m, v = adam_update(w_ref[...], m_ref[...], v_ref[...], read_gradient(parts))
    w = jnp.where(reset, fresh_ref[...].astype(jnp.float32), w)
    w = w * inverse_rms(w)
    w_out[...] = w
    m_out[...] = jnp.where(reset, 0.0, m)
    v_out[...] = jnp.where(reset, 0.0, v)
    block[...] = w.astype(block.dtype)


def update(kernel, code, states, fresh, parts, extra, name):
    rows, width = states[0].shape
    tile = 16

    def last_rows(value):
        skipped = (value.shape[0] - rows) // tile
        return pl.BlockSpec((tile, value.shape[1]), lambda i: (i + skipped, 0))

    operands = [code] + list(states) + list(fresh) + list(parts)
    out_spec = pl.BlockSpec((tile, width), lambda i: (i, 0))
    wide = jax.ShapeDtypeStruct((rows, width), jnp.float32)
    narrow = jax.ShapeDtypeStruct((rows, width), jnp.bfloat16)
    return pl.pallas_call(
        kernel,
        grid=(rows // tile,),
        in_specs=[last_rows(value) for value in operands],
        out_specs=(out_spec,) * (3 + extra),
        out_shape=(wide,) * 3 + (narrow,) * extra,
        cost_estimate=cost(40 * rows * width, 40 * rows * width),
        compiler_params=params(12),
        name=name,
    )(*operands)


def place_kernel(plan, size, rows, wholes, count, *refs):
    pieces, refs = refs[:count], refs[count:]
    outs, (stage, sems_in, sems_out, sems_pack) = refs[wholes:-4], refs[-4:]
    coming, going = [], []
    for i, (piece, block, whole, offset, other_core, pack) in enumerate(plan):
        source = pieces[piece].at[pl.ds(block * rows, rows)]
        coming.append(pltpu.make_async_copy(source, stage.at[i], sems_in.at[i]))
        start = pl.multiple_of(owner_at(offset, other_core, size) * rows, rows)
        target = outs[whole].at[pl.ds(start, rows)]
        copies = [pltpu.make_async_copy(stage.at[i], target, sems_out.at[i])]
        if pack is not None:
            target = outs[2].at[pl.ds(pack * rows, rows)]
            copies.append(pltpu.make_async_copy(stage.at[i], target, sems_pack.at[pack]))
        going.append(copies)
    for copy in coming:
        copy.start()
    for copy, copies in zip(coming, going):
        copy.wait()
        for later in reversed(copies):
            later.start()
    for copies in going:
        for copy in copies:
            copy.wait()


def place(near, far, wholes, size, rows, pack=True):
    operands = [block for _, _, block in near] + [value for value, _ in far]
    plan = []
    for i, (whole, offset, _) in enumerate(near):
        plan.append((i, 0, whole, offset, 0, i if pack else None))
    for i, (_, places) in enumerate(far):
        for block, (whole, offset) in enumerate(places):
            plan.append((len(near) + i, block, whole, offset, 1, None))
    width, dtype = operands[0].shape[1], operands[0].dtype
    out_shape = [jax.ShapeDtypeStruct((size * rows, width), dtype)] * 2
    packed = len(near) if pack else 0
    if packed:
        out_shape.append(jax.ShapeDtypeStruct((packed * rows, width), dtype))
    first = wholes is None
    count = len(operands)
    if not first:
        operands += list(wholes)
    anywhere = pl.BlockSpec(memory_space=pl.ANY)
    out = pl.pallas_call(
        functools.partial(place_kernel, plan, size, rows, 0 if first else 2, count),
        out_shape=out_shape,
        in_specs=[anywhere] * len(operands),
        out_specs=[anywhere] * len(out_shape),
        scratch_shapes=[
            pltpu.VMEM((len(plan), rows, width), dtype),
            pltpu.SemaphoreType.DMA((len(plan),)),
            pltpu.SemaphoreType.DMA((len(plan),)),
            pltpu.SemaphoreType.DMA((max(packed, 1),)),
        ],
        input_output_aliases={} if first else {count: 0, count + 1: 1},
        compiler_params=params(10),
        cost_estimate=cost(0, 4 * len(plan) * rows * width),
        name="place",
    )(*operands)
    return (out[:2], out[2]) if packed else (out, None)


def gathered(blocks, size, rows):
    chips = size // 2
    left_hops = (chips - 1) // 2
    moving = [[block, block] for block in blocks]
    near = [(whole, 0, block) for whole, block in enumerate(blocks)]
    wholes, far = None, []
    for hop in range(1, chips // 2 + 1):
        sides = ((1, -hop), (-1, hop))[: 1 + (hop <= left_hops)]
        for whole in range(2):
            moving[whole] = [shift(moving[whole][i], step, size) for i, (step, _) in enumerate(sides)]
        held = [value for _, _, value in near]
        held, moving[0] = lax.optimization_barrier((held, moving[0]))
        near = [(whole, offset, value) for (whole, offset, _), value in zip(near, held)]
        wholes, packed = place(near, far[:-1], wholes, size, rows)
        moving[1] = after(moving[1], packed)
        far = far[-1:] + [(swap(packed, 1, size), [(whole, offset) for whole, offset, _ in near])]
        near = [
            (whole, offset, moving[whole][i])
            for whole in range(2)
            for i, (_, offset) in enumerate(sides)
        ]
    last_far = [(swap(value, 1, size), [(whole, offset)]) for whole, offset, value in near]
    wholes, _ = place(near, far, wholes, size, rows, pack=False)
    wholes, _ = place([], last_far, wholes, size, rows, pack=False)
    return wholes


def shards(
    x_rows,
    out_grad,
    enc_coef,
    latent_act,
    enc_w,
    enc_m,
    enc_v,
    dec_w,
    dec_m,
    dec_v,
    dead_order,
    pick_rows,
    send_count,
):
    rows = enc_w.shape[0]
    size = lax.axis_size("latent")
    chips = size // 2
    own = jnp.concatenate([send_count, dead_order], axis=1)
    dec = product(after(latent_act, own), out_grad, size, rows)
    table = gather_table(own, size, dec[0])
    dec_core = [swap(dec[0], 1, size), swap(dec[2], 1, size)]
    dec_kept = [dec[1], dec[3]]

    def advance(moving, step, kept, from_core, slot):
        came = shift(moving, step, size).astype(jnp.float32)
        return (came + term(kept, from_core, slot, rows)).astype(jnp.bfloat16)

    def begin(kept, from_core):
        return [term(kept, from_core, slot, rows).astype(jnp.bfloat16) for slot in range(2)]

    dec_moving = begin(after(dec_kept, table[0]), dec_core)
    *enc, code = product(
        after(enc_coef, *dec_moving), x_rows, size, rows, pick_rows[0].T, table
    )
    enc_core = [swap(enc[0], 1, size), swap(enc[2], 1, size)]
    enc_kept = [enc[1], enc[3]]
    dec_kept = after(dec_kept, enc[0])
    enc_moving = begin(enc_kept, enc_core)
    for slot in range(2, chips - 1):
        side = slot % 2
        step = 1 - 2 * side
        dec_moving[side] = advance(dec_moving[side], step, dec_kept, dec_core, slot)
        enc_moving[side] = advance(enc_moving[side], step, enc_kept, enc_core, slot)
    dec_parts, enc_parts = (
        [kept[1], from_core[1], shift(moving[0], 1, size), shift(moving[1], -1, size)]
        for kept, from_core, moving in (
            (dec_kept, dec_core, dec_moving),
            (enc_kept, enc_core, enc_moving),
        )
    )
    enc_out, enc_mo, enc_vo, enc_block, fresh = update(
        enc_kernel, code, (enc_w, enc_m, enc_v), (), enc_parts, 2, "enc_update"
    )
    dec_out, dec_mo, dec_vo, dec_block = update(
        dec_kernel, code, (dec_w, dec_m, dec_v), (fresh,), dec_parts, 1, "dec_update"
    )
    enc_full, dec_full = gathered((enc_block, dec_block), size, rows)
    return (enc_out, enc_mo, enc_vo, dec_out, dec_mo, dec_vo, enc_full, dec_full)


def solution(mesh):
    split = P(("groups", "latent"), None)
    placed = (split,) * 11 + (P(("groups", "latent"), None, None), split)
    return jax.shard_map(
        shards,
        mesh=mesh,
        in_specs=placed,
        out_specs=(split,) * 6 + (P("groups", None),) * 2,
        check_vma=False,
    )
```

```python
import functools

import jax
import jax.numpy as jnp
from jax import lax
from jax.experimental import pallas as pl
from jax.experimental.pallas import tpu as pltpu
from jax.sharding import PartitionSpec as P

beta_one = 0.9
beta_two = 0.99
first_fix = 1.0 - 0.9**4
second_fix = 1.0 - 0.99**4
learn_rate = 0.02
adam_eps = 1e-08
reset_gain = 0.01
norm_eps = 1e-06

KEPT = -1
ABSENT = -2


def adam_update(weight, moment, second, gradient):
    moment_new = beta_one * moment + (1.0 - beta_one) * gradient
    second_new = beta_two * second + (1.0 - beta_two) * gradient * gradient
    weight_new = weight - learn_rate * (moment_new / first_fix) / (
        jnp.sqrt(second_new / second_fix) + adam_eps
    )
    return (weight_new, moment_new, second_new)


def inverse_rms(value):
    return lax.rsqrt(jnp.mean(value * value, axis=1, keepdims=True) + norm_eps)


def swap(value, bits, size):
    return lax.ppermute(value, "latent", [(i, i ^ bits) for i in range(size)])


def after(value, *others):
    return lax.optimization_barrier((value,) + others)[0]


def params(mebibytes):
    return pltpu.CompilerParams(vmem_limit_bytes=mebibytes * 2**20)


def cost(flops, moved):
    return pl.CostEstimate(flops=int(flops), bytes_accessed=int(moved), transcendentals=0)


def chip_at(position, chips):
    return jnp.where(position < chips // 2, 2 * position, 2 * (chips - 1 - position) + 1)


def position_of(chip, chips):
    return jnp.where(chip % 2 == 0, chip // 2, chips - 1 - chip // 2)


def owner_at(offset, other_core, size):
    me = lax.axis_index("latent")
    chips = size // 2
    position = lax.rem(position_of(me // 2, chips) + offset + chips, chips)
    return 2 * chip_at(position, chips) + ((me % 2) ^ other_core)


def shift(value, step, size):
    chips = size // 2
    ring = [2 * q for q in range(chips // 2)] + [2 * q + 1 for q in reversed(range(chips // 2))]
    pairs = [
        (2 * ring[p] + core, 2 * ring[(p + step) % chips] + core)
        for p in range(chips)
        for core in range(2)
    ]
    return lax.ppermute(value, "latent", pairs)


def gather_table(row, size):
    stages, step = [], 1
    pieces = [row]
    while step < size:
        if step > 1:
            pieces = [jnp.concatenate(pieces, axis=0)]
        pieces += [swap(pieces[0], step * k, size) for k in range(1, min(4, size // step))]
        stages.append(pieces)
        step *= len(pieces)
    return stages


def ordered_rows(size, rows, by_latent, by_slot):
    chips = size // 2
    for block in range(size):
        group, inside = block // chips, block % chips
        slot = group * (chips // 2) + inside % (chips // 2)
        far = chips // 2 - slot // 2
        offset = far if slot % 2 == 0 else 1 - far
        owner = owner_at(offset, 1 - inside // (chips // 2), size)
        begin = pl.multiple_of(owner * rows, rows)
        by_slot[block * rows : (block + 1) * rows] = by_latent[pl.ds(begin, rows)]


def row_codes(size, rows, table, picks_ref):
    me = lax.axis_index("latent")
    counts = table[:, :size]
    order = table[:, size:]
    source = me ^ lax.broadcasted_iota(jnp.int32, (size, 1), 0)
    before = jnp.sum(jnp.where(source < me, counts, 0), axis=0, keepdims=True)
    total = jnp.sum(counts, axis=0, keepdims=True)
    owners = lax.broadcasted_iota(jnp.int32, (size, size), 1) == source

    def by_key(row):
        return jnp.sum(jnp.where(owners, row, 0), axis=1, keepdims=True)

    begin, here = by_key(before), by_key(counts[:1])
    place = lax.broadcasted_iota(jnp.int32, (size, rows), 1)
    token = jnp.full((size, rows), ABSENT, jnp.int32)
    for c in range(picks_ref.shape[0]):
        own = (place == begin + c) & (here > c)
        token = jnp.where(own, by_key(picks_ref[c : c + 1]), token)
    token = jnp.where(place < by_key(total), token, KEPT)
    latent = lax.broadcasted_iota(jnp.int32, (size * rows, 1), 0)
    keys = lax.broadcasted_iota(jnp.int32, (size * rows, size), 1)
    spread = (keys == (me ^ (latent // rows))).astype(jnp.float32)

    def by_row(values):
        return jnp.dot(spread, values.astype(jnp.float32), precision=lax.Precision.HIGHEST)

    is_latent = by_row(order) == (latent % rows).astype(jnp.float32)
    code = jnp.sum(jnp.where(is_latent, by_row(token), 0.0), axis=1, keepdims=True)
    return (code + jnp.where(code < 0, -0.5, 0.5)).astype(jnp.int32)


def multiply(by_slot, right_ref, outs):
    out = jnp.dot(by_slot[...], right_ref[...], preferred_element_type=jnp.float32)
    part = outs[0].shape[0]
    for i, ref in enumerate(outs):
        ref[...] = out[i * part : (i + 1) * part].astype(ref.dtype)


def product_kernel(size, rows, coef_ref, right_ref, *refs):
    outs, (by_latent, by_slot) = refs[:4], refs[4:]

    @pl.when(pl.program_id(0) == 0)
    def _():
        by_latent[...] = coef_ref[...].T
        ordered_rows(size, rows, by_latent, by_slot)

    multiply(by_slot, right_ref, outs)


def select_kernel(size, rows, count, coef_ref, right_ref, picks_ref, *refs):
    pieces, refs = refs[:count], refs[count:]
    outs, own_code, (by_latent, by_slot, table, codes) = refs[:4], refs[4], refs[5:]

    @pl.when(pl.program_id(0) == 0)
    def _():
        height = size // count
        for i, piece in enumerate(pieces):
            table[i * height : (i + 1) * height] = piece[...]
        code = row_codes(size, rows, table[...], picks_ref)
        codes[...] = code
        own_code[...] = codes[pl.ds(pl.multiple_of(lax.axis_index("latent") * rows, rows), rows)]
        tokens = lax.broadcasted_iota(jnp.int32, by_latent.shape, 1)
        by_latent[...] = jnp.where(
            code == KEPT, coef_ref[...].T, (tokens == code).astype(by_latent.dtype)
        )
        ordered_rows(size, rows, by_latent, by_slot)

    multiply(by_slot, right_ref, outs)


def product(coef, right, size, rows, vmem, picks=None, table=()):
    tokens, latents = coef.shape
    width = right.shape[1]
    tile = 512
    part = latents // 4
    fixed = lambda j: (0, 0)
    in_specs = [pl.BlockSpec((tokens, latents), fixed), pl.BlockSpec((tokens, tile), lambda j: (0, j))]
    out_specs = [pl.BlockSpec((part, tile), lambda j: (0, j))] * 4
    out_shape = [jax.ShapeDtypeStruct((part, width), coef.dtype)] * 4
    scratch = [pltpu.VMEM((latents, tokens), coef.dtype)] * 2
    kernel = functools.partial(product_kernel, size, rows)
    operands = [coef, right]
    if picks is not None:
        kernel = functools.partial(select_kernel, size, rows, len(table))
        operands += [picks] + list(table)
        in_specs += [pl.BlockSpec(value.shape, fixed) for value in operands[2:]]
        out_specs.append(pl.BlockSpec((rows, 1), fixed))
        out_shape.append(jax.ShapeDtypeStruct((rows, 1), jnp.int32))
        scratch += [
            pltpu.VMEM((size, table[0].shape[1]), jnp.int32),
            pltpu.VMEM((latents, 1), jnp.int32),
        ]
    return pl.pallas_call(
        kernel,
        grid=(width // tile,),
        in_specs=in_specs,
        out_specs=out_specs,
        out_shape=out_shape,
        scratch_shapes=scratch,
        compiler_params=params(vmem),
        cost_estimate=cost(
            2 * latents * tokens * width, 2 * (tokens * width + latents * (tokens + width))
        ),
        name="product" if picks is None else "select_product",
    )(*operands)


def term(kept, from_core, slot, rows):
    slots = kept[0].shape[0] // rows
    group, begin = slot // slots, slot % slots * rows
    pair = (kept[group], from_core[group])
    return sum(value[begin : begin + rows].astype(jnp.float32) for value in pair)


def read_gradient(refs):
    return sum(ref[...].astype(jnp.float32) for ref in refs)


def enc_kernel(code_ref, w_ref, m_ref, v_ref, *refs):
    parts, (w_out, m_out, v_out, block, fresh) = refs[:-5], refs[-5:]
    gradient = read_gradient(parts)
    reset = code_ref[...] != KEPT
    w, m, v = adam_update(w_ref[...], m_ref[...], v_ref[...], gradient)
    w = jnp.where(reset, reset_gain * gradient * inverse_rms(gradient), w)
    w_out[...] = w
    m_out[...] = jnp.where(reset, 0.0, m)
    v_out[...] = jnp.where(reset, 0.0, v)
    block[...] = w.astype(block.dtype)
    fresh[...] = gradient.astype(fresh.dtype)


def dec_kernel(code_ref, w_ref, m_ref, v_ref, fresh_ref, enc_block, *refs):
    parts, (w_out, m_out, v_out, blocks) = refs[:-4], refs[-4:]
    reset = code_ref[...] != KEPT
    w, m, v = adam_update(w_ref[...], m_ref[...], v_ref[...], read_gradient(parts))
    w = jnp.where(reset, fresh_ref[...].astype(jnp.float32), w)
    w = w * inverse_rms(w)
    w_out[...] = w
    m_out[...] = jnp.where(reset, 0.0, m)
    v_out[...] = jnp.where(reset, 0.0, v)
    blocks[0] = enc_block[...]
    blocks[1] = w.astype(blocks.dtype)


def update(kernel, code, states, others, parts, last_shapes, name):
    rows, width = states[0].shape
    tile = 16

    def last_rows(value):
        skipped = (value.shape[0] - rows) // tile
        return pl.BlockSpec((tile, value.shape[1]), lambda i: (i + skipped, 0))

    operands = [code] + list(states) + list(others) + list(parts)
    out_shape = [jax.ShapeDtypeStruct((rows, width), jnp.float32)] * 3
    out_specs = [pl.BlockSpec((tile, width), lambda i: (i, 0))] * 3
    for pair in last_shapes:
        lead = (2,) if pair else ()
        out_shape.append(jax.ShapeDtypeStruct(lead + (rows, width), jnp.bfloat16))
        out_specs.append(
            pl.BlockSpec(lead + (tile, width), lambda i, pair=pair: (0, i, 0) if pair else (i, 0))
        )
    return pl.pallas_call(
        kernel,
        grid=(rows // tile,),
        in_specs=[last_rows(value) for value in operands],
        out_specs=out_specs,
        out_shape=out_shape,
        cost_estimate=cost(40 * rows * width, 40 * rows * width),
        compiler_params=params(12),
        name=name,
    )(*operands)


def place_kernel(plan, size, rows, count, *refs):
    pieces, outs, sems = refs[:count], refs[-3:-1], refs[-1]
    copies = []
    for i, (offset, other_core, column) in enumerate(plan):
        start = pl.multiple_of(owner_at(offset, other_core, size) * rows, rows)
        for whole, out in enumerate(outs):
            source = pieces[i].at[pl.ds(whole * rows, rows)]
            target = out.at[pl.ds(start, rows), pl.ds(column, pieces[i].shape[1])]
            copies.append(pltpu.make_async_copy(source, target, sems.at[i, whole]))
    for copy in copies:
        copy.start()
    for copy in copies:
        copy.wait()


def place(pieces, wholes, size, rows, width):
    operands = [value for _, _, _, value in pieces]
    plan = [piece[:3] for piece in pieces]
    count = len(operands)
    first = wholes is None
    if not first:
        operands += list(wholes)
    anywhere = pl.BlockSpec(memory_space=pl.ANY)
    return pl.pallas_call(
        functools.partial(place_kernel, plan, size, rows, count),
        out_shape=[jax.ShapeDtypeStruct((size * rows, width), operands[0].dtype)] * 2,
        in_specs=[anywhere] * len(operands),
        out_specs=[anywhere] * 2,
        scratch_shapes=[pltpu.SemaphoreType.DMA((count, 2))],
        input_output_aliases={} if first else {count: 0, count + 1: 1},
        compiler_params=params(4),
        cost_estimate=cost(0, 8 * count * rows * width),
        name="place",
    )(*operands)


def gathered(block, size, rows):
    chips = size // 2
    width = block.shape[1]
    half = width // 2
    hops = chips // 2
    right = left = block
    near, far, wholes = [(0, 0, 0, block)], [], None
    for hop in range(1, hops + 1):
        if hop == hops:
            right, left = right[:, :half], left[:, half:]
        right, left = shift(right, 1, size), shift(left, -1, size)
        sent = [(offset, 1, column, swap(value, 1, size)) for offset, _, column, value in near]
        wholes = place(near + far, wholes, size, rows, width)
        far = sent
        right, left, wholes = lax.optimization_barrier((right, left, wholes))
        near = [(-hop, 0, 0, right), (hop, 0, half if hop == hops else 0, left)]
    sent = [(offset, 1, column, swap(value, 1, size)) for offset, _, column, value in near]
    wholes = place(near + far, wholes, size, rows, width)
    return place(sent, wholes, size, rows, width)


def shards(
    x_rows,
    out_grad,
    enc_coef,
    latent_act,
    enc_w,
    enc_m,
    enc_v,
    dec_w,
    dec_m,
    dec_v,
    dead_order,
    pick_rows,
    send_count,
):
    rows, width = enc_w.shape
    half = width // 2
    size = lax.axis_size("latent")
    chips = size // 2
    stages = gather_table(jnp.concatenate([send_count, dead_order], axis=1), size)
    table = stages[-1]
    dec = product(latent_act, out_grad, size, rows, 56)
    dec_far = after(dec[0], *stages[0])
    dec_kept, dec_core = [dec[1], dec[3]], [swap(dec_far, 1, size), swap(dec[2], 1, size)]

    def begin(kept, from_core):
        far = term(kept, from_core, 0, rows).astype(jnp.bfloat16)
        return [far[:, :half], far[:, half:]]

    def travel(moving):
        return [shift(moving[0], 1, size), shift(moving[1], -1, size)]

    def advance(came, kept, from_core, hop):
        moving = []
        for side, value in enumerate(came):
            value = value.astype(jnp.float32)
            if value.shape[1] < width:
                pads = ((0, 0, 0), (0, half, 0) if side == 0 else (half, 0, 0))
                value = lax.pad(value, jnp.float32(0), pads)
            value = value + term(kept, from_core, 2 * hop - side, rows)
            moving.append(value.astype(jnp.bfloat16))
        return moving

    dec_moving = begin(dec_kept, dec_core)
    *enc, code = product(
        after(enc_coef, *dec_moving), x_rows, size, rows, 24, pick_rows[0].T, table
    )
    dec_came = travel(dec_moving)
    enc_far, enc_near = after((enc[0], enc[2]), *dec_came)
    enc_kept, enc_core = [enc[1], enc[3]], [swap(enc_far, 1, size), swap(enc_near, 1, size)]
    enc_came = travel(begin(enc_kept, enc_core))
    for hop in range(1, chips // 2):
        dec_came = travel(advance(dec_came, dec_kept, dec_core, hop))
        enc_came = travel(advance(enc_came, enc_kept, enc_core, hop))
    enc_out, enc_mo, enc_vo, enc_block, fresh = update(
        enc_kernel,
        code,
        (enc_w, enc_m, enc_v),
        (),
        [enc_kept[1], enc_core[1]] + enc_came,
        (False, False),
        "enc_update",
    )
    dec_out, dec_mo, dec_vo, blocks = update(
        dec_kernel,
        code,
        (dec_w, dec_m, dec_v),
        (fresh, enc_block),
        [dec_kept[1], dec_core[1]] + dec_came,
        (True,),
        "dec_update",
    )
    enc_full, dec_full = gathered(blocks.reshape(2 * rows, width), size, rows)
    return (enc_out, enc_mo, enc_vo, dec_out, dec_mo, dec_vo, enc_full, dec_full)


def solution(mesh):
    split = P(("groups", "latent"), None)
    placed = (split,) * 11 + (P(("groups", "latent"), None, None), split)
    return jax.shard_map(
        shards,
        mesh=mesh,
        in_specs=placed,
        out_specs=(split,) * 6 + (P("groups", None),) * 2,
        check_vma=False,
    )
```

```python
import functools

import jax
import jax.numpy as jnp
from jax import lax
from jax.experimental import pallas as pl
from jax.experimental.pallas import tpu as pltpu
from jax.sharding import PartitionSpec as P

beta_one = 0.9
beta_two = 0.99
first_fix = 1.0 - 0.9**4
second_fix = 1.0 - 0.99**4
learn_rate = 0.02
adam_eps = 1e-08
reset_gain = 0.01
norm_eps = 1e-06

KEPT = -1
ABSENT = -2


def adam_update(weight, moment, second, gradient):
    moment_new = beta_one * moment + (1.0 - beta_one) * gradient
    second_new = beta_two * second + (1.0 - beta_two) * gradient * gradient
    weight_new = weight - learn_rate * (moment_new / first_fix) / (
        jnp.sqrt(second_new / second_fix) + adam_eps
    )
    return (weight_new, moment_new, second_new)


def inverse_rms(value):
    return lax.rsqrt(jnp.mean(value * value, axis=1, keepdims=True) + norm_eps)


def swap(value, bits, size):
    return lax.ppermute(value, "latent", [(i, i ^ bits) for i in range(size)])


def after(value, *others):
    return lax.optimization_barrier((value,) + others)[0]


def tied(*values):
    return lax.optimization_barrier(values)


def params(mebibytes):
    return pltpu.CompilerParams(vmem_limit_bytes=mebibytes * 2**20)


def cost(flops, moved):
    return pl.CostEstimate(flops=int(flops), bytes_accessed=int(moved), transcendentals=0)


def chip_at(position, chips):
    return jnp.where(position < chips // 2, 2 * position, 2 * (chips - 1 - position) + 1)


def position_of(chip, chips):
    return jnp.where(chip % 2 == 0, chip // 2, chips - 1 - chip // 2)


def owner_at(offset, other_core, size):
    me = lax.axis_index("latent")
    chips = size // 2
    position = lax.rem(position_of(me // 2, chips) + offset + chips, chips)
    return 2 * chip_at(position, chips) + ((me % 2) ^ other_core)


def shift(value, step, size):
    chips = size // 2
    ring = [2 * q for q in range(chips // 2)] + [2 * q + 1 for q in reversed(range(chips // 2))]
    pairs = [
        (2 * ring[p] + core, 2 * ring[(p + step) % chips] + core)
        for p in range(chips)
        for core in range(2)
    ]
    return lax.ppermute(value, "latent", pairs)


def gather_table(row, size):
    stages, step = [], 1
    pieces = [row]
    while step < size:
        if step > 1:
            pieces = [jnp.concatenate(pieces, axis=0)]
        pieces += [swap(pieces[0], step * k, size) for k in range(1, min(4, size // step))]
        stages.append(pieces)
        step *= len(pieces)
    return stages


def ordered_rows(size, rows, by_latent, groups):
    chips = size // 2
    for block in range(size):
        group, inside = block // chips, block % chips
        slot = group * (chips // 2) + inside % (chips // 2)
        far = chips // 2 - slot // 2
        offset = far if slot % 2 == 0 else 1 - far
        owner = owner_at(offset, 1 - inside // (chips // 2), size)
        begin = pl.multiple_of(owner * rows, rows)
        groups[group][inside * rows : (inside + 1) * rows] = by_latent[pl.ds(begin, rows)]


def row_codes(size, rows, table, picks_ref):
    me = lax.axis_index("latent")
    counts = table[:, :size]
    order = table[:, size:]
    source = me ^ lax.broadcasted_iota(jnp.int32, (size, 1), 0)
    before = jnp.sum(jnp.where(source < me, counts, 0), axis=0, keepdims=True)
    total = jnp.sum(counts, axis=0, keepdims=True)
    owners = lax.broadcasted_iota(jnp.int32, (size, size), 1) == source

    def by_key(row):
        return jnp.sum(jnp.where(owners, row, 0), axis=1, keepdims=True)

    begin, here = by_key(before), by_key(counts[:1])
    place = lax.broadcasted_iota(jnp.int32, (size, rows), 1)
    token = jnp.full((size, rows), ABSENT, jnp.int32)
    for c in range(picks_ref.shape[0]):
        own = (place == begin + c) & (here > c)
        token = jnp.where(own, by_key(picks_ref[c : c + 1]), token)
    token = jnp.where(place < by_key(total), token, KEPT)
    latent = lax.broadcasted_iota(jnp.int32, (size * rows, 1), 0)
    keys = lax.broadcasted_iota(jnp.int32, (size * rows, size), 1)
    spread = (keys == (me ^ (latent // rows))).astype(jnp.float32)

    def by_row(values):
        return jnp.dot(spread, values.astype(jnp.float32), precision=lax.Precision.HIGHEST)

    is_latent = by_row(order) == (latent % rows).astype(jnp.float32)
    code = jnp.sum(jnp.where(is_latent, by_row(token), 0.0), axis=1, keepdims=True)
    return (code + jnp.where(code < 0, -0.5, 0.5)).astype(jnp.int32)


def multiply(left_ref, right_ref, outs):
    out = jnp.dot(left_ref[...], right_ref[...], preferred_element_type=jnp.float32)
    part = outs[0].shape[0]
    for i, ref in enumerate(outs):
        ref[...] = out[i * part : (i + 1) * part].astype(ref.dtype)


def far_kernel(size, rows, coef_ref, right_ref, *refs):
    outs, near_left, (by_latent, left) = refs[:2], refs[2], refs[3:]

    @pl.when(pl.program_id(0) == 0)
    def _():
        by_latent[...] = coef_ref[...].T
        ordered_rows(size, rows, by_latent, (left, near_left))

    multiply(left, right_ref, outs)


def select_far_kernel(size, rows, count, coef_ref, right_ref, picks_ref, *refs):
    pieces, refs = refs[:count], refs[count:]
    outs, near_left, own_code, (by_latent, left, table, codes) = refs[:2], refs[2], refs[3], refs[4:]

    @pl.when(pl.program_id(0) == 0)
    def _():
        height = size // count
        for i, piece in enumerate(pieces):
            table[i * height : (i + 1) * height] = piece[...]
        code = row_codes(size, rows, table[...], picks_ref)
        codes[...] = code
        own_code[...] = codes[pl.ds(pl.multiple_of(lax.axis_index("latent") * rows, rows), rows)]
        tokens = lax.broadcasted_iota(jnp.int32, by_latent.shape, 1)
        by_latent[...] = jnp.where(
            code == KEPT, coef_ref[...].T, (tokens == code).astype(by_latent.dtype)
        )
        ordered_rows(size, rows, by_latent, (left, near_left))

    multiply(left, right_ref, outs)


def near_kernel(left_ref, right_ref, *outs):
    multiply(left_ref, right_ref, outs)


def product(kernel, left, right, others, out_more, scratch, name):
    tokens, width = right.shape
    tile = 512
    part = left.size // tokens // (4 if out_more else 2)
    fixed = lambda j: (0, 0)
    in_specs = [pl.BlockSpec(left.shape, fixed), pl.BlockSpec((tokens, tile), lambda j: (0, j))]
    return pl.pallas_call(
        kernel,
        grid=(width // tile,),
        in_specs=in_specs + [pl.BlockSpec(value.shape, fixed) for value in others],
        out_specs=[pl.BlockSpec((part, tile), lambda j: (0, j))] * 2
        + [pl.BlockSpec(value.shape, fixed) for value in out_more],
        out_shape=[jax.ShapeDtypeStruct((part, width), left.dtype)] * 2 + list(out_more),
        scratch_shapes=scratch,
        compiler_params=params(20),
        cost_estimate=cost(
            4 * part * tokens * width, 2 * (tokens * width + 2 * part * (tokens + width))
        ),
        name=name,
    )(left, right, *others)


def far_product(coef, right, size, rows, picks=None, table=()):
    tokens, latents = coef.shape
    near_left = jax.ShapeDtypeStruct((latents // 2, tokens), coef.dtype)
    scratch = [
        pltpu.VMEM((latents, tokens), coef.dtype),
        pltpu.VMEM((latents // 2, tokens), coef.dtype),
    ]
    if picks is None:
        kernel = functools.partial(far_kernel, size, rows)
        return product(kernel, coef, right, [], [near_left], scratch, "far_product")
    kernel = functools.partial(select_far_kernel, size, rows, len(table))
    scratch += [
        pltpu.VMEM((size, table[0].shape[1]), jnp.int32),
        pltpu.VMEM((latents, 1), jnp.int32),
    ]
    code = jax.ShapeDtypeStruct((rows, 1), jnp.int32)
    others = [picks] + list(table)
    return product(kernel, coef, right, others, [near_left, code], scratch, "select_far_product")


def near_product(left, right):
    return product(near_kernel, left, right, [], [], [], "near_product")


def term(kept, from_core, slot, rows):
    slots = kept[0].shape[0] // rows
    group, begin = slot // slots, slot % slots * rows
    pair = (kept[group], from_core[group])
    return sum(value[begin : begin + rows].astype(jnp.float32) for value in pair)


def read_gradient(refs):
    return sum(ref[...].astype(jnp.float32) for ref in refs)


def enc_kernel(code_ref, w_ref, m_ref, v_ref, *refs):
    parts, (w_out, m_out, v_out, block, fresh) = refs[:-5], refs[-5:]
    gradient = read_gradient(parts)
    reset = code_ref[...] != KEPT
    w, m, v = adam_update(w_ref[...], m_ref[...], v_ref[...], gradient)
    w = jnp.where(reset, reset_gain * gradient * inverse_rms(gradient), w)
    w_out[...] = w
    m_out[...] = jnp.where(reset, 0.0, m)
    v_out[...] = jnp.where(reset, 0.0, v)
    block[...] = w.astype(block.dtype)
    fresh[...] = gradient.astype(fresh.dtype)


def dec_kernel(code_ref, w_ref, m_ref, v_ref, fresh_ref, enc_block, *refs):
    parts, (w_out, m_out, v_out, blocks) = refs[:-4], refs[-4:]
    reset = code_ref[...] != KEPT
    w, m, v = adam_update(w_ref[...], m_ref[...], v_ref[...], read_gradient(parts))
    w = jnp.where(reset, fresh_ref[...].astype(jnp.float32), w)
    w = w * inverse_rms(w)
    w_out[...] = w
    m_out[...] = jnp.where(reset, 0.0, m)
    v_out[...] = jnp.where(reset, 0.0, v)
    blocks[0] = enc_block[...]
    blocks[1] = w.astype(blocks.dtype)


def update(kernel, code, states, others, parts, last_shapes, name):
    rows, width = states[0].shape
    tile = 16

    def last_rows(value):
        skipped = (value.shape[0] - rows) // tile
        return pl.BlockSpec((tile, value.shape[1]), lambda i: (i + skipped, 0))

    operands = [code] + list(states) + list(others) + list(parts)
    out_shape = [jax.ShapeDtypeStruct((rows, width), jnp.float32)] * 3
    out_specs = [pl.BlockSpec((tile, width), lambda i: (i, 0))] * 3
    for pair in last_shapes:
        lead = (2,) if pair else ()
        out_shape.append(jax.ShapeDtypeStruct(lead + (rows, width), jnp.bfloat16))
        out_specs.append(
            pl.BlockSpec(lead + (tile, width), lambda i, pair=pair: (0, i, 0) if pair else (i, 0))
        )
    return pl.pallas_call(
        kernel,
        grid=(rows // tile,),
        in_specs=[last_rows(value) for value in operands],
        out_specs=out_specs,
        out_shape=out_shape,
        cost_estimate=cost(40 * rows * width, 40 * rows * width),
        compiler_params=params(12),
        name=name,
    )(*operands)


def place_kernel(plan, size, rows, count, *refs):
    pieces, outs, sems = refs[:count], refs[-3:-1], refs[-1]
    copies = []
    for i, (offset, other_core, column) in enumerate(plan):
        start = pl.multiple_of(owner_at(offset, other_core, size) * rows, rows)
        for whole, out in enumerate(outs):
            source = pieces[i].at[pl.ds(whole * rows, rows)]
            target = out.at[pl.ds(start, rows), pl.ds(column, pieces[i].shape[1])]
            copies.append(pltpu.make_async_copy(source, target, sems.at[i, whole]))
    for copy in copies:
        copy.start()
    for copy in copies:
        copy.wait()


def place(pieces, wholes, size, rows, width):
    operands = [value for _, _, _, value in pieces]
    plan = [piece[:3] for piece in pieces]
    count = len(operands)
    first = wholes is None
    if not first:
        operands += list(wholes)
    anywhere = pl.BlockSpec(memory_space=pl.ANY)
    return pl.pallas_call(
        functools.partial(place_kernel, plan, size, rows, count),
        out_shape=[jax.ShapeDtypeStruct((size * rows, width), operands[0].dtype)] * 2,
        in_specs=[anywhere] * len(operands),
        out_specs=[anywhere] * 2,
        scratch_shapes=[pltpu.SemaphoreType.DMA((count, 2))],
        input_output_aliases={} if first else {count: 0, count + 1: 1},
        compiler_params=params(4),
        cost_estimate=cost(0, 8 * count * rows * width),
        name="place",
    )(*operands)


def gathered(block, size, rows):
    chips = size // 2
    width = block.shape[1]
    half = width // 2
    hops = chips // 2
    right = left = block
    near, far, wholes = [(0, 0, 0, block)], [], None
    for hop in range(1, hops + 1):
        if hop == hops:
            right, left = right[:, :half], left[:, half:]
        right, left = shift(right, 1, size), shift(left, -1, size)
        sent = [(offset, 1, column, swap(value, 1, size)) for offset, _, column, value in near]
        wholes = place(near + far, wholes, size, rows, width)
        far = sent
        right, left, wholes = lax.optimization_barrier((right, left, wholes))
        near = [(-hop, 0, 0, right), (hop, 0, half if hop == hops else 0, left)]
    sent = [(offset, 1, column, swap(value, 1, size)) for offset, _, column, value in near]
    wholes = place(near + far, wholes, size, rows, width)
    return place(sent, wholes, size, rows, width)


def shards(
    x_rows,
    out_grad,
    enc_coef,
    latent_act,
    enc_w,
    enc_m,
    enc_v,
    dec_w,
    dec_m,
    dec_v,
    dead_order,
    pick_rows,
    send_count,
):
    rows, width = enc_w.shape
    half = width // 2
    size = lax.axis_size("latent")
    chips = size // 2
    stages = gather_table(jnp.concatenate([send_count, dead_order], axis=1), size)
    table = stages[-1]
    dec_sent, dec_kept, dec_left = far_product(latent_act, out_grad, size, rows)
    dec_sent = after(dec_sent, *stages[0])
    dec_kept, dec_core = [dec_kept], [swap(dec_sent, 1, size)]

    def begin(kept, from_core):
        far = term(kept, from_core, 0, rows).astype(jnp.bfloat16)
        return [far[:, :half], far[:, half:]]

    def travel(moving):
        return [shift(moving[0], 1, size), shift(moving[1], -1, size)]

    def advance(came, kept, from_core, hop):
        moving = []
        for side, value in enumerate(came):
            value = value.astype(jnp.float32)
            if value.shape[1] < width:
                pads = ((0, 0, 0), (0, half, 0) if side == 0 else (half, 0, 0))
                value = lax.pad(value, jnp.float32(0), pads)
            value = value + term(kept, from_core, 2 * hop - side, rows)
            moving.append(value.astype(jnp.bfloat16))
        return moving

    dec_moving = begin(dec_kept, after(dec_core, table[0]))
    enc_sent, enc_kept, enc_left, code = far_product(
        after(enc_coef, *dec_moving), x_rows, size, rows, pick_rows[0].T, table
    )
    dec_came, enc_sent = tied(travel(dec_moving), enc_sent)
    enc_kept, enc_core = [enc_kept], [swap(enc_sent, 1, size)]
    dec_moving = advance(dec_came, dec_kept, dec_core, 1)
    dec_came = travel(dec_moving)
    dec_sent, kept = near_product(after(dec_left, enc_sent, *dec_moving), out_grad)
    dec_kept.append(kept)
    enc_moving, dec_came, dec_sent = tied(
        begin(after(enc_kept, dec_sent), enc_core), dec_came, dec_sent
    )
    dec_core.append(swap(dec_sent, 1, size))
    enc_sent, kept = near_product(after(enc_left, dec_sent), x_rows)
    enc_kept.append(kept)
    enc_came, enc_sent = tied(travel(enc_moving), enc_sent)
    enc_core.append(swap(enc_sent, 1, size))
    dec_came = after(dec_came, enc_sent)
    for hop in range(2, chips // 2 + 1):
        if hop < chips // 2:
            dec_moving = advance(dec_came, dec_kept, dec_core, hop)
            dec_came = travel(dec_moving)
            enc_came = after(enc_came, *dec_moving)
        enc_moving = advance(enc_came, enc_kept, enc_core, hop - 1)
        enc_came = travel(enc_moving)
        dec_came = after(dec_came, *enc_moving)
    enc_out, enc_mo, enc_vo, enc_block, fresh = update(
        enc_kernel,
        code,
        (enc_w, enc_m, enc_v),
        (),
        [enc_kept[1], enc_core[1]] + enc_came,
        (False, False),
        "enc_update",
    )
    dec_out, dec_mo, dec_vo, blocks = update(
        dec_kernel,
        code,
        (dec_w, dec_m, dec_v),
        (fresh, enc_block),
        [dec_kept[1], dec_core[1]] + dec_came,
        (True,),
        "dec_update",
    )
    enc_full, dec_full = gathered(blocks.reshape(2 * rows, width), size, rows)
    return (enc_out, enc_mo, enc_vo, dec_out, dec_mo, dec_vo, enc_full, dec_full)


def solution(mesh):
    split = P(("groups", "latent"), None)
    placed = (split,) * 11 + (P(("groups", "latent"), None, None), split)
    return jax.shard_map(
        shards,
        mesh=mesh,
        in_specs=placed,
        out_specs=(split,) * 6 + (P("groups", None),) * 2,
        check_vma=False,
    )
```

```python
import functools

import jax
import jax.numpy as jnp
from jax import lax
from jax.experimental import pallas as pl
from jax.experimental.pallas import tpu as pltpu
from jax.sharding import PartitionSpec as P

beta_one = 0.9
beta_two = 0.99
first_fix = 1.0 - 0.9**4
second_fix = 1.0 - 0.99**4
learn_rate = 0.02
adam_eps = 1e-08
reset_gain = 0.01
norm_eps = 1e-06

KEPT = -1
ABSENT = -2


def adam_update(weight, moment, second, gradient):
    moment_new = beta_one * moment + (1.0 - beta_one) * gradient
    second_new = beta_two * second + (1.0 - beta_two) * gradient * gradient
    weight_new = weight - learn_rate * (moment_new / first_fix) / (
        jnp.sqrt(second_new / second_fix) + adam_eps
    )
    return (weight_new, moment_new, second_new)


def inverse_rms(value):
    return lax.rsqrt(jnp.mean(value * value, axis=1, keepdims=True) + norm_eps)


def swap(value, bits, size):
    return lax.ppermute(value, "latent", [(i, i ^ bits) for i in range(size)])


def after(value, *others):
    return lax.optimization_barrier((value,) + others)[0]


def tied(*values):
    return lax.optimization_barrier(values)


def params(mebibytes):
    return pltpu.CompilerParams(vmem_limit_bytes=mebibytes * 2**20)


def cost(flops, moved):
    return pl.CostEstimate(flops=int(flops), bytes_accessed=int(moved), transcendentals=0)


def chip_at(position, chips):
    return jnp.where(position < chips // 2, 2 * position, 2 * (chips - 1 - position) + 1)


def position_of(chip, chips):
    return jnp.where(chip % 2 == 0, chip // 2, chips - 1 - chip // 2)


def owner_at(offset, other_core, size):
    me = lax.axis_index("latent")
    chips = size // 2
    position = lax.rem(position_of(me // 2, chips) + offset + chips, chips)
    return 2 * chip_at(position, chips) + ((me % 2) ^ other_core)


def shift(value, step, size):
    chips = size // 2
    ring = [2 * q for q in range(chips // 2)] + [2 * q + 1 for q in reversed(range(chips // 2))]
    pairs = [
        (2 * ring[p] + core, 2 * ring[(p + step) % chips] + core)
        for p in range(chips)
        for core in range(2)
    ]
    return lax.ppermute(value, "latent", pairs)


def gather_table(row, size):
    stages, step = [], 1
    pieces = [row]
    while step < size:
        if step > 1:
            pieces = [jnp.concatenate(pieces, axis=0)]
        pieces += [swap(pieces[0], step * k, size) for k in range(1, min(4, size // step))]
        stages.append(pieces)
        step *= len(pieces)
    return stages


def ordered_rows(size, rows, by_latent, by_slot):
    chips = size // 2
    for block in range(size):
        group, inside = block // chips, block % chips
        slot = group * (chips // 2) + inside % (chips // 2)
        far = chips // 2 - slot // 2
        offset = far if slot % 2 == 0 else 1 - far
        owner = owner_at(offset, 1 - inside // (chips // 2), size)
        begin = pl.multiple_of(owner * rows, rows)
        by_slot[block * rows : (block + 1) * rows] = by_latent[pl.ds(begin, rows)]


def row_codes(size, rows, table, picks_ref):
    me = lax.axis_index("latent")
    counts = table[:, :size]
    order = table[:, size:]
    source = me ^ lax.broadcasted_iota(jnp.int32, (size, 1), 0)
    before = jnp.sum(jnp.where(source < me, counts, 0), axis=0, keepdims=True)
    total = jnp.sum(counts, axis=0, keepdims=True)
    owners = lax.broadcasted_iota(jnp.int32, (size, size), 1) == source

    def by_key(row):
        return jnp.sum(jnp.where(owners, row, 0), axis=1, keepdims=True)

    begin, here = by_key(before), by_key(counts[:1])
    place = lax.broadcasted_iota(jnp.int32, (size, rows), 1)
    token = jnp.full((size, rows), ABSENT, jnp.int32)
    for c in range(picks_ref.shape[0]):
        own = (place == begin + c) & (here > c)
        token = jnp.where(own, by_key(picks_ref[c : c + 1]), token)
    token = jnp.where(place < by_key(total), token, KEPT)
    latent = lax.broadcasted_iota(jnp.int32, (size * rows, 1), 0)
    keys = lax.broadcasted_iota(jnp.int32, (size * rows, size), 1)
    spread = (keys == (me ^ (latent // rows))).astype(jnp.float32)

    def by_row(values):
        return jnp.dot(spread, values.astype(jnp.float32), precision=lax.Precision.HIGHEST)

    is_latent = by_row(order) == (latent % rows).astype(jnp.float32)
    code = jnp.sum(jnp.where(is_latent, by_row(token), 0.0), axis=1, keepdims=True)
    return (code + jnp.where(code < 0, -0.5, 0.5)).astype(jnp.int32)


def product_kernel(size, rows, count, coef_ref, right_hbm, *refs):
    if count:
        picks_ref, pieces, refs = refs[0], refs[1 : count + 1], refs[count + 1 :]
        outs, own_code, table, codes = refs[:4], refs[4], refs[-2], refs[-1]
        refs = refs[5:-2]
    else:
        outs, refs = refs[:4], refs[4:]
    right, by_latent, left, total, stage, sems_in, sems_out = refs
    tokens, width = right.shape
    part = outs[0].shape[0]
    reads, passes, tile = 8, 2, 512
    height, depth = tokens // reads, tokens // passes

    def read(i):
        span = pl.ds(i * height, height)
        return pltpu.make_async_copy(right_hbm.at[span], right.at[span], sems_in.at[i])

    def write(i, group):
        columns = pl.ds(pl.multiple_of(i * tile, tile), tile)
        return pltpu.make_async_copy(
            stage.at[pl.ds(group * part, part), columns],
            outs[group].at[:, columns],
            sems_out.at[i, group],
        )

    for i in range(reads):
        read(i).start()
    if count:
        piece_rows = size // count
        for i, piece in enumerate(pieces):
            table[i * piece_rows : (i + 1) * piece_rows] = piece[...]
        code = row_codes(size, rows, table[...], picks_ref)
        codes[...] = code
        own_code[...] = codes[pl.ds(pl.multiple_of(lax.axis_index("latent") * rows, rows), rows)]
        chosen = lax.broadcasted_iota(jnp.int32, by_latent.shape, 1) == code
        by_latent[...] = jnp.where(code == KEPT, coef_ref[...].T, chosen.astype(by_latent.dtype))
    else:
        by_latent[...] = coef_ref[...].T
    ordered_rows(size, rows, by_latent, left)
    for step in range(passes):
        for i in range(step * reads // passes, (step + 1) * reads // passes):
            read(i).wait()
        span = slice(step * depth, (step + 1) * depth)

        @pl.loop(0, width // tile)
        def _(i):
            columns = pl.ds(pl.multiple_of(i * tile, tile), tile)
            out = jnp.dot(left[:, span], right[span, columns], preferred_element_type=jnp.float32)
            if step > 0:
                out = out + total[:, columns]
            if step < passes - 1:
                total[:, columns] = out
            else:
                stage[:, columns] = out.astype(stage.dtype)
                for group in range(4):
                    write(i, group).start()

    @pl.loop(0, width // tile)
    def _(i):
        for group in range(4):
            write(i, group).wait()


def product(coef, right, size, rows, picks=None, table=()):
    tokens, latents = coef.shape
    width = right.shape[1]
    part = latents // 4
    vmem, anywhere = (pl.BlockSpec(memory_space=space) for space in (pltpu.VMEM, pl.ANY))
    others = [] if picks is None else [picks] + list(table)
    out_shape = [jax.ShapeDtypeStruct((part, width), coef.dtype)] * 4
    scratch = [
        pltpu.VMEM((tokens, width), coef.dtype),
        pltpu.VMEM((latents, tokens), coef.dtype),
        pltpu.VMEM((latents, tokens), coef.dtype),
        pltpu.VMEM((latents, width), jnp.float32),
        pltpu.VMEM((latents, width), coef.dtype),
        pltpu.SemaphoreType.DMA((8,)),
        pltpu.SemaphoreType.DMA((width // 512, 4)),
    ]
    if others:
        out_shape.append(jax.ShapeDtypeStruct((rows, 1), jnp.int32))
        scratch += [
            pltpu.VMEM((size, table[0].shape[1]), jnp.int32),
            pltpu.VMEM((latents, 1), jnp.int32),
        ]
    return pl.pallas_call(
        functools.partial(product_kernel, size, rows, len(table)),
        in_specs=[vmem, anywhere] + [vmem] * len(others),
        out_specs=[anywhere] * 4 + [vmem] * (len(out_shape) - 4),
        out_shape=out_shape,
        scratch_shapes=scratch,
        compiler_params=params(56),
        cost_estimate=cost(
            2 * latents * tokens * width, 2 * (tokens * width + latents * (tokens + width))
        ),
        name="select_product" if others else "product",
    )(coef, right, *others)


def term(kept, from_core, slot, rows):
    slots = kept[0].shape[0] // rows
    group, begin = slot // slots, slot % slots * rows
    pair = (kept[group], from_core[group])
    return sum(value[begin : begin + rows].astype(jnp.float32) for value in pair)


def read_gradient(refs):
    return sum(ref[...].astype(jnp.float32) for ref in refs)


def enc_kernel(code_ref, w_ref, m_ref, v_ref, *refs):
    parts, (w_out, m_out, v_out, block, fresh) = refs[:-5], refs[-5:]
    gradient = read_gradient(parts)
    reset = code_ref[...] != KEPT
    w, m, v = adam_update(w_ref[...], m_ref[...], v_ref[...], gradient)
    w = jnp.where(reset, reset_gain * gradient * inverse_rms(gradient), w)
    w_out[...] = w
    m_out[...] = jnp.where(reset, 0.0, m)
    v_out[...] = jnp.where(reset, 0.0, v)
    block[...] = w.astype(block.dtype)
    fresh[...] = gradient.astype(fresh.dtype)


def dec_kernel(code_ref, w_ref, m_ref, v_ref, fresh_ref, enc_block, *refs):
    parts, (w_out, m_out, v_out, blocks) = refs[:-4], refs[-4:]
    reset = code_ref[...] != KEPT
    w, m, v = adam_update(w_ref[...], m_ref[...], v_ref[...], read_gradient(parts))
    w = jnp.where(reset, fresh_ref[...].astype(jnp.float32), w)
    w = w * inverse_rms(w)
    w_out[...] = w
    m_out[...] = jnp.where(reset, 0.0, m)
    v_out[...] = jnp.where(reset, 0.0, v)
    blocks[0] = enc_block[...]
    blocks[1] = w.astype(blocks.dtype)


def update(kernel, code, states, others, parts, last_shapes, name):
    rows, width = states[0].shape
    tile = 16

    def last_rows(value):
        skipped = (value.shape[0] - rows) // tile
        return pl.BlockSpec((tile, value.shape[1]), lambda i: (i + skipped, 0))

    operands = [code] + list(states) + list(others) + list(parts)
    out_shape = [jax.ShapeDtypeStruct((rows, width), jnp.float32)] * 3
    out_specs = [pl.BlockSpec((tile, width), lambda i: (i, 0))] * 3
    for pair in last_shapes:
        lead = (2,) if pair else ()
        out_shape.append(jax.ShapeDtypeStruct(lead + (rows, width), jnp.bfloat16))
        out_specs.append(
            pl.BlockSpec(lead + (tile, width), lambda i, pair=pair: (0, i, 0) if pair else (i, 0))
        )
    return pl.pallas_call(
        kernel,
        grid=(rows // tile,),
        in_specs=[last_rows(value) for value in operands],
        out_specs=out_specs,
        out_shape=out_shape,
        cost_estimate=cost(40 * rows * width, 40 * rows * width),
        compiler_params=params(12),
        name=name,
    )(*operands)


def place_kernel(plan, size, rows, count, *refs):
    pieces, outs, sems = refs[:count], refs[-3:-1], refs[-1]
    copies = []
    for i, (offset, other_core, column) in enumerate(plan):
        start = pl.multiple_of(owner_at(offset, other_core, size) * rows, rows)
        for whole, out in enumerate(outs):
            source = pieces[i].at[pl.ds(whole * rows, rows)]
            target = out.at[pl.ds(start, rows), pl.ds(column, pieces[i].shape[1])]
            copies.append(pltpu.make_async_copy(source, target, sems.at[i, whole]))
    for copy in copies:
        copy.start()
    for copy in copies:
        copy.wait()


def place(pieces, wholes, size, rows, width):
    operands = [value for _, _, _, value in pieces]
    plan = [piece[:3] for piece in pieces]
    count = len(operands)
    first = wholes is None
    if not first:
        operands += list(wholes)
    anywhere = pl.BlockSpec(memory_space=pl.ANY)
    return pl.pallas_call(
        functools.partial(place_kernel, plan, size, rows, count),
        out_shape=[jax.ShapeDtypeStruct((size * rows, width), operands[0].dtype)] * 2,
        in_specs=[anywhere] * len(operands),
        out_specs=[anywhere] * 2,
        scratch_shapes=[pltpu.SemaphoreType.DMA((count, 2))],
        input_output_aliases={} if first else {count: 0, count + 1: 1},
        compiler_params=params(4),
        cost_estimate=cost(0, 8 * count * rows * width),
        name="place",
    )(*operands)


def gathered(block, size, rows):
    chips = size // 2
    width = block.shape[1]
    half = width // 2
    hops = chips // 2
    right = left = block
    near, far, wholes = [(0, 0, 0, block)], [], None
    for hop in range(1, hops + 1):
        if hop == hops:
            right, left = right[:, :half], left[:, half:]
        right, left = shift(right, 1, size), shift(left, -1, size)
        sent = [(offset, 1, column, swap(value, 1, size)) for offset, _, column, value in near]
        wholes = place(near + far, wholes, size, rows, width)
        far = sent
        right, left, wholes = lax.optimization_barrier((right, left, wholes))
        near = [(-hop, 0, 0, right), (hop, 0, half if hop == hops else 0, left)]
    sent = [(offset, 1, column, swap(value, 1, size)) for offset, _, column, value in near]
    wholes = place(near + far, wholes, size, rows, width)
    return place(sent, wholes, size, rows, width)


def shards(
    x_rows,
    out_grad,
    enc_coef,
    latent_act,
    enc_w,
    enc_m,
    enc_v,
    dec_w,
    dec_m,
    dec_v,
    dead_order,
    pick_rows,
    send_count,
):
    rows, width = enc_w.shape
    half = width // 2
    size = lax.axis_size("latent")
    chips = size // 2
    stages = gather_table(jnp.concatenate([send_count, dead_order], axis=1), size)
    table = stages[-1]
    def begin(kept, from_core):
        far = term(kept, from_core, 0, rows).astype(jnp.bfloat16)
        return [far[:, :half], far[:, half:]]

    def travel(moving):
        return [shift(moving[0], 1, size), shift(moving[1], -1, size)]

    def advance(came, kept, from_core, hop):
        moving = []
        for side, value in enumerate(came):
            value = value.astype(jnp.float32)
            if value.shape[1] < width:
                pads = ((0, 0, 0), (0, half, 0) if side == 0 else (half, 0, 0))
                value = lax.pad(value, jnp.float32(0), pads)
            value = value + term(kept, from_core, 2 * hop - side, rows)
            moving.append(value.astype(jnp.bfloat16))
        return moving

    dec = product(latent_act, out_grad, size, rows)
    dec_far = after(dec[0], *stages[0])
    dec_kept, dec_core = [dec[1], dec[3]], [swap(dec_far, 1, size), swap(dec[2], 1, size)]
    dec_moving = begin(dec_kept, after(dec_core, table[0]))
    *enc, code = product(
        after(enc_coef, *dec_moving), x_rows, size, rows, pick_rows[0].T, table
    )
    dec_came, enc_far = tied(travel(dec_moving), enc[0])
    enc_kept, enc_core = [enc[1], enc[3]], [swap(enc_far, 1, size), swap(enc[2], 1, size)]
    dec_moving = advance(dec_came, dec_kept, dec_core, 1)
    dec_came = travel(dec_moving)
    enc_moving = begin(enc_kept, after(enc_core, *dec_moving))
    enc_came = travel(enc_moving)
    dec_came = after(dec_came, *enc_moving)
    for hop in range(1, chips // 2):
        if hop + 1 < chips // 2:
            dec_moving = advance(dec_came, dec_kept, dec_core, hop + 1)
            dec_came = travel(dec_moving)
            enc_came = after(enc_came, *dec_moving)
        enc_moving = advance(enc_came, enc_kept, enc_core, hop)
        enc_came = travel(enc_moving)
        dec_came = after(dec_came, *enc_moving)
    enc_out, enc_mo, enc_vo, enc_block, fresh = update(
        enc_kernel,
        code,
        (enc_w, enc_m, enc_v),
        (),
        [enc_kept[1], enc_core[1]] + enc_came,
        (False, False),
        "enc_update",
    )
    dec_out, dec_mo, dec_vo, blocks = update(
        dec_kernel,
        code,
        (dec_w, dec_m, dec_v),
        (fresh, enc_block),
        [dec_kept[1], dec_core[1]] + dec_came,
        (True,),
        "dec_update",
    )
    enc_full, dec_full = gathered(blocks.reshape(2 * rows, width), size, rows)
    return (enc_out, enc_mo, enc_vo, dec_out, dec_mo, dec_vo, enc_full, dec_full)


def solution(mesh):
    split = P(("groups", "latent"), None)
    placed = (split,) * 11 + (P(("groups", "latent"), None, None), split)
    return jax.shard_map(
        shards,
        mesh=mesh,
        in_specs=placed,
        out_specs=(split,) * 6 + (P("groups", None),) * 2,
        check_vma=False,
    )
```

```python
import functools

import jax
import jax.numpy as jnp
from jax import lax
from jax.experimental import pallas as pl
from jax.experimental.pallas import tpu as pltpu
from jax.sharding import PartitionSpec as P

beta_one = 0.9
beta_two = 0.99
first_fix = 1.0 - 0.9**4
second_fix = 1.0 - 0.99**4
learn_rate = 0.02
adam_eps = 1e-08
reset_gain = 0.01
norm_eps = 1e-06

KEPT = -1
ABSENT = -2


def adam_update(weight, moment, second, gradient):
    moment_new = beta_one * moment + (1.0 - beta_one) * gradient
    second_new = beta_two * second + (1.0 - beta_two) * gradient * gradient
    weight_new = weight - learn_rate * (moment_new / first_fix) / (
        jnp.sqrt(second_new / second_fix) + adam_eps
    )
    return (weight_new, moment_new, second_new)


def inverse_rms(value):
    return lax.rsqrt(jnp.mean(value * value, axis=1, keepdims=True) + norm_eps)


def swap(value, bits, size):
    return lax.ppermute(value, "latent", [(i, i ^ bits) for i in range(size)])


def after(value, *others):
    return lax.optimization_barrier((value,) + others)[0]


def tied(*values):
    return lax.optimization_barrier(values)


def params(mebibytes):
    return pltpu.CompilerParams(vmem_limit_bytes=mebibytes * 2**20)


def cost(flops, moved):
    return pl.CostEstimate(flops=int(flops), bytes_accessed=int(moved), transcendentals=0)


def chip_at(position, chips):
    return jnp.where(position < chips // 2, 2 * position, 2 * (chips - 1 - position) + 1)


def position_of(chip, chips):
    return jnp.where(chip % 2 == 0, chip // 2, chips - 1 - chip // 2)


def owner_at(offset, other_core, size):
    me = lax.axis_index("latent")
    chips = size // 2
    position = lax.rem(position_of(me // 2, chips) + offset + chips, chips)
    return 2 * chip_at(position, chips) + ((me % 2) ^ other_core)


def shift(value, step, size):
    chips = size // 2
    ring = [2 * q for q in range(chips // 2)] + [2 * q + 1 for q in reversed(range(chips // 2))]
    pairs = [
        (2 * ring[p] + core, 2 * ring[(p + step) % chips] + core)
        for p in range(chips)
        for core in range(2)
    ]
    return lax.ppermute(value, "latent", pairs)


def gather_table(row, size):
    stages, step = [], 1
    pieces = [row]
    while step < size:
        if step > 1:
            pieces = [jnp.concatenate(pieces, axis=0)]
        pieces += [swap(pieces[0], step * k, size) for k in range(1, min(4, size // step))]
        stages.append(pieces)
        step *= len(pieces)
    return stages


def ordered_rows(size, rows, by_latent, by_slot):
    chips = size // 2
    for block in range(size):
        group, inside = block // chips, block % chips
        slot = group * (chips // 2) + inside % (chips // 2)
        far = chips // 2 - slot // 2
        offset = far if slot % 2 == 0 else 1 - far
        owner = owner_at(offset, 1 - inside // (chips // 2), size)
        begin = pl.multiple_of(owner * rows, rows)
        by_slot[block * rows : (block + 1) * rows] = by_latent[pl.ds(begin, rows)]


def row_codes(size, rows, table, picks_ref):
    me = lax.axis_index("latent")
    counts = table[:, :size]
    order = table[:, size:]
    source = me ^ lax.broadcasted_iota(jnp.int32, (size, 1), 0)
    before = jnp.sum(jnp.where(source < me, counts, 0), axis=0, keepdims=True)
    total = jnp.sum(counts, axis=0, keepdims=True)
    owners = lax.broadcasted_iota(jnp.int32, (size, size), 1) == source

    def by_key(row):
        return jnp.sum(jnp.where(owners, row, 0), axis=1, keepdims=True)

    begin, here = by_key(before), by_key(counts[:1])
    place = lax.broadcasted_iota(jnp.int32, (size, rows), 1)
    token = jnp.full((size, rows), ABSENT, jnp.int32)
    for c in range(picks_ref.shape[0]):
        own = (place == begin + c) & (here > c)
        token = jnp.where(own, by_key(picks_ref[c : c + 1]), token)
    token = jnp.where(place < by_key(total), token, KEPT)
    latent = lax.broadcasted_iota(jnp.int32, (size * rows, 1), 0)
    keys = lax.broadcasted_iota(jnp.int32, (size * rows, size), 1)
    spread = (keys == (me ^ (latent // rows))).astype(jnp.float32)

    def by_row(values):
        return jnp.dot(spread, values.astype(jnp.float32), precision=lax.Precision.HIGHEST)

    is_latent = by_row(order) == (latent % rows).astype(jnp.float32)
    code = jnp.sum(jnp.where(is_latent, by_row(token), 0.0), axis=1, keepdims=True)
    return (code + jnp.where(code < 0, -0.5, 0.5)).astype(jnp.int32)


def multiply(by_slot, right_ref, outs):
    out = jnp.dot(by_slot[...], right_ref[...], preferred_element_type=jnp.float32)
    part = outs[0].shape[0]
    for i, ref in enumerate(outs):
        ref[...] = out[i * part : (i + 1) * part].astype(ref.dtype)


def stream_kernel(size, rows, coef_ref, right_hbm, *refs):
    outs, (right, by_latent, by_slot, stage, sems_in, sems_out) = refs[:4], refs[4:]
    tokens, width = right.shape
    part = outs[0].shape[0]
    pieces, cuts = sems_in.shape
    tile, height = width // pieces, tokens // cuts
    reads, writes = [], []
    for i in range(pieces):
        columns = pl.ds(i * tile, tile)
        reads.append([])
        for cut in range(cuts):
            span = pl.ds(cut * height, height)
            reads[i].append(
                pltpu.make_async_copy(
                    right_hbm.at[span, columns], right.at[span, columns], sems_in.at[i, cut]
                )
            )
        for group, out in enumerate(outs):
            source = stage.at[pl.ds(group * part, part), columns]
            writes.append(pltpu.make_async_copy(source, out.at[:, columns], sems_out.at[i, group]))
    for read in sum(reads, []):
        read.start()
    by_latent[...] = coef_ref[...].T
    ordered_rows(size, rows, by_latent, by_slot)
    for i in range(pieces):
        for read in reads[i]:
            read.wait()
        columns = slice(i * tile, (i + 1) * tile)
        out = jnp.dot(by_slot[...], right[:, columns], preferred_element_type=jnp.float32)
        stage[:, columns] = out.astype(stage.dtype)
        for write in writes[4 * i : 4 * i + 4]:
            write.start()
    for write in writes:
        write.wait()


def stream_product(coef, right, size, rows):
    tokens, latents = coef.shape
    width = right.shape[1]
    part = latents // 4
    pieces, cuts = 4, 4
    anywhere = pl.BlockSpec(memory_space=pl.ANY)
    return pl.pallas_call(
        functools.partial(stream_kernel, size, rows),
        in_specs=[pl.BlockSpec(memory_space=pltpu.VMEM), anywhere],
        out_specs=[anywhere] * 4,
        out_shape=[jax.ShapeDtypeStruct((part, width), coef.dtype)] * 4,
        scratch_shapes=[
            pltpu.VMEM((tokens, width), coef.dtype),
            pltpu.VMEM((latents, tokens), coef.dtype),
            pltpu.VMEM((latents, tokens), coef.dtype),
            pltpu.VMEM((latents, width), coef.dtype),
            pltpu.SemaphoreType.DMA((pieces, cuts)),
            pltpu.SemaphoreType.DMA((pieces, 4)),
        ],
        compiler_params=params(56),
        cost_estimate=cost(
            2 * latents * tokens * width, 2 * (tokens * width + latents * (tokens + width))
        ),
        name="product",
    )(coef, right)


def select_kernel(size, rows, count, coef_ref, right_ref, picks_ref, *refs):
    pieces, refs = refs[:count], refs[count:]
    outs, own_code, (by_latent, by_slot, table, codes) = refs[:4], refs[4], refs[5:]

    @pl.when(pl.program_id(0) == 0)
    def _():
        height = size // count
        for i, piece in enumerate(pieces):
            table[i * height : (i + 1) * height] = piece[...]
        code = row_codes(size, rows, table[...], picks_ref)
        codes[...] = code
        own_code[...] = codes[pl.ds(pl.multiple_of(lax.axis_index("latent") * rows, rows), rows)]
        tokens = lax.broadcasted_iota(jnp.int32, by_latent.shape, 1)
        by_latent[...] = jnp.where(
            code == KEPT, coef_ref[...].T, (tokens == code).astype(by_latent.dtype)
        )
        ordered_rows(size, rows, by_latent, by_slot)

    multiply(by_slot, right_ref, outs)


def select_product(coef, right, size, rows, picks, table):
    tokens, latents = coef.shape
    width = right.shape[1]
    tile = 512
    part = latents // 4
    fixed = lambda j: (0, 0)
    operands = [coef, right, picks] + list(table)
    in_specs = [pl.BlockSpec(value.shape, fixed) for value in operands]
    in_specs[1] = pl.BlockSpec((tokens, tile), lambda j: (0, j))
    return pl.pallas_call(
        functools.partial(select_kernel, size, rows, len(table)),
        grid=(width // tile,),
        in_specs=in_specs,
        out_specs=[pl.BlockSpec((part, tile), lambda j: (0, j))] * 4
        + [pl.BlockSpec((rows, 1), fixed)],
        out_shape=[jax.ShapeDtypeStruct((part, width), coef.dtype)] * 4
        + [jax.ShapeDtypeStruct((rows, 1), jnp.int32)],
        scratch_shapes=[
            pltpu.VMEM((latents, tokens), coef.dtype),
            pltpu.VMEM((latents, tokens), coef.dtype),
            pltpu.VMEM((size, table[0].shape[1]), jnp.int32),
            pltpu.VMEM((latents, 1), jnp.int32),
        ],
        compiler_params=params(24),
        cost_estimate=cost(
            2 * latents * tokens * width, 2 * (tokens * width + latents * (tokens + width))
        ),
        name="select_product",
    )(*operands)


def term(kept, from_core, slot, rows):
    slots = kept[0].shape[0] // rows
    group, begin = slot // slots, slot % slots * rows
    pair = (kept[group], from_core[group])
    return sum(value[begin : begin + rows].astype(jnp.float32) for value in pair)


def read_gradient(refs):
    return sum(ref[...].astype(jnp.float32) for ref in refs)


def enc_kernel(code_ref, w_ref, m_ref, v_ref, *refs):
    parts, (w_out, m_out, v_out, block, fresh) = refs[:-5], refs[-5:]
    gradient = read_gradient(parts)
    reset = code_ref[...] != KEPT
    w, m, v = adam_update(w_ref[...], m_ref[...], v_ref[...], gradient)
    w = jnp.where(reset, reset_gain * gradient * inverse_rms(gradient), w)
    w_out[...] = w
    m_out[...] = jnp.where(reset, 0.0, m)
    v_out[...] = jnp.where(reset, 0.0, v)
    block[...] = w.astype(block.dtype)
    fresh[...] = gradient.astype(fresh.dtype)


def dec_kernel(code_ref, w_ref, m_ref, v_ref, fresh_ref, enc_block, *refs):
    parts, (w_out, m_out, v_out, blocks) = refs[:-4], refs[-4:]
    reset = code_ref[...] != KEPT
    w, m, v = adam_update(w_ref[...], m_ref[...], v_ref[...], read_gradient(parts))
    w = jnp.where(reset, fresh_ref[...].astype(jnp.float32), w)
    w = w * inverse_rms(w)
    w_out[...] = w
    m_out[...] = jnp.where(reset, 0.0, m)
    v_out[...] = jnp.where(reset, 0.0, v)
    blocks[0] = enc_block[...]
    blocks[1] = w.astype(blocks.dtype)


def update(kernel, code, states, others, parts, last_shapes, name):
    rows, width = states[0].shape
    tile = 16

    def last_rows(value):
        skipped = (value.shape[0] - rows) // tile
        return pl.BlockSpec((tile, value.shape[1]), lambda i: (i + skipped, 0))

    operands = [code] + list(states) + list(others) + list(parts)
    out_shape = [jax.ShapeDtypeStruct((rows, width), jnp.float32)] * 3
    out_specs = [pl.BlockSpec((tile, width), lambda i: (i, 0))] * 3
    for pair in last_shapes:
        lead = (2,) if pair else ()
        out_shape.append(jax.ShapeDtypeStruct(lead + (rows, width), jnp.bfloat16))
        out_specs.append(
            pl.BlockSpec(lead + (tile, width), lambda i, pair=pair: (0, i, 0) if pair else (i, 0))
        )
    return pl.pallas_call(
        kernel,
        grid=(rows // tile,),
        in_specs=[last_rows(value) for value in operands],
        out_specs=out_specs,
        out_shape=out_shape,
        cost_estimate=cost(40 * rows * width, 40 * rows * width),
        compiler_params=params(12),
        name=name,
    )(*operands)


def place_kernel(plan, size, rows, count, *refs):
    pieces, outs, sems = refs[:count], refs[-3:-1], refs[-1]
    copies = []
    for i, (offset, other_core, column) in enumerate(plan):
        start = pl.multiple_of(owner_at(offset, other_core, size) * rows, rows)
        for whole, out in enumerate(outs):
            source = pieces[i].at[pl.ds(whole * rows, rows)]
            target = out.at[pl.ds(start, rows), pl.ds(column, pieces[i].shape[1])]
            copies.append(pltpu.make_async_copy(source, target, sems.at[i, whole]))
    for copy in copies:
        copy.start()
    for copy in copies:
        copy.wait()


def place(pieces, wholes, size, rows, width):
    operands = [value for _, _, _, value in pieces]
    plan = [piece[:3] for piece in pieces]
    count = len(operands)
    first = wholes is None
    if not first:
        operands += list(wholes)
    anywhere = pl.BlockSpec(memory_space=pl.ANY)
    return pl.pallas_call(
        functools.partial(place_kernel, plan, size, rows, count),
        out_shape=[jax.ShapeDtypeStruct((size * rows, width), operands[0].dtype)] * 2,
        in_specs=[anywhere] * len(operands),
        out_specs=[anywhere] * 2,
        scratch_shapes=[pltpu.SemaphoreType.DMA((count, 2))],
        input_output_aliases={} if first else {count: 0, count + 1: 1},
        compiler_params=params(4),
        cost_estimate=cost(0, 8 * count * rows * width),
        name="place",
    )(*operands)


def gathered(block, size, rows):
    chips = size // 2
    width = block.shape[1]
    half = width // 2
    hops = chips // 2
    right = left = block
    near, far, wholes = [(0, 0, 0, block)], [], None
    for hop in range(1, hops + 1):
        if hop == hops:
            right, left = right[:, :half], left[:, half:]
        right, left = shift(right, 1, size), shift(left, -1, size)
        sent = [(offset, 1, column, swap(value, 1, size)) for offset, _, column, value in near]
        wholes = place(near + far, wholes, size, rows, width)
        far = sent
        right, left, wholes = lax.optimization_barrier((right, left, wholes))
        near = [(-hop, 0, 0, right), (hop, 0, half if hop == hops else 0, left)]
    sent = [(offset, 1, column, swap(value, 1, size)) for offset, _, column, value in near]
    wholes = place(near + far, wholes, size, rows, width)
    return place(sent, wholes, size, rows, width)


def shards(
    x_rows,
    out_grad,
    enc_coef,
    latent_act,
    enc_w,
    enc_m,
    enc_v,
    dec_w,
    dec_m,
    dec_v,
    dead_order,
    pick_rows,
    send_count,
):
    rows, width = enc_w.shape
    half = width // 2
    size = lax.axis_size("latent")
    chips = size // 2
    stages = gather_table(jnp.concatenate([send_count, dead_order], axis=1), size)
    table = stages[-1]
    def begin(kept, from_core):
        far = term(kept, from_core, 0, rows).astype(jnp.bfloat16)
        return [far[:, :half], far[:, half:]]

    def travel(moving):
        return [shift(moving[0], 1, size), shift(moving[1], -1, size)]

    def advance(came, kept, from_core, hop):
        moving = []
        for side, value in enumerate(came):
            value = value.astype(jnp.float32)
            if value.shape[1] < width:
                pads = ((0, 0, 0), (0, half, 0) if side == 0 else (half, 0, 0))
                value = lax.pad(value, jnp.float32(0), pads)
            value = value + term(kept, from_core, 2 * hop - side, rows)
            moving.append(value.astype(jnp.bfloat16))
        return moving

    dec = stream_product(latent_act, out_grad, size, rows)
    dec_far = after(dec[0], *stages[0])
    dec_kept, dec_core = [dec[1], dec[3]], [swap(dec_far, 1, size), swap(after(dec[2], table[0]), 1, size)]
    dec_moving = begin(dec_kept, after(dec_core, table[0]))
    *enc, code = select_product(
        after(enc_coef, *dec_moving), x_rows, size, rows, pick_rows[0].T, table
    )
    dec_came, enc_far = tied(travel(dec_moving), enc[0])
    enc_kept, enc_core = [enc[1], enc[3]], [swap(enc_far, 1, size), swap(enc[2], 1, size)]
    dec_moving = advance(dec_came, dec_kept, dec_core, 1)
    dec_came = travel(dec_moving)
    enc_moving = begin(enc_kept, after(enc_core, *dec_moving))
    enc_came = travel(enc_moving)
    dec_came = after(dec_came, *enc_moving)
    for hop in range(1, chips // 2):
        if hop + 1 < chips // 2:
            dec_moving = advance(dec_came, dec_kept, dec_core, hop + 1)
            dec_came = travel(dec_moving)
            enc_came = after(enc_came, *dec_moving)
        enc_moving = advance(enc_came, enc_kept, enc_core, hop)
        enc_came = travel(enc_moving)
        dec_came = after(dec_came, *enc_moving)
    enc_out, enc_mo, enc_vo, enc_block, fresh = update(
        enc_kernel,
        code,
        (enc_w, enc_m, enc_v),
        (),
        [enc_kept[1], enc_core[1]] + enc_came,
        (False, False),
        "enc_update",
    )
    dec_out, dec_mo, dec_vo, blocks = update(
        dec_kernel,
        code,
        (dec_w, dec_m, dec_v),
        (fresh, enc_block),
        [dec_kept[1], dec_core[1]] + dec_came,
        (True,),
        "dec_update",
    )
    enc_full, dec_full = gathered(blocks.reshape(2 * rows, width), size, rows)
    return (enc_out, enc_mo, enc_vo, dec_out, dec_mo, dec_vo, enc_full, dec_full)


def solution(mesh):
    split = P(("groups", "latent"), None)
    placed = (split,) * 11 + (P(("groups", "latent"), None, None), split)
    return jax.shard_map(
        shards,
        mesh=mesh,
        in_specs=placed,
        out_specs=(split,) * 6 + (P("groups", None),) * 2,
        check_vma=False,
    )
```

```python
import functools

import jax
import jax.numpy as jnp
from jax import lax
from jax.experimental import pallas as pl
from jax.experimental.pallas import tpu as pltpu
from jax.sharding import PartitionSpec as P

beta_one = 0.9
beta_two = 0.99
first_fix = 1.0 - 0.9**4
second_fix = 1.0 - 0.99**4
learn_rate = 0.02
adam_eps = 1e-08
reset_gain = 0.01
norm_eps = 1e-06

KEPT = -1
ABSENT = -2


def adam_update(weight, moment, second, gradient):
    moment_new = beta_one * moment + (1.0 - beta_one) * gradient
    second_new = beta_two * second + (1.0 - beta_two) * gradient * gradient
    weight_new = weight - learn_rate * (moment_new / first_fix) / (
        jnp.sqrt(second_new / second_fix) + adam_eps
    )
    return (weight_new, moment_new, second_new)


def inverse_rms(value):
    return lax.rsqrt(jnp.mean(value * value, axis=1, keepdims=True) + norm_eps)


def swap(value, bits, size):
    return lax.ppermute(value, "latent", [(i, i ^ bits) for i in range(size)])


def after(value, *others):
    return lax.optimization_barrier((value,) + others)[0]


def tied(*values):
    return lax.optimization_barrier(values)


def params(mebibytes):
    return pltpu.CompilerParams(vmem_limit_bytes=mebibytes * 2**20)


def cost(flops, moved):
    return pl.CostEstimate(flops=int(flops), bytes_accessed=int(moved), transcendentals=0)


def chip_at(position, chips):
    return jnp.where(position < chips // 2, 2 * position, 2 * (chips - 1 - position) + 1)


def position_of(chip, chips):
    return jnp.where(chip % 2 == 0, chip // 2, chips - 1 - chip // 2)


def owner_at(offset, other_core, size):
    me = lax.axis_index("latent")
    chips = size // 2
    position = lax.rem(position_of(me // 2, chips) + offset + chips, chips)
    return 2 * chip_at(position, chips) + ((me % 2) ^ other_core)


def shift(value, step, size):
    chips = size // 2
    ring = [2 * q for q in range(chips // 2)] + [2 * q + 1 for q in reversed(range(chips // 2))]
    pairs = [
        (2 * ring[p] + core, 2 * ring[(p + step) % chips] + core)
        for p in range(chips)
        for core in range(2)
    ]
    return lax.ppermute(value, "latent", pairs)


def gather_table(row, size):
    stages, step = [], 1
    pieces = [row]
    while step < size:
        if step > 1:
            pieces = [jnp.concatenate(pieces, axis=0)]
        pieces += [swap(pieces[0], step * k, size) for k in range(1, min(4, size // step))]
        stages.append(pieces)
        step *= len(pieces)
    return stages


def ordered_rows(size, rows, by_latent, by_slot):
    chips = size // 2
    for block in range(size):
        group, inside = block // chips, block % chips
        slot = group * (chips // 2) + inside % (chips // 2)
        far = chips // 2 - slot // 2
        offset = far if slot % 2 == 0 else 1 - far
        owner = owner_at(offset, 1 - inside // (chips // 2), size)
        begin = pl.multiple_of(owner * rows, rows)
        by_slot[block * rows : (block + 1) * rows] = by_latent[pl.ds(begin, rows)]


def row_codes(size, rows, table, picks_ref):
    me = lax.axis_index("latent")
    counts = table[:, :size]
    order = table[:, size:]
    source = me ^ lax.broadcasted_iota(jnp.int32, (size, 1), 0)
    before = jnp.sum(jnp.where(source < me, counts, 0), axis=0, keepdims=True)
    total = jnp.sum(counts, axis=0, keepdims=True)
    owners = lax.broadcasted_iota(jnp.int32, (size, size), 1) == source

    def by_key(row):
        return jnp.sum(jnp.where(owners, row, 0), axis=1, keepdims=True)

    begin, here = by_key(before), by_key(counts[:1])
    place = lax.broadcasted_iota(jnp.int32, (size, rows), 1)
    token = jnp.full((size, rows), ABSENT, jnp.int32)
    for c in range(picks_ref.shape[0]):
        own = (place == begin + c) & (here > c)
        token = jnp.where(own, by_key(picks_ref[c : c + 1]), token)
    token = jnp.where(place < by_key(total), token, KEPT)
    latent = lax.broadcasted_iota(jnp.int32, (size * rows, 1), 0)
    keys = lax.broadcasted_iota(jnp.int32, (size * rows, size), 1)
    spread = (keys == (me ^ (latent // rows))).astype(jnp.float32)

    def by_row(values):
        return jnp.dot(spread, values.astype(jnp.float32), precision=lax.Precision.HIGHEST)

    is_latent = by_row(order) == (latent % rows).astype(jnp.float32)
    code = jnp.sum(jnp.where(is_latent, by_row(token), 0.0), axis=1, keepdims=True)
    return (code + jnp.where(code < 0, -0.5, 0.5)).astype(jnp.int32)


def multiply(by_slot, right_ref, outs):
    out = jnp.dot(by_slot[...], right_ref[...], preferred_element_type=jnp.float32)
    part = outs[0].shape[0]
    for i, ref in enumerate(outs):
        ref[...] = out[i * part : (i + 1) * part].astype(ref.dtype)


def stream_kernel(size, rows, coef_ref, right_hbm, *refs):
    outs, (right, by_latent, by_slot, stage, sems_in, sems_out) = refs[:4], refs[4:]
    tokens, width = right.shape
    part = outs[0].shape[0]
    pieces, cuts = sems_in.shape
    tile, height = width // pieces, tokens // cuts
    reads, writes = [], []
    for i in range(pieces):
        columns = pl.ds(i * tile, tile)
        reads.append([])
        for cut in range(cuts):
            span = pl.ds(cut * height, height)
            reads[i].append(
                pltpu.make_async_copy(
                    right_hbm.at[span, columns], right.at[span, columns], sems_in.at[i, cut]
                )
            )
        for group, out in enumerate(outs):
            source = stage.at[pl.ds(group * part, part), columns]
            writes.append(pltpu.make_async_copy(source, out.at[:, columns], sems_out.at[i, group]))
    for read in sum(reads, []):
        read.start()
    by_latent[...] = coef_ref[...].T
    ordered_rows(size, rows, by_latent, by_slot)
    for i in range(pieces):
        for read in reads[i]:
            read.wait()
        columns = slice(i * tile, (i + 1) * tile)
        out = jnp.dot(by_slot[...], right[:, columns], preferred_element_type=jnp.float32)
        stage[:, columns] = out.astype(stage.dtype)
        for write in writes[4 * i : 4 * i + 4]:
            write.start()
    for write in writes:
        write.wait()


def stream_product(coef, right, size, rows):
    tokens, latents = coef.shape
    width = right.shape[1]
    part = latents // 4
    pieces, cuts = 4, 4
    anywhere = pl.BlockSpec(memory_space=pl.ANY)
    return pl.pallas_call(
        functools.partial(stream_kernel, size, rows),
        in_specs=[pl.BlockSpec(memory_space=pltpu.VMEM), anywhere],
        out_specs=[anywhere] * 4,
        out_shape=[jax.ShapeDtypeStruct((part, width), coef.dtype)] * 4,
        scratch_shapes=[
            pltpu.VMEM((tokens, width), coef.dtype),
            pltpu.VMEM((latents, tokens), coef.dtype),
            pltpu.VMEM((latents, tokens), coef.dtype),
            pltpu.VMEM((latents, width), coef.dtype),
            pltpu.SemaphoreType.DMA((pieces, cuts)),
            pltpu.SemaphoreType.DMA((pieces, 4)),
        ],
        compiler_params=params(50),
        cost_estimate=cost(
            2 * latents * tokens * width, 2 * (tokens * width + latents * (tokens + width))
        ),
        name="product",
    )(coef, right)


def select_kernel(size, rows, count, coef_ref, right_ref, picks_ref, *refs):
    pieces, refs = refs[:count], refs[count:]
    outs, own_code, (by_latent, by_slot, table, codes) = refs[:4], refs[4], refs[5:]

    @pl.when(pl.program_id(0) == 0)
    def _():
        height = size // count
        for i, piece in enumerate(pieces):
            table[i * height : (i + 1) * height] = piece[...]
        code = row_codes(size, rows, table[...], picks_ref)
        codes[...] = code
        own_code[...] = codes[pl.ds(pl.multiple_of(lax.axis_index("latent") * rows, rows), rows)]
        tokens = lax.broadcasted_iota(jnp.int32, by_latent.shape, 1)
        by_latent[...] = jnp.where(
            code == KEPT, coef_ref[...].T, (tokens == code).astype(by_latent.dtype)
        )
        ordered_rows(size, rows, by_latent, by_slot)

    multiply(by_slot, right_ref, outs)


def select_product(coef, right, size, rows, picks, table):
    tokens, latents = coef.shape
    width = right.shape[1]
    tile = 512
    part = latents // 4
    fixed = lambda j: (0, 0)
    operands = [coef, right, picks] + list(table)
    in_specs = [pl.BlockSpec(value.shape, fixed) for value in operands]
    in_specs[1] = pl.BlockSpec((tokens, tile), lambda j: (0, j))
    return pl.pallas_call(
        functools.partial(select_kernel, size, rows, len(table)),
        grid=(width // tile,),
        in_specs=in_specs,
        out_specs=[pl.BlockSpec((part, tile), lambda j: (0, j))] * 4
        + [pl.BlockSpec((rows, 1), fixed)],
        out_shape=[jax.ShapeDtypeStruct((part, width), coef.dtype)] * 4
        + [jax.ShapeDtypeStruct((rows, 1), jnp.int32)],
        scratch_shapes=[
            pltpu.VMEM((latents, tokens), coef.dtype),
            pltpu.VMEM((latents, tokens), coef.dtype),
            pltpu.VMEM((size, table[0].shape[1]), jnp.int32),
            pltpu.VMEM((latents, 1), jnp.int32),
        ],
        compiler_params=params(24),
        cost_estimate=cost(
            2 * latents * tokens * width, 2 * (tokens * width + latents * (tokens + width))
        ),
        name="select_product",
    )(*operands)


def term(kept, from_core, slot, rows):
    slots = kept[0].shape[0] // rows
    group, begin = slot // slots, slot % slots * rows
    pair = (kept[group], from_core[group])
    return sum(value[begin : begin + rows].astype(jnp.float32) for value in pair)


def read_gradient(refs):
    return sum(ref[...].astype(jnp.float32) for ref in refs)


def enc_kernel(code_ref, w_ref, m_ref, v_ref, *refs):
    parts, (w_out, m_out, v_out, block, fresh) = refs[:-5], refs[-5:]
    gradient = read_gradient(parts)
    reset = code_ref[...] != KEPT
    w, m, v = adam_update(w_ref[...], m_ref[...], v_ref[...], gradient)
    w = jnp.where(reset, reset_gain * gradient * inverse_rms(gradient), w)
    w_out[...] = w
    m_out[...] = jnp.where(reset, 0.0, m)
    v_out[...] = jnp.where(reset, 0.0, v)
    block[...] = w.astype(block.dtype)
    fresh[...] = gradient.astype(fresh.dtype)


def dec_kernel(code_ref, w_ref, m_ref, v_ref, fresh_ref, enc_block, *refs):
    parts, (w_out, m_out, v_out, blocks) = refs[:-4], refs[-4:]
    reset = code_ref[...] != KEPT
    w, m, v = adam_update(w_ref[...], m_ref[...], v_ref[...], read_gradient(parts))
    w = jnp.where(reset, fresh_ref[...].astype(jnp.float32), w)
    w = w * inverse_rms(w)
    w_out[...] = w
    m_out[...] = jnp.where(reset, 0.0, m)
    v_out[...] = jnp.where(reset, 0.0, v)
    blocks[0] = enc_block[...]
    blocks[1] = w.astype(blocks.dtype)


def update(kernel, code, states, others, parts, last_shapes, name):
    rows, width = states[0].shape
    tile = 16

    def last_rows(value):
        skipped = (value.shape[0] - rows) // tile
        return pl.BlockSpec((tile, value.shape[1]), lambda i: (i + skipped, 0))

    operands = [code] + list(states) + list(others) + list(parts)
    out_shape = [jax.ShapeDtypeStruct((rows, width), jnp.float32)] * 3
    out_specs = [pl.BlockSpec((tile, width), lambda i: (i, 0))] * 3
    for pair in last_shapes:
        lead = (2,) if pair else ()
        out_shape.append(jax.ShapeDtypeStruct(lead + (rows, width), jnp.bfloat16))
        out_specs.append(
            pl.BlockSpec(lead + (tile, width), lambda i, pair=pair: (0, i, 0) if pair else (i, 0))
        )
    return pl.pallas_call(
        kernel,
        grid=(rows // tile,),
        in_specs=[last_rows(value) for value in operands],
        out_specs=out_specs,
        out_shape=out_shape,
        cost_estimate=cost(40 * rows * width, 40 * rows * width),
        compiler_params=params(12),
        name=name,
    )(*operands)


def place_kernel(plan, size, rows, count, *refs):
    pieces, outs, sems = refs[:count], refs[-3:-1], refs[-1]
    copies = []
    for i, (offset, other_core, column) in enumerate(plan):
        start = pl.multiple_of(owner_at(offset, other_core, size) * rows, rows)
        for whole, out in enumerate(outs):
            source = pieces[i].at[pl.ds(whole * rows, rows)]
            target = out.at[pl.ds(start, rows), pl.ds(column, pieces[i].shape[1])]
            copies.append(pltpu.make_async_copy(source, target, sems.at[i, whole]))
    for copy in copies:
        copy.start()
    for copy in copies:
        copy.wait()


def place(pieces, wholes, size, rows, width):
    operands = [value for _, _, _, value in pieces]
    plan = [piece[:3] for piece in pieces]
    count = len(operands)
    first = wholes is None
    if not first:
        operands += list(wholes)
    anywhere = pl.BlockSpec(memory_space=pl.ANY)
    return pl.pallas_call(
        functools.partial(place_kernel, plan, size, rows, count),
        out_shape=[jax.ShapeDtypeStruct((size * rows, width), operands[0].dtype)] * 2,
        in_specs=[anywhere] * len(operands),
        out_specs=[anywhere] * 2,
        scratch_shapes=[pltpu.SemaphoreType.DMA((count, 2))],
        input_output_aliases={} if first else {count: 0, count + 1: 1},
        compiler_params=params(4),
        cost_estimate=cost(0, 8 * count * rows * width),
        name="place",
    )(*operands)


def gathered(block, size, rows):
    chips = size // 2
    width = block.shape[1]
    half = width // 2
    hops = chips // 2
    right = left = block
    near, far, wholes = [(0, 0, 0, block)], [], None
    for hop in range(1, hops + 1):
        if hop == hops:
            right, left = right[:, :half], left[:, half:]
        right, left = shift(right, 1, size), shift(left, -1, size)
        sent = [(offset, 1, column, swap(value, 1, size)) for offset, _, column, value in near]
        wholes = place(near + far, wholes, size, rows, width)
        far = sent
        right, wholes = tied(right, wholes)
        left = after(left, right)
        near = [(-hop, 0, 0, right), (hop, 0, half if hop == hops else 0, left)]
    sent = [(offset, 1, column, swap(value, 1, size)) for offset, _, column, value in near]
    wholes = place(near + far, wholes, size, rows, width)
    return place(sent, wholes, size, rows, width)


def shards(
    x_rows,
    out_grad,
    enc_coef,
    latent_act,
    enc_w,
    enc_m,
    enc_v,
    dec_w,
    dec_m,
    dec_v,
    dead_order,
    pick_rows,
    send_count,
):
    rows, width = enc_w.shape
    half = width // 2
    size = lax.axis_size("latent")
    chips = size // 2
    stages = gather_table(jnp.concatenate([send_count, dead_order], axis=1), size)
    table = stages[-1]
    def begin(kept, from_core):
        far = term(kept, from_core, 0, rows).astype(jnp.bfloat16)
        return [far[:, :half], far[:, half:]]

    def travel(moving):
        return [shift(moving[0], 1, size), shift(moving[1], -1, size)]

    def advance(came, kept, from_core, hop, order):
        following = []
        for side, value in enumerate(came):
            value = after(value, order).astype(jnp.float32)
            if value.shape[1] < width:
                pads = ((0, 0, 0), (0, half, 0) if side == 0 else (half, 0, 0))
                value = lax.pad(value, jnp.float32(0), pads)
            value = value + term(kept, from_core, 2 * hop - side, rows)
            order = value.astype(jnp.bfloat16)
            following.append(shift(order, 1 - 2 * side, size))
        return following, order

    dec = stream_product(latent_act, out_grad, size, rows)
    dec_far = after(dec[0], *stages[0])
    dec_kept, dec_core = [dec[1], dec[3]], [swap(dec_far, 1, size), swap(after(dec[2], table[0]), 1, size)]
    dec_moving = begin(dec_kept, after(dec_core, table[0]))
    *enc, code = select_product(
        after(enc_coef, *dec_moving), x_rows, size, rows, pick_rows[0].T, table
    )
    dec_came, enc_far = tied(travel(dec_moving), enc[0])
    enc_kept, enc_core = [enc[1], enc[3]], [swap(enc_far, 1, size), swap(enc[2], 1, size)]
    dec_came, order = advance(dec_came, dec_kept, dec_core, 1, enc[0])
    enc_moving = begin(enc_kept, after(enc_core, order))
    enc_came, order = travel(enc_moving), enc_moving[1]
    for hop in range(1, chips // 2):
        if hop + 1 < chips // 2:
            dec_came, order = advance(dec_came, dec_kept, dec_core, hop + 1, order)
        else:
            dec_came, order = tied(dec_came, order)
        enc_came, order = advance(enc_came, enc_kept, enc_core, hop, order)
    enc_out, enc_mo, enc_vo, enc_block, fresh = update(
        enc_kernel,
        code,
        (enc_w, enc_m, enc_v),
        (),
        [enc_kept[1], enc_core[1]] + enc_came,
        (False, False),
        "enc_update",
    )
    dec_out, dec_mo, dec_vo, blocks = update(
        dec_kernel,
        code,
        (dec_w, dec_m, dec_v),
        (fresh, enc_block),
        [dec_kept[1], dec_core[1]] + dec_came,
        (True,),
        "dec_update",
    )
    enc_full, dec_full = gathered(blocks.reshape(2 * rows, width), size, rows)
    return (enc_out, enc_mo, enc_vo, dec_out, dec_mo, dec_vo, enc_full, dec_full)


def solution(mesh):
    split = P(("groups", "latent"), None)
    placed = (split,) * 11 + (P(("groups", "latent"), None, None), split)
    return jax.shard_map(
        shards,
        mesh=mesh,
        in_specs=placed,
        out_specs=(split,) * 6 + (P("groups", None),) * 2,
        check_vma=False,
    )
```

```python
import functools

import jax
import jax.numpy as jnp
from jax import lax
from jax.experimental import pallas as pl
from jax.experimental.pallas import tpu as pltpu
from jax.sharding import PartitionSpec as P

beta_one = 0.9
beta_two = 0.99
first_fix = 1.0 - 0.9**4
second_fix = 1.0 - 0.99**4
learn_rate = 0.02
adam_eps = 1e-08
reset_gain = 0.01
norm_eps = 1e-06

KEPT = -1
ABSENT = -2


def adam_update(weight, moment, second, gradient):
    moment_new = beta_one * moment + (1.0 - beta_one) * gradient
    second_new = beta_two * second + (1.0 - beta_two) * gradient * gradient
    weight_new = weight - learn_rate * (moment_new / first_fix) / (
        jnp.sqrt(second_new / second_fix) + adam_eps
    )
    return (weight_new, moment_new, second_new)


def inverse_rms(value):
    return lax.rsqrt(jnp.mean(value * value, axis=1, keepdims=True) + norm_eps)


def swap(value, bits, size):
    return lax.ppermute(value, "latent", [(i, i ^ bits) for i in range(size)])


def after(value, *others):
    return lax.optimization_barrier((value,) + others)[0]


def tied(*values):
    return lax.optimization_barrier(values)


def params(mebibytes):
    return pltpu.CompilerParams(vmem_limit_bytes=mebibytes * 2**20)


def cost(flops, moved):
    return pl.CostEstimate(flops=int(flops), bytes_accessed=int(moved), transcendentals=0)


def chip_at(position, chips):
    return jnp.where(position < chips // 2, 2 * position, 2 * (chips - 1 - position) + 1)


def position_of(chip, chips):
    return jnp.where(chip % 2 == 0, chip // 2, chips - 1 - chip // 2)


def owner_at(offset, other_core, size):
    me = lax.axis_index("latent")
    chips = size // 2
    position = lax.rem(position_of(me // 2, chips) + offset + chips, chips)
    return 2 * chip_at(position, chips) + ((me % 2) ^ other_core)


def shift(value, step, size):
    chips = size // 2
    ring = [2 * q for q in range(chips // 2)] + [2 * q + 1 for q in reversed(range(chips // 2))]
    pairs = [
        (2 * ring[p] + core, 2 * ring[(p + step) % chips] + core)
        for p in range(chips)
        for core in range(2)
    ]
    return lax.ppermute(value, "latent", pairs)


def gather_table(row, size):
    stages, step = [], 1
    pieces = [row]
    while step < size:
        if step > 1:
            pieces = [jnp.concatenate(pieces, axis=0)]
        pieces += [swap(pieces[0], step * k, size) for k in range(1, min(4, size // step))]
        stages.append(pieces)
        step *= len(pieces)
    return stages


def ordered_rows(size, rows, by_latent, groups):
    chips = size // 2
    for block in range(size):
        group, inside = block // chips, block % chips
        slot = group * (chips // 2) + inside % (chips // 2)
        far = chips // 2 - slot // 2
        offset = far if slot % 2 == 0 else 1 - far
        owner = owner_at(offset, 1 - inside // (chips // 2), size)
        begin = pl.multiple_of(owner * rows, rows)
        groups[group][inside * rows : (inside + 1) * rows] = by_latent[pl.ds(begin, rows)]


def row_codes(size, rows, table, picks_ref):
    me = lax.axis_index("latent")
    counts = table[:, :size]
    order = table[:, size:]
    source = me ^ lax.broadcasted_iota(jnp.int32, (size, 1), 0)
    before = jnp.sum(jnp.where(source < me, counts, 0), axis=0, keepdims=True)
    total = jnp.sum(counts, axis=0, keepdims=True)
    owners = lax.broadcasted_iota(jnp.int32, (size, size), 1) == source

    def by_key(row):
        return jnp.sum(jnp.where(owners, row, 0), axis=1, keepdims=True)

    begin, here = by_key(before), by_key(counts[:1])
    place = lax.broadcasted_iota(jnp.int32, (size, rows), 1)
    token = jnp.full((size, rows), ABSENT, jnp.int32)
    for c in range(picks_ref.shape[0]):
        own = (place == begin + c) & (here > c)
        token = jnp.where(own, by_key(picks_ref[c : c + 1]), token)
    token = jnp.where(place < by_key(total), token, KEPT)
    latent = lax.broadcasted_iota(jnp.int32, (size * rows, 1), 0)
    keys = lax.broadcasted_iota(jnp.int32, (size * rows, size), 1)
    spread = (keys == (me ^ (latent // rows))).astype(jnp.float32)

    def by_row(values):
        return jnp.dot(spread, values.astype(jnp.float32), precision=lax.Precision.HIGHEST)

    is_latent = by_row(order) == (latent % rows).astype(jnp.float32)
    code = jnp.sum(jnp.where(is_latent, by_row(token), 0.0), axis=1, keepdims=True)
    return (code + jnp.where(code < 0, -0.5, 0.5)).astype(jnp.int32)


def stream_kernel(size, rows, coef_ref, right_hbm, *refs):
    outs, (right, by_latent, by_slot, stage, sems_in, sems_out) = refs[:4], refs[4:]
    tokens, width = right.shape
    part = outs[0].shape[0]
    pieces, cuts = sems_in.shape
    tile, height = width // pieces, tokens // cuts
    reads, writes = [], []
    for i in range(pieces):
        columns = pl.ds(i * tile, tile)
        reads.append([])
        for cut in range(cuts):
            span = pl.ds(cut * height, height)
            reads[i].append(
                pltpu.make_async_copy(
                    right_hbm.at[span, columns], right.at[span, columns], sems_in.at[i, cut]
                )
            )
        for group, out in enumerate(outs):
            source = stage.at[pl.ds(group * part, part), columns]
            writes.append(pltpu.make_async_copy(source, out.at[:, columns], sems_out.at[i, group]))
    for read in sum(reads, []):
        read.start()
    by_latent[...] = coef_ref[...].T
    far_rows = by_slot.shape[0] // 2
    ordered_rows(
        size, rows, by_latent, (by_slot.at[pl.ds(0, far_rows)], by_slot.at[pl.ds(far_rows, far_rows)])
    )
    for i in range(pieces):
        for read in reads[i]:
            read.wait()
        columns = slice(i * tile, (i + 1) * tile)
        out = jnp.dot(by_slot[...], right[:, columns], preferred_element_type=jnp.float32)
        stage[:, columns] = out.astype(stage.dtype)
        for write in writes[4 * i : 4 * i + 4]:
            write.start()
    for write in writes:
        write.wait()


def stream_product(coef, right, size, rows):
    tokens, latents = coef.shape
    width = right.shape[1]
    part = latents // 4
    pieces, cuts = 4, 4
    anywhere = pl.BlockSpec(memory_space=pl.ANY)
    return pl.pallas_call(
        functools.partial(stream_kernel, size, rows),
        in_specs=[pl.BlockSpec(memory_space=pltpu.VMEM), anywhere],
        out_specs=[anywhere] * 4,
        out_shape=[jax.ShapeDtypeStruct((part, width), coef.dtype)] * 4,
        scratch_shapes=[
            pltpu.VMEM((tokens, width), coef.dtype),
            pltpu.VMEM((latents, tokens), coef.dtype),
            pltpu.VMEM((latents, tokens), coef.dtype),
            pltpu.VMEM((latents, width), coef.dtype),
            pltpu.SemaphoreType.DMA((pieces, cuts)),
            pltpu.SemaphoreType.DMA((pieces, 4)),
        ],
        compiler_params=params(50),
        cost_estimate=cost(
            2 * latents * tokens * width, 2 * (tokens * width + latents * (tokens + width))
        ),
        name="product",
    )(coef, right)


def multiply(left_ref, right_ref, outs):
    out = jnp.dot(left_ref[...], right_ref[...], preferred_element_type=jnp.float32)
    part = outs[0].shape[0]
    for i, ref in enumerate(outs):
        ref[...] = out[i * part : (i + 1) * part].astype(ref.dtype)


def select_far_kernel(size, rows, count, coef_ref, right_ref, picks_ref, *refs):
    pieces, refs = refs[:count], refs[count:]
    outs, near_left, own_code, (by_latent, left, table, codes) = refs[:2], refs[2], refs[3], refs[4:]

    @pl.when(pl.program_id(0) == 0)
    def _():
        height = size // count
        for i, piece in enumerate(pieces):
            table[i * height : (i + 1) * height] = piece[...]
        code = row_codes(size, rows, table[...], picks_ref)
        codes[...] = code
        own_code[...] = codes[pl.ds(pl.multiple_of(lax.axis_index("latent") * rows, rows), rows)]
        tokens = lax.broadcasted_iota(jnp.int32, by_latent.shape, 1)
        by_latent[...] = jnp.where(
            code == KEPT, coef_ref[...].T, (tokens == code).astype(by_latent.dtype)
        )
        ordered_rows(size, rows, by_latent, (left, near_left))

    multiply(left, right_ref, outs)


def near_kernel(left_ref, right_ref, *outs):
    multiply(left_ref, right_ref, outs)


def product(kernel, left, right, others, out_more, scratch, name):
    tokens, width = right.shape
    tile = 512
    part = left.size // tokens // (4 if out_more else 2)
    fixed = lambda j: (0, 0)
    in_specs = [pl.BlockSpec(left.shape, fixed), pl.BlockSpec((tokens, tile), lambda j: (0, j))]
    return pl.pallas_call(
        kernel,
        grid=(width // tile,),
        in_specs=in_specs + [pl.BlockSpec(value.shape, fixed) for value in others],
        out_specs=[pl.BlockSpec((part, tile), lambda j: (0, j))] * 2
        + [pl.BlockSpec(value.shape, fixed) for value in out_more],
        out_shape=[jax.ShapeDtypeStruct((part, width), left.dtype)] * 2 + list(out_more),
        scratch_shapes=scratch,
        compiler_params=params(20),
        cost_estimate=cost(
            4 * part * tokens * width, 2 * (tokens * width + 2 * part * (tokens + width))
        ),
        name=name,
    )(left, right, *others)


def far_product(coef, right, size, rows, picks, table):
    tokens, latents = coef.shape
    near_left = jax.ShapeDtypeStruct((latents // 2, tokens), coef.dtype)
    code = jax.ShapeDtypeStruct((rows, 1), jnp.int32)
    scratch = [
        pltpu.VMEM((latents, tokens), coef.dtype),
        pltpu.VMEM((latents // 2, tokens), coef.dtype),
        pltpu.VMEM((size, table[0].shape[1]), jnp.int32),
        pltpu.VMEM((latents, 1), jnp.int32),
    ]
    kernel = functools.partial(select_far_kernel, size, rows, len(table))
    others = [picks] + list(table)
    return product(kernel, coef, right, others, [near_left, code], scratch, "far_product")


def near_product(left, right):
    return product(near_kernel, left, right, [], [], [], "near_product")


def term(kept, from_core, slot, rows):
    slots = kept[0].shape[0] // rows
    group, begin = slot // slots, slot % slots * rows
    pair = (kept[group], from_core[group])
    return sum(value[begin : begin + rows].astype(jnp.float32) for value in pair)


def read_gradient(refs):
    return sum(ref[...].astype(jnp.float32) for ref in refs)


def enc_kernel(code_ref, w_ref, m_ref, v_ref, *refs):
    parts, (w_out, m_out, v_out, block, fresh) = refs[:-5], refs[-5:]
    gradient = read_gradient(parts)
    reset = code_ref[...] != KEPT
    w, m, v = adam_update(w_ref[...], m_ref[...], v_ref[...], gradient)
    w = jnp.where(reset, reset_gain * gradient * inverse_rms(gradient), w)
    w_out[...] = w
    m_out[...] = jnp.where(reset, 0.0, m)
    v_out[...] = jnp.where(reset, 0.0, v)
    block[...] = w.astype(block.dtype)
    fresh[...] = gradient.astype(fresh.dtype)


def dec_kernel(code_ref, w_ref, m_ref, v_ref, fresh_ref, enc_block, *refs):
    parts, (w_out, m_out, v_out, blocks) = refs[:-4], refs[-4:]
    reset = code_ref[...] != KEPT
    w, m, v = adam_update(w_ref[...], m_ref[...], v_ref[...], read_gradient(parts))
    w = jnp.where(reset, fresh_ref[...].astype(jnp.float32), w)
    w = w * inverse_rms(w)
    w_out[...] = w
    m_out[...] = jnp.where(reset, 0.0, m)
    v_out[...] = jnp.where(reset, 0.0, v)
    blocks[0] = enc_block[...]
    blocks[1] = w.astype(blocks.dtype)


def update(kernel, code, states, others, parts, last_shapes, name):
    rows, width = states[0].shape
    tile = 16

    def last_rows(value):
        skipped = (value.shape[0] - rows) // tile
        return pl.BlockSpec((tile, value.shape[1]), lambda i: (i + skipped, 0))

    operands = [code] + list(states) + list(others) + list(parts)
    out_shape = [jax.ShapeDtypeStruct((rows, width), jnp.float32)] * 3
    out_specs = [pl.BlockSpec((tile, width), lambda i: (i, 0))] * 3
    for pair in last_shapes:
        lead = (2,) if pair else ()
        out_shape.append(jax.ShapeDtypeStruct(lead + (rows, width), jnp.bfloat16))
        out_specs.append(
            pl.BlockSpec(lead + (tile, width), lambda i, pair=pair: (0, i, 0) if pair else (i, 0))
        )
    return pl.pallas_call(
        kernel,
        grid=(rows // tile,),
        in_specs=[last_rows(value) for value in operands],
        out_specs=out_specs,
        out_shape=out_shape,
        cost_estimate=cost(40 * rows * width, 40 * rows * width),
        compiler_params=params(12),
        name=name,
    )(*operands)


def place_kernel(plan, size, rows, count, *refs):
    pieces, outs, sems = refs[:count], refs[-3:-1], refs[-1]
    copies = []
    for i, (offset, other_core, column) in enumerate(plan):
        start = pl.multiple_of(owner_at(offset, other_core, size) * rows, rows)
        for whole, out in enumerate(outs):
            source = pieces[i].at[pl.ds(whole * rows, rows)]
            target = out.at[pl.ds(start, rows), pl.ds(column, pieces[i].shape[1])]
            copies.append(pltpu.make_async_copy(source, target, sems.at[i, whole]))
    for copy in copies:
        copy.start()
    for copy in copies:
        copy.wait()


def place(pieces, wholes, size, rows, width):
    operands = [value for _, _, _, value in pieces]
    plan = [piece[:3] for piece in pieces]
    count = len(operands)
    first = wholes is None
    if not first:
        operands += list(wholes)
    anywhere = pl.BlockSpec(memory_space=pl.ANY)
    return pl.pallas_call(
        functools.partial(place_kernel, plan, size, rows, count),
        out_shape=[jax.ShapeDtypeStruct((size * rows, width), operands[0].dtype)] * 2,
        in_specs=[anywhere] * len(operands),
        out_specs=[anywhere] * 2,
        scratch_shapes=[pltpu.SemaphoreType.DMA((count, 2))],
        input_output_aliases={} if first else {count: 0, count + 1: 1},
        compiler_params=params(4),
        cost_estimate=cost(0, 8 * count * rows * width),
        name="place",
    )(*operands)


def gathered(block, size, rows):
    chips = size // 2
    width = block.shape[1]
    half = width // 2
    hops = chips // 2
    right = left = block
    near, far, wholes = [(0, 0, 0, block)], [], None
    for hop in range(1, hops + 1):
        if hop == hops:
            right, left = right[:, :half], left[:, half:]
        right, left = shift(right, 1, size), shift(left, -1, size)
        sent = [(offset, 1, column, swap(value, 1, size)) for offset, _, column, value in near]
        wholes = place(near + far, wholes, size, rows, width)
        far = sent
        right, wholes = tied(right, wholes)
        left = after(left, right)
        near = [(-hop, 0, 0, right), (hop, 0, half if hop == hops else 0, left)]
    sent = [(offset, 1, column, swap(value, 1, size)) for offset, _, column, value in near]
    wholes = place(near + far, wholes, size, rows, width)
    return place(sent, wholes, size, rows, width)


def shards(
    x_rows,
    out_grad,
    enc_coef,
    latent_act,
    enc_w,
    enc_m,
    enc_v,
    dec_w,
    dec_m,
    dec_v,
    dead_order,
    pick_rows,
    send_count,
):
    rows, width = enc_w.shape
    half = width // 2
    size = lax.axis_size("latent")
    chips = size // 2
    stages = gather_table(jnp.concatenate([send_count, dead_order], axis=1), size)
    table = stages[-1]
    def begin(kept, from_core):
        far = term(kept, from_core, 0, rows).astype(jnp.bfloat16)
        return [far[:, :half], far[:, half:]]

    def travel(moving):
        return [shift(moving[0], 1, size), shift(moving[1], -1, size)]

    def advance(came, kept, from_core, hop, order):
        moving = []
        for side, value in enumerate(after(came, order)):
            value = value.astype(jnp.float32)
            if value.shape[1] < width:
                pads = ((0, 0, 0), (0, half, 0) if side == 0 else (half, 0, 0))
                value = lax.pad(value, jnp.float32(0), pads)
            value = value + term(kept, from_core, 2 * hop - side, rows)
            moving.append(value.astype(jnp.bfloat16))
        return travel(moving), moving

    dec = stream_product(latent_act, out_grad, size, rows)
    dec_far = after(dec[0], *stages[0])
    dec_kept, dec_core = [dec[1], dec[3]], [swap(dec_far, 1, size), swap(after(dec[2], table[0]), 1, size)]
    dec_moving = begin(dec_kept, after(dec_core, table[0]))
    enc_sent, kept, enc_left, code = far_product(
        after(enc_coef, *dec_moving), x_rows, size, rows, pick_rows[0].T, table
    )
    dec_came, enc_sent = tied(travel(dec_moving), enc_sent)
    enc_kept, enc_core = [kept], [swap(enc_sent, 1, size)]
    dec_came, order = advance(dec_came, dec_kept, dec_core, 1, enc_sent)
    enc_moving = begin(enc_kept, after(enc_core, order))
    enc_sent, kept = near_product(after(enc_left, *enc_moving), x_rows)
    enc_came, enc_sent = tied(travel(enc_moving), enc_sent)
    enc_kept.append(kept)
    enc_core.append(swap(enc_sent, 1, size))
    order = enc_sent
    for hop in range(1, chips // 2):
        if hop + 1 < chips // 2:
            dec_came, order = advance(dec_came, dec_kept, dec_core, hop + 1, order)
        else:
            order = (order, dec_came)
        enc_came, order = advance(enc_came, enc_kept, enc_core, hop, order)
    enc_out, enc_mo, enc_vo, enc_block, fresh = update(
        enc_kernel,
        code,
        (enc_w, enc_m, enc_v),
        (),
        [enc_kept[1], enc_core[1]] + enc_came,
        (False, False),
        "enc_update",
    )
    dec_out, dec_mo, dec_vo, blocks = update(
        dec_kernel,
        code,
        (dec_w, dec_m, dec_v),
        (fresh, enc_block),
        [dec_kept[1], dec_core[1]] + dec_came,
        (True,),
        "dec_update",
    )
    enc_full, dec_full = gathered(blocks.reshape(2 * rows, width), size, rows)
    return (enc_out, enc_mo, enc_vo, dec_out, dec_mo, dec_vo, enc_full, dec_full)


def solution(mesh):
    split = P(("groups", "latent"), None)
    placed = (split,) * 11 + (P(("groups", "latent"), None, None), split)
    return jax.shard_map(
        shards,
        mesh=mesh,
        in_specs=placed,
        out_specs=(split,) * 6 + (P("groups", None),) * 2,
        check_vma=False,
    )
```

```python
import functools

import jax
import jax.numpy as jnp
from jax import lax
from jax.experimental import pallas as pl
from jax.experimental.pallas import tpu as pltpu
from jax.sharding import PartitionSpec as P

beta_one = 0.9
beta_two = 0.99
first_fix = 1.0 - 0.9**4
second_fix = 1.0 - 0.99**4
learn_rate = 0.02
adam_eps = 1e-08
reset_gain = 0.01
norm_eps = 1e-06

KEPT = -1
ABSENT = -2


def adam_update(weight, moment, second, gradient):
    moment_new = beta_one * moment + (1.0 - beta_one) * gradient
    second_new = beta_two * second + (1.0 - beta_two) * gradient * gradient
    weight_new = weight - learn_rate * (moment_new / first_fix) / (
        jnp.sqrt(second_new / second_fix) + adam_eps
    )
    return (weight_new, moment_new, second_new)


def inverse_rms(value):
    return lax.rsqrt(jnp.mean(value * value, axis=1, keepdims=True) + norm_eps)


def swap(value, bits, size):
    return lax.ppermute(value, "latent", [(i, i ^ bits) for i in range(size)])


def after(value, *others):
    return lax.optimization_barrier((value,) + others)[0]


def tied(*values):
    return lax.optimization_barrier(values)


def params(mebibytes):
    return pltpu.CompilerParams(vmem_limit_bytes=mebibytes * 2**20)


def cost(flops, moved):
    return pl.CostEstimate(flops=int(flops), bytes_accessed=int(moved), transcendentals=0)


def chip_at(position, chips):
    return jnp.where(position < chips // 2, 2 * position, 2 * (chips - 1 - position) + 1)


def position_of(chip, chips):
    return jnp.where(chip % 2 == 0, chip // 2, chips - 1 - chip // 2)


def owner_at(offset, other_core, size):
    me = lax.axis_index("latent")
    chips = size // 2
    position = lax.rem(position_of(me // 2, chips) + offset + chips, chips)
    return 2 * chip_at(position, chips) + ((me % 2) ^ other_core)


def shift(value, step, size):
    chips = size // 2
    ring = [2 * q for q in range(chips // 2)] + [2 * q + 1 for q in reversed(range(chips // 2))]
    pairs = [
        (2 * ring[p] + core, 2 * ring[(p + step) % chips] + core)
        for p in range(chips)
        for core in range(2)
    ]
    return lax.ppermute(value, "latent", pairs)


def gather_table(row, size):
    stages, step = [], 1
    pieces = [row]
    while step < size:
        if step > 1:
            pieces = [jnp.concatenate(pieces, axis=0)]
        pieces += [swap(pieces[0], step * k, size) for k in range(1, min(4, size // step))]
        stages.append(pieces)
        step *= len(pieces)
    return stages


def ordered_rows(size, rows, by_latent, groups):
    chips = size // 2
    for block in range(size):
        group, inside = block // chips, block % chips
        slot = group * (chips // 2) + inside % (chips // 2)
        far = chips // 2 - slot // 2
        offset = far if slot % 2 == 0 else 1 - far
        owner = owner_at(offset, 1 - inside // (chips // 2), size)
        begin = pl.multiple_of(owner * rows, rows)
        groups[group][inside * rows : (inside + 1) * rows] = by_latent[pl.ds(begin, rows)]


def row_codes(size, rows, table, picks_ref):
    me = lax.axis_index("latent")
    counts = table[:, :size]
    order = table[:, size:]
    source = me ^ lax.broadcasted_iota(jnp.int32, (size, 1), 0)
    before = jnp.sum(jnp.where(source < me, counts, 0), axis=0, keepdims=True)
    total = jnp.sum(counts, axis=0, keepdims=True)
    owners = lax.broadcasted_iota(jnp.int32, (size, size), 1) == source

    def by_key(row):
        return jnp.sum(jnp.where(owners, row, 0), axis=1, keepdims=True)

    begin, here = by_key(before), by_key(counts[:1])
    place = lax.broadcasted_iota(jnp.int32, (size, rows), 1)
    token = jnp.full((size, rows), ABSENT, jnp.int32)
    for c in range(picks_ref.shape[0]):
        own = (place == begin + c) & (here > c)
        token = jnp.where(own, by_key(picks_ref[c : c + 1]), token)
    token = jnp.where(place < by_key(total), token, KEPT)
    latent = lax.broadcasted_iota(jnp.int32, (size * rows, 1), 0)
    keys = lax.broadcasted_iota(jnp.int32, (size * rows, size), 1)
    spread = (keys == (me ^ (latent // rows))).astype(jnp.float32)

    def by_row(values):
        return jnp.dot(spread, values.astype(jnp.float32), precision=lax.Precision.HIGHEST)

    is_latent = by_row(order) == (latent % rows).astype(jnp.float32)
    code = jnp.sum(jnp.where(is_latent, by_row(token), 0.0), axis=1, keepdims=True)
    return (code + jnp.where(code < 0, -0.5, 0.5)).astype(jnp.int32)


def stream_kernel(size, rows, coef_ref, right_hbm, *refs):
    outs, (right, by_latent, by_slot, stage, sems_in, sems_out) = refs[:4], refs[4:]
    tokens, width = right.shape
    part = outs[0].shape[0]
    pieces, cuts = sems_in.shape
    tile, height = width // pieces, tokens // cuts
    reads, writes = [], []
    for i in range(pieces):
        columns = pl.ds(i * tile, tile)
        reads.append([])
        for cut in range(cuts):
            span = pl.ds(cut * height, height)
            reads[i].append(
                pltpu.make_async_copy(
                    right_hbm.at[span, columns], right.at[span, columns], sems_in.at[i, cut]
                )
            )
        for group, out in enumerate(outs):
            source = stage.at[pl.ds(group * part, part), columns]
            writes.append(pltpu.make_async_copy(source, out.at[:, columns], sems_out.at[i, group]))
    for read in sum(reads, []):
        read.start()
    by_latent[...] = coef_ref[...].T
    far_rows = by_slot.shape[0] // 2
    ordered_rows(
        size, rows, by_latent, (by_slot.at[pl.ds(0, far_rows)], by_slot.at[pl.ds(far_rows, far_rows)])
    )
    for i in range(pieces):
        for read in reads[i]:
            read.wait()
        columns = slice(i * tile, (i + 1) * tile)
        out = jnp.dot(by_slot[...], right[:, columns], preferred_element_type=jnp.float32)
        stage[:, columns] = out.astype(stage.dtype)
        for write in writes[4 * i : 4 * i + 4]:
            write.start()
    for write in writes:
        write.wait()


def stream_product(coef, right, size, rows):
    tokens, latents = coef.shape
    width = right.shape[1]
    part = latents // 4
    pieces, cuts = 4, 4
    anywhere = pl.BlockSpec(memory_space=pl.ANY)
    return pl.pallas_call(
        functools.partial(stream_kernel, size, rows),
        in_specs=[pl.BlockSpec(memory_space=pltpu.VMEM), anywhere],
        out_specs=[anywhere] * 4,
        out_shape=[jax.ShapeDtypeStruct((part, width), coef.dtype)] * 4,
        scratch_shapes=[
            pltpu.VMEM((tokens, width), coef.dtype),
            pltpu.VMEM((latents, tokens), coef.dtype),
            pltpu.VMEM((latents, tokens), coef.dtype),
            pltpu.VMEM((latents, width), coef.dtype),
            pltpu.SemaphoreType.DMA((pieces, cuts)),
            pltpu.SemaphoreType.DMA((pieces, 4)),
        ],
        compiler_params=params(50),
        cost_estimate=cost(
            2 * latents * tokens * width, 2 * (tokens * width + latents * (tokens + width))
        ),
        name="product",
    )(coef, right)


def multiply(left_ref, right_ref, outs):
    out = jnp.dot(left_ref[...], right_ref[...], preferred_element_type=jnp.float32)
    part = outs[0].shape[0]
    for i, ref in enumerate(outs):
        ref[...] = out[i * part : (i + 1) * part].astype(ref.dtype)


def select_far_kernel(size, rows, count, coef_ref, right_ref, picks_ref, *refs):
    pieces, refs = refs[:count], refs[count:]
    outs, near_left, own_code, (by_latent, left, table, codes) = refs[:2], refs[2], refs[3], refs[4:]

    @pl.when(pl.program_id(0) == 0)
    def _():
        height = size // count
        for i, piece in enumerate(pieces):
            table[i * height : (i + 1) * height] = piece[...]
        code = row_codes(size, rows, table[...], picks_ref)
        codes[...] = code
        own_code[...] = codes[pl.ds(pl.multiple_of(lax.axis_index("latent") * rows, rows), rows)]
        tokens = lax.broadcasted_iota(jnp.int32, by_latent.shape, 1)
        by_latent[...] = jnp.where(
            code == KEPT, coef_ref[...].T, (tokens == code).astype(by_latent.dtype)
        )
        ordered_rows(size, rows, by_latent, (left, near_left))

    multiply(left, right_ref, outs)


def near_kernel(left_ref, right_ref, *outs):
    multiply(left_ref, right_ref, outs)


def product(kernel, left, right, others, out_more, scratch, name):
    tokens, width = right.shape
    tile = 512
    part = left.size // tokens // (4 if out_more else 2)
    fixed = lambda j: (0, 0)
    in_specs = [pl.BlockSpec(left.shape, fixed), pl.BlockSpec((tokens, tile), lambda j: (0, j))]
    return pl.pallas_call(
        kernel,
        grid=(width // tile,),
        in_specs=in_specs + [pl.BlockSpec(value.shape, fixed) for value in others],
        out_specs=[pl.BlockSpec((part, tile), lambda j: (0, j))] * 2
        + [pl.BlockSpec(value.shape, fixed) for value in out_more],
        out_shape=[jax.ShapeDtypeStruct((part, width), left.dtype)] * 2 + list(out_more),
        scratch_shapes=scratch,
        compiler_params=params(20),
        cost_estimate=cost(
            4 * part * tokens * width, 2 * (tokens * width + 2 * part * (tokens + width))
        ),
        name=name,
    )(left, right, *others)


def far_product(coef, right, size, rows, picks, table):
    tokens, latents = coef.shape
    near_left = jax.ShapeDtypeStruct((latents // 2, tokens), coef.dtype)
    code = jax.ShapeDtypeStruct((rows, 1), jnp.int32)
    scratch = [
        pltpu.VMEM((latents, tokens), coef.dtype),
        pltpu.VMEM((latents // 2, tokens), coef.dtype),
        pltpu.VMEM((size, table[0].shape[1]), jnp.int32),
        pltpu.VMEM((latents, 1), jnp.int32),
    ]
    kernel = functools.partial(select_far_kernel, size, rows, len(table))
    others = [picks] + list(table)
    return product(kernel, coef, right, others, [near_left, code], scratch, "far_product")


def near_product(left, right):
    return product(near_kernel, left, right, [], [], [], "near_product")


def term(kept, from_core, slot, rows):
    slots = kept[0].shape[0] // rows
    group, begin = slot // slots, slot % slots * rows
    pair = (kept[group], from_core[group])
    return sum(value[begin : begin + rows].astype(jnp.float32) for value in pair)


def updated(refs):
    code, states, terms = refs[0], refs[1:7], refs[7:15]
    reset = code[...] != KEPT
    enc_grad, dec_grad = (
        sum(ref[...].astype(jnp.float32) for ref in half) for half in (terms[:4], terms[4:])
    )
    enc = adam_update(*(ref[...] for ref in states[:3]), enc_grad)
    dec = adam_update(*(ref[...] for ref in states[3:]), dec_grad)
    enc_w = jnp.where(reset, reset_gain * enc_grad * inverse_rms(enc_grad), enc[0])
    dec_w = jnp.where(reset, enc_grad, dec[0])
    dec_w = dec_w * inverse_rms(dec_w)
    moments = [jnp.where(reset, 0.0, value) for value in enc[1:] + dec[1:]]
    return [enc_w] + moments[:2] + [dec_w] + moments[2:]


def blocks_kernel(*refs):
    results, blocks = updated(refs), refs[-1]
    blocks[0] = results[0].astype(blocks.dtype)
    blocks[1] = results[3].astype(blocks.dtype)


def states_kernel(*refs):
    for ref, value in zip(refs[-6:], updated(refs)):
        ref[...] = value


def update(code, states, enc_parts, dec_parts, came, blocks_only):
    rows, width = states[0].shape
    tile = 16

    def row_tile(value, skipped):
        return pl.BlockSpec((tile, value.shape[1]), lambda i: (i + skipped // tile, 0))

    operands = [(value, 0) for value in [code] + list(states)]
    for parts, first in ((enc_parts, 0), (dec_parts, rows)):
        operands += [(value, value.shape[0] - rows) for value in parts]
        operands += [(value, first) for value in came]
    if blocks_only:
        out_shape = [jax.ShapeDtypeStruct((2, rows, width), jnp.bfloat16)]
        out_specs = [pl.BlockSpec((2, tile, width), lambda i: (0, i, 0))]
    else:
        out_shape = [jax.ShapeDtypeStruct((rows, width), jnp.float32)] * 6
        out_specs = [pl.BlockSpec((tile, width), lambda i: (i, 0))] * 6
    return pl.pallas_call(
        blocks_kernel if blocks_only else states_kernel,
        grid=(rows // tile,),
        in_specs=[row_tile(*operand) for operand in operands],
        out_specs=out_specs,
        out_shape=out_shape,
        cost_estimate=cost(10 * rows * width, 10 * rows * width),
        compiler_params=params(20),
        name="blocks" if blocks_only else "states",
    )(*(value for value, _ in operands))


def place_kernel(plan, size, rows, count, *refs):
    pieces, outs, sems = refs[:count], refs[-3:-1], refs[-1]
    copies = []
    for i, (offset, other_core, column) in enumerate(plan):
        start = pl.multiple_of(owner_at(offset, other_core, size) * rows, rows)
        for whole, out in enumerate(outs):
            source = pieces[i].at[pl.ds(whole * rows, rows)]
            target = out.at[pl.ds(start, rows), pl.ds(column, pieces[i].shape[1])]
            copies.append(pltpu.make_async_copy(source, target, sems.at[i, whole]))
    for copy in copies:
        copy.start()
    for copy in copies:
        copy.wait()


def place(pieces, wholes, size, rows, width):
    operands = [value for _, _, _, value in pieces]
    plan = [piece[:3] for piece in pieces]
    count = len(operands)
    first = wholes is None
    if not first:
        operands += list(wholes)
    anywhere = pl.BlockSpec(memory_space=pl.ANY)
    return pl.pallas_call(
        functools.partial(place_kernel, plan, size, rows, count),
        out_shape=[jax.ShapeDtypeStruct((size * rows, width), operands[0].dtype)] * 2,
        in_specs=[anywhere] * len(operands),
        out_specs=[anywhere] * 2,
        scratch_shapes=[pltpu.SemaphoreType.DMA((count, 2))],
        input_output_aliases={} if first else {count: 0, count + 1: 1},
        compiler_params=params(4),
        cost_estimate=cost(0, 8 * count * rows * width),
        name="place",
    )(*operands)


def gathered(block, order, size, rows):
    chips = size // 2
    width = block.shape[1]
    half = width // 2
    hops = chips // 2
    right = left = block
    near, far, wholes = [(0, 0, 0, after(block, order))], [], None
    for hop in range(1, hops + 1):
        if hop == hops:
            right, left = right[:, :half], left[:, half:]
        right, left = shift(right, 1, size), shift(left, -1, size)
        sent = [(offset, 1, column, swap(value, 1, size)) for offset, _, column, value in near]
        wholes = place(near + far, wholes, size, rows, width)
        far = sent
        right, wholes = tied(right, wholes)
        left = after(left, right)
        near = [(-hop, 0, 0, right), (hop, 0, half if hop == hops else 0, left)]
    sent = [(offset, 1, column, swap(value, 1, size)) for offset, _, column, value in near]
    wholes = place(near, wholes, size, rows, width)
    return place(far + sent, wholes, size, rows, width)


def shards(
    x_rows,
    out_grad,
    enc_coef,
    latent_act,
    enc_w,
    enc_m,
    enc_v,
    dec_w,
    dec_m,
    dec_v,
    dead_order,
    pick_rows,
    send_count,
):
    rows, width = enc_w.shape
    half = width // 2
    size = lax.axis_size("latent")
    chips = size // 2
    stages = gather_table(jnp.concatenate([send_count, dead_order], axis=1), size)
    table = stages[-1]
    dec = stream_product(latent_act, out_grad, size, rows)
    dec_far = after(dec[0], *stages[0])
    dec_kept = [dec[1], dec[3]]
    dec_core = [swap(dec_far, 1, size), swap(after(dec[2], table[0]), 1, size)]
    enc_sent, kept, enc_left, code = far_product(
        enc_coef, x_rows, size, rows, pick_rows[0].T, table
    )
    enc_kept, enc_core = [kept], [swap(enc_sent, 1, size)]

    def both(slot):
        terms = [term(*pair, slot, rows) for pair in ((enc_kept, enc_core), (dec_kept, dec_core))]
        return jnp.concatenate(terms, axis=0)

    def travel(moving):
        return [shift(moving[0], 1, size), shift(moving[1], -1, size)]

    far = both(0).astype(jnp.bfloat16)
    moving = [far[:, :half], far[:, half:]]
    enc_sent, kept = near_product(after(enc_left, *moving), x_rows)
    came, enc_sent = tied(travel(moving), enc_sent)
    enc_kept.append(kept)
    enc_core.append(swap(enc_sent, 1, size))
    for hop in range(1, chips // 2):
        moving = []
        for side, value in enumerate(came):
            value = value.astype(jnp.float32)
            if value.shape[1] < width:
                pads = ((0, 0, 0), (0, half, 0) if side == 0 else (half, 0, 0))
                value = lax.pad(value, jnp.float32(0), pads)
            moving.append((value + both(2 * hop - side)).astype(jnp.bfloat16))
        came = travel(moving)
    states = (enc_w, enc_m, enc_v, dec_w, dec_m, dec_v)
    parts = ([enc_kept[1], enc_core[1]], [dec_kept[1], dec_core[1]], came)
    (blocks,) = update(code, states, *parts, True)
    results = update(code, after(states, blocks), *parts, False)
    enc_full, dec_full = gathered(blocks.reshape(2 * rows, width), results[0], size, rows)
    return (*results, enc_full, dec_full)


def solution(mesh):
    split = P(("groups", "latent"), None)
    placed = (split,) * 11 + (P(("groups", "latent"), None, None), split)
    return jax.shard_map(
        shards,
        mesh=mesh,
        in_specs=placed,
        out_specs=(split,) * 6 + (P("groups", None),) * 2,
        check_vma=False,
    )
```

```python
import functools

import jax
import jax.numpy as jnp
from jax import lax
from jax.experimental import pallas as pl
from jax.experimental.pallas import tpu as pltpu
from jax.sharding import PartitionSpec as P

beta_one = 0.9
beta_two = 0.99
first_fix = 1.0 - 0.9**4
second_fix = 1.0 - 0.99**4
learn_rate = 0.02
adam_eps = 1e-08
reset_gain = 0.01
norm_eps = 1e-06

KEPT = -1
ABSENT = -2


def adam_update(weight, moment, second, gradient):
    moment_new = beta_one * moment + (1.0 - beta_one) * gradient
    second_new = beta_two * second + (1.0 - beta_two) * gradient * gradient
    weight_new = weight - learn_rate * (moment_new / first_fix) / (
        jnp.sqrt(second_new / second_fix) + adam_eps
    )
    return (weight_new, moment_new, second_new)


def inverse_rms(value):
    return lax.rsqrt(jnp.mean(value * value, axis=1, keepdims=True) + norm_eps)


def swap(value, bits, size):
    return lax.ppermute(value, "latent", [(i, i ^ bits) for i in range(size)])


def after(value, *others):
    return lax.optimization_barrier((value,) + others)[0]


def tied(*values):
    return lax.optimization_barrier(values)


def params(mebibytes):
    return pltpu.CompilerParams(vmem_limit_bytes=mebibytes * 2**20)


def cost(flops, moved):
    return pl.CostEstimate(flops=int(flops), bytes_accessed=int(moved), transcendentals=0)


def chip_at(position, chips):
    return jnp.where(position < chips // 2, 2 * position, 2 * (chips - 1 - position) + 1)


def position_of(chip, chips):
    return jnp.where(chip % 2 == 0, chip // 2, chips - 1 - chip // 2)


def owner_at(offset, other_core, size):
    me = lax.axis_index("latent")
    chips = size // 2
    position = lax.rem(position_of(me // 2, chips) + offset + chips, chips)
    return 2 * chip_at(position, chips) + ((me % 2) ^ other_core)


def shift(value, step, size):
    chips = size // 2
    ring = [2 * q for q in range(chips // 2)] + [2 * q + 1 for q in reversed(range(chips // 2))]
    pairs = [
        (2 * ring[p] + core, 2 * ring[(p + step) % chips] + core)
        for p in range(chips)
        for core in range(2)
    ]
    return lax.ppermute(value, "latent", pairs)


def gather_table(row, size):
    stages, step = [], 1
    pieces = [row]
    while step < size:
        if step > 1:
            pieces = [jnp.concatenate(pieces, axis=0)]
        pieces += [swap(pieces[0], step * k, size) for k in range(1, min(4, size // step))]
        stages.append(pieces)
        step *= len(pieces)
    return stages


def ordered_rows(size, rows, by_latent, groups):
    chips = size // 2
    for block in range(size):
        group, inside = block // chips, block % chips
        slot = group * (chips // 2) + inside % (chips // 2)
        far = chips // 2 - slot // 2
        offset = far if slot % 2 == 0 else 1 - far
        owner = owner_at(offset, 1 - inside // (chips // 2), size)
        begin = pl.multiple_of(owner * rows, rows)
        groups[group][inside * rows : (inside + 1) * rows] = by_latent[pl.ds(begin, rows)]


def row_codes(size, rows, table, picks_ref):
    me = lax.axis_index("latent")
    counts = table[:, :size]
    order = table[:, size:]
    source = me ^ lax.broadcasted_iota(jnp.int32, (size, 1), 0)
    before = jnp.sum(jnp.where(source < me, counts, 0), axis=0, keepdims=True)
    total = jnp.sum(counts, axis=0, keepdims=True)
    owners = lax.broadcasted_iota(jnp.int32, (size, size), 1) == source

    def by_key(row):
        return jnp.sum(jnp.where(owners, row, 0), axis=1, keepdims=True)

    begin, here = by_key(before), by_key(counts[:1])
    place = lax.broadcasted_iota(jnp.int32, (size, rows), 1)
    token = jnp.full((size, rows), ABSENT, jnp.int32)
    for c in range(picks_ref.shape[0]):
        own = (place == begin + c) & (here > c)
        token = jnp.where(own, by_key(picks_ref[c : c + 1]), token)
    token = jnp.where(place < by_key(total), token, KEPT)
    latent = lax.broadcasted_iota(jnp.int32, (size * rows, 1), 0)
    keys = lax.broadcasted_iota(jnp.int32, (size * rows, size), 1)
    spread = (keys == (me ^ (latent // rows))).astype(jnp.float32)

    def by_row(values):
        return jnp.dot(spread, values.astype(jnp.float32), precision=lax.Precision.HIGHEST)

    is_latent = by_row(order) == (latent % rows).astype(jnp.float32)
    code = jnp.sum(jnp.where(is_latent, by_row(token), 0.0), axis=1, keepdims=True)
    return (code + jnp.where(code < 0, -0.5, 0.5)).astype(jnp.int32)


def stream_kernel(size, rows, coef_hbm, right_hbm, *refs):
    outs, near_left, refs = refs[:2], refs[2], refs[3:]
    coef, right, by_latent, left, near_rows, stage, sems_left, sems_in, sems_out = refs
    tokens, width = right.shape
    part = outs[0].shape[0]
    pieces, cuts = sems_in.shape
    tile, height = width // pieces, tokens // cuts
    reads, writes = [], []
    for i in range(pieces):
        columns = pl.ds(i * tile, tile)
        reads.append([])
        for cut in range(cuts):
            span = pl.ds(cut * height, height)
            reads[i].append(
                pltpu.make_async_copy(
                    right_hbm.at[span, columns], right.at[span, columns], sems_in.at[i, cut]
                )
            )
        for group, out in enumerate(outs):
            source = stage.at[pl.ds(group * part, part), columns]
            writes.append(pltpu.make_async_copy(source, out.at[:, columns], sems_out.at[i, group]))
    read_coef = pltpu.make_async_copy(coef_hbm, coef, sems_left.at[0])
    write_near = pltpu.make_async_copy(near_rows, near_left, sems_left.at[1])
    read_coef.start()
    for read in sum(reads, []):
        read.start()
    read_coef.wait()
    by_latent[...] = coef[...].T
    ordered_rows(size, rows, by_latent, (left, near_rows))
    write_near.start()
    for i in range(pieces):
        for read in reads[i]:
            read.wait()
        columns = slice(i * tile, (i + 1) * tile)
        out = jnp.dot(left[...], right[:, columns], preferred_element_type=jnp.float32)
        stage[:, columns] = out.astype(stage.dtype)
        for write in writes[2 * i : 2 * i + 2]:
            write.start()
    for write in writes + [write_near]:
        write.wait()


def stream_far_product(coef, right, size, rows):
    tokens, latents = coef.shape
    width = right.shape[1]
    part, half = latents // 4, latents // 2
    pieces, cuts = 4, 4
    anywhere = pl.BlockSpec(memory_space=pl.ANY)
    return pl.pallas_call(
        functools.partial(stream_kernel, size, rows),
        in_specs=[anywhere] * 2,
        out_specs=[anywhere] * 3,
        out_shape=[jax.ShapeDtypeStruct((part, width), coef.dtype)] * 2
        + [jax.ShapeDtypeStruct((half, tokens), coef.dtype)],
        scratch_shapes=[
            pltpu.VMEM((tokens, latents), coef.dtype),
            pltpu.VMEM((tokens, width), coef.dtype),
            pltpu.VMEM((latents, tokens), coef.dtype),
            pltpu.VMEM((half, tokens), coef.dtype),
            pltpu.VMEM((half, tokens), coef.dtype),
            pltpu.VMEM((half, width), coef.dtype),
            pltpu.SemaphoreType.DMA((2,)),
            pltpu.SemaphoreType.DMA((pieces, cuts)),
            pltpu.SemaphoreType.DMA((pieces, 2)),
        ],
        compiler_params=params(52),
        cost_estimate=cost(
            latents * tokens * width, 2 * (tokens * width + latents * tokens) + latents * width
        ),
        name="stream_far_product",
    )(coef, right)


def multiply(left_ref, right_ref, outs):
    out = jnp.dot(left_ref[...], right_ref[...], preferred_element_type=jnp.float32)
    part = outs[0].shape[0]
    for i, ref in enumerate(outs):
        ref[...] = out[i * part : (i + 1) * part].astype(ref.dtype)


def select_far_kernel(size, rows, count, coef_ref, right_ref, picks_ref, *refs):
    pieces, refs = refs[:count], refs[count:]
    outs, near_left, own_code, (by_latent, left, table, codes) = refs[:2], refs[2], refs[3], refs[4:]

    @pl.when(pl.program_id(0) == 0)
    def _():
        height = size // count
        for i, piece in enumerate(pieces):
            table[i * height : (i + 1) * height] = piece[...]
        code = row_codes(size, rows, table[...], picks_ref)
        codes[...] = code
        own_code[...] = codes[pl.ds(pl.multiple_of(lax.axis_index("latent") * rows, rows), rows)]
        tokens = lax.broadcasted_iota(jnp.int32, by_latent.shape, 1)
        by_latent[...] = jnp.where(
            code == KEPT, coef_ref[...].T, (tokens == code).astype(by_latent.dtype)
        )
        ordered_rows(size, rows, by_latent, (left, near_left))

    multiply(left, right_ref, outs)


def near_kernel(left_ref, right_ref, *outs):
    multiply(left_ref, right_ref, outs)


def product(kernel, left, right, others, out_more, scratch, name):
    tokens, width = right.shape
    tile = 512
    part = left.size // tokens // (4 if out_more else 2)
    fixed = lambda j: (0, 0)
    in_specs = [pl.BlockSpec(left.shape, fixed), pl.BlockSpec((tokens, tile), lambda j: (0, j))]
    return pl.pallas_call(
        kernel,
        grid=(width // tile,),
        in_specs=in_specs + [pl.BlockSpec(value.shape, fixed) for value in others],
        out_specs=[pl.BlockSpec((part, tile), lambda j: (0, j))] * 2
        + [pl.BlockSpec(value.shape, fixed) for value in out_more],
        out_shape=[jax.ShapeDtypeStruct((part, width), left.dtype)] * 2 + list(out_more),
        scratch_shapes=scratch,
        compiler_params=params(20),
        cost_estimate=cost(
            12 * part * tokens * width, 2 * (tokens * width + 2 * part * (tokens + width))
        ),
        name=name,
    )(left, right, *others)


def far_product(coef, right, size, rows, picks, table):
    tokens, latents = coef.shape
    near_left = jax.ShapeDtypeStruct((latents // 2, tokens), coef.dtype)
    code = jax.ShapeDtypeStruct((rows, 1), jnp.int32)
    scratch = [
        pltpu.VMEM((latents, tokens), coef.dtype),
        pltpu.VMEM((latents // 2, tokens), coef.dtype),
        pltpu.VMEM((size, table[0].shape[1]), jnp.int32),
        pltpu.VMEM((latents, 1), jnp.int32),
    ]
    kernel = functools.partial(select_far_kernel, size, rows, len(table))
    others = [picks] + list(table)
    return product(kernel, coef, right, others, [near_left, code], scratch, "far_product")


def near_product(left, right):
    return product(near_kernel, left, right, [], [], [], "near_product")


def term(kept, from_core, slot, rows):
    slots = kept[0].shape[0] // rows
    group, begin = slot // slots, slot % slots * rows
    pair = (kept[group], from_core[group])
    return sum(value[begin : begin + rows].astype(jnp.float32) for value in pair)


def updated(refs):
    code, states, terms = refs[0], refs[1:7], refs[7:15]
    reset = code[...] != KEPT
    enc_grad, dec_grad = (
        sum(ref[...].astype(jnp.float32) for ref in half) for half in (terms[:4], terms[4:])
    )
    enc = adam_update(*(ref[...] for ref in states[:3]), enc_grad)
    dec = adam_update(*(ref[...] for ref in states[3:]), dec_grad)
    enc_w = jnp.where(reset, reset_gain * enc_grad * inverse_rms(enc_grad), enc[0])
    dec_w = jnp.where(reset, enc_grad, dec[0])
    dec_w = dec_w * inverse_rms(dec_w)
    moments = [jnp.where(reset, 0.0, value) for value in enc[1:] + dec[1:]]
    return [enc_w] + moments[:2] + [dec_w] + moments[2:]


def blocks_kernel(*refs):
    results, blocks = updated(refs), refs[-1]
    blocks[0] = results[0].astype(blocks.dtype)
    blocks[1] = results[3].astype(blocks.dtype)


def states_kernel(*refs):
    for ref, value in zip(refs[-6:], updated(refs)):
        ref[...] = value


def update(code, states, enc_parts, dec_parts, came, blocks_only):
    rows, width = states[0].shape
    tile = 16

    def row_tile(value, skipped):
        return pl.BlockSpec((tile, value.shape[1]), lambda i: (i + skipped // tile, 0))

    operands = [(value, 0) for value in [code] + list(states)]
    for parts, first in ((enc_parts, 0), (dec_parts, rows)):
        operands += [(value, value.shape[0] - rows) for value in parts]
        operands += [(value, first) for value in came]
    if blocks_only:
        out_shape = [jax.ShapeDtypeStruct((2, rows, width), jnp.bfloat16)]
        out_specs = [pl.BlockSpec((2, tile, width), lambda i: (0, i, 0))]
    else:
        out_shape = [jax.ShapeDtypeStruct((rows, width), jnp.float32)] * 6
        out_specs = [pl.BlockSpec((tile, width), lambda i: (i, 0))] * 6
    return pl.pallas_call(
        blocks_kernel if blocks_only else states_kernel,
        grid=(rows // tile,),
        in_specs=[row_tile(*operand) for operand in operands],
        out_specs=out_specs,
        out_shape=out_shape,
        cost_estimate=cost(10 * rows * width, 10 * rows * width),
        compiler_params=params(20),
        name="blocks" if blocks_only else "states",
    )(*(value for value, _ in operands))


def place_kernel(plan, size, rows, count, *refs):
    pieces, outs, sems = refs[:count], refs[-3:-1], refs[-1]
    copies = []
    for i, (offset, other_core, column) in enumerate(plan):
        start = pl.multiple_of(owner_at(offset, other_core, size) * rows, rows)
        for whole, out in enumerate(outs):
            source = pieces[i].at[pl.ds(whole * rows, rows)]
            target = out.at[pl.ds(start, rows), pl.ds(column, pieces[i].shape[1])]
            copies.append(pltpu.make_async_copy(source, target, sems.at[i, whole]))
    for copy in copies:
        copy.start()
    for copy in copies:
        copy.wait()


def place(pieces, wholes, size, rows, width):
    operands = [value for _, _, _, value in pieces]
    plan = [piece[:3] for piece in pieces]
    count = len(operands)
    first = wholes is None
    if not first:
        operands += list(wholes)
    anywhere = pl.BlockSpec(memory_space=pl.ANY)
    return pl.pallas_call(
        functools.partial(place_kernel, plan, size, rows, count),
        out_shape=[jax.ShapeDtypeStruct((size * rows, width), operands[0].dtype)] * 2,
        in_specs=[anywhere] * len(operands),
        out_specs=[anywhere] * 2,
        scratch_shapes=[pltpu.SemaphoreType.DMA((count, 2))],
        input_output_aliases={} if first else {count: 0, count + 1: 1},
        compiler_params=params(4),
        cost_estimate=cost(0, 8 * count * rows * width),
        name="place",
    )(*operands)


def gathered(block, order, size, rows):
    chips = size // 2
    width = block.shape[1]
    half = width // 2
    hops = chips // 2
    right = left = block
    near, far, wholes = [(0, 0, 0, after(block, order))], [], None
    for hop in range(1, hops + 1):
        if hop == hops:
            right, left = right[:, :half], left[:, half:]
        right, left = shift(right, 1, size), shift(left, -1, size)
        sent = [(offset, 1, column, swap(value, 1, size)) for offset, _, column, value in near]
        wholes = place(near + far, wholes, size, rows, width)
        far = sent
        right, wholes = tied(right, wholes)
        left = after(left, right)
        near = [(-hop, 0, 0, right), (hop, 0, half if hop == hops else 0, left)]
    sent = [(offset, 1, column, swap(value, 1, size)) for offset, _, column, value in near]
    wholes = place(near, wholes, size, rows, width)
    return place(far + sent, wholes, size, rows, width)


def shards(
    x_rows,
    out_grad,
    enc_coef,
    latent_act,
    enc_w,
    enc_m,
    enc_v,
    dec_w,
    dec_m,
    dec_v,
    dead_order,
    pick_rows,
    send_count,
):
    rows, width = enc_w.shape
    half = width // 2
    size = lax.axis_size("latent")
    chips = size // 2
    stages = gather_table(jnp.concatenate([send_count, dead_order], axis=1), size)
    table = stages[-1]
    dec_sent, kept, dec_left = stream_far_product(latent_act, out_grad, size, rows)
    dec_sent = after(dec_sent, *stages[0])
    dec_kept, dec_core = [kept], [swap(dec_sent, 1, size)]
    enc_sent, kept, enc_left, code = far_product(
        after(enc_coef, dec_sent), x_rows, size, rows, pick_rows[0].T, table
    )
    enc_kept, enc_core = [kept], [swap(enc_sent, 1, size)]

    def both(slot):
        terms = [term(*pair, slot, rows) for pair in ((enc_kept, enc_core), (dec_kept, dec_core))]
        return jnp.concatenate(terms, axis=0)

    def travel(moving):
        return [shift(moving[0], 1, size), shift(moving[1], -1, size)]

    far = both(0).astype(jnp.bfloat16)
    moving = [far[:, :half], far[:, half:]]
    enc_sent, kept = near_product(after(enc_left, *moving), x_rows)
    came, enc_sent = tied(travel(moving), enc_sent)
    enc_kept.append(kept)
    enc_core.append(swap(enc_sent, 1, size))
    for hop in range(1, chips // 2):
        moving = []
        for side, value in enumerate(came):
            value = value.astype(jnp.float32)
            if value.shape[1] < width:
                pads = ((0, 0, 0), (0, half, 0) if side == 0 else (half, 0, 0))
                value = lax.pad(value, jnp.float32(0), pads)
            moving.append((value + both(2 * hop - side)).astype(jnp.bfloat16))
        came = travel(moving)
        if hop == 1:
            dec_sent, kept = near_product(after(dec_left, *moving), out_grad)
            dec_kept.append(kept)
            dec_core.append(swap(dec_sent, 1, size))
    states = (enc_w, enc_m, enc_v, dec_w, dec_m, dec_v)
    parts = ([enc_kept[1], enc_core[1]], [dec_kept[1], dec_core[1]], came)
    (blocks,) = update(code, states, *parts, True)
    results = update(code, after(states, blocks), *parts, False)
    enc_full, dec_full = gathered(blocks.reshape(2 * rows, width), results[0], size, rows)
    return (*results, enc_full, dec_full)


def solution(mesh):
    split = P(("groups", "latent"), None)
    placed = (split,) * 11 + (P(("groups", "latent"), None, None), split)
    return jax.shard_map(
        shards,
        mesh=mesh,
        in_specs=placed,
        out_specs=(split,) * 6 + (P("groups", None),) * 2,
        check_vma=False,
    )
```

```python
import functools

import jax
import jax.numpy as jnp
from jax import lax
from jax.experimental import pallas as pl
from jax.experimental.pallas import tpu as pltpu
from jax.sharding import PartitionSpec as P

beta_one = 0.9
beta_two = 0.99
first_fix = 1.0 - 0.9**4
second_fix = 1.0 - 0.99**4
learn_rate = 0.02
adam_eps = 1e-08
reset_gain = 0.01
norm_eps = 1e-06

KEPT = -1
ABSENT = -2


def adam_update(weight, moment, second, gradient):
    moment_new = beta_one * moment + (1.0 - beta_one) * gradient
    second_new = beta_two * second + (1.0 - beta_two) * gradient * gradient
    weight_new = weight - learn_rate * (moment_new / first_fix) / (
        jnp.sqrt(second_new / second_fix) + adam_eps
    )
    return (weight_new, moment_new, second_new)


def inverse_rms(value):
    return lax.rsqrt(jnp.mean(value * value, axis=1, keepdims=True) + norm_eps)


def swap(value, bits, size):
    return lax.ppermute(value, "latent", [(i, i ^ bits) for i in range(size)])


def after(value, *others):
    return lax.optimization_barrier((value,) + others)[0]


def tied(*values):
    return lax.optimization_barrier(values)


def params(mebibytes):
    return pltpu.CompilerParams(vmem_limit_bytes=mebibytes * 2**20)


def cost(flops, moved):
    return pl.CostEstimate(flops=int(flops), bytes_accessed=int(moved), transcendentals=0)


def chip_at(position, chips):
    return jnp.where(position < chips // 2, 2 * position, 2 * (chips - 1 - position) + 1)


def position_of(chip, chips):
    return jnp.where(chip % 2 == 0, chip // 2, chips - 1 - chip // 2)


def owner_at(offset, other_core, size):
    me = lax.axis_index("latent")
    chips = size // 2
    position = lax.rem(position_of(me // 2, chips) + offset + chips, chips)
    return 2 * chip_at(position, chips) + ((me % 2) ^ other_core)


def shift(value, step, size):
    chips = size // 2
    ring = [2 * q for q in range(chips // 2)] + [2 * q + 1 for q in reversed(range(chips // 2))]
    pairs = [
        (2 * ring[p] + core, 2 * ring[(p + step) % chips] + core)
        for p in range(chips)
        for core in range(2)
    ]
    return lax.ppermute(value, "latent", pairs)


def gather_table(row, size):
    stages, step = [], 1
    pieces = [row]
    while step < size:
        if step > 1:
            pieces = [jnp.concatenate(pieces, axis=0)]
        pieces += [swap(pieces[0], step * k, size) for k in range(1, min(4, size // step))]
        stages.append(pieces)
        step *= len(pieces)
    return stages


def ordered_rows(size, rows, by_latent, groups):
    chips = size // 2
    for block in range(size):
        group, inside = block // chips, block % chips
        slot = group * (chips // 2) + inside % (chips // 2)
        far = chips // 2 - slot // 2
        offset = far if slot % 2 == 0 else 1 - far
        owner = owner_at(offset, 1 - inside // (chips // 2), size)
        begin = pl.multiple_of(owner * rows, rows)
        groups[group][inside * rows : (inside + 1) * rows] = by_latent[pl.ds(begin, rows)]


def row_codes(size, rows, table, picks_ref):
    me = lax.axis_index("latent")
    counts = table[:, :size]
    order = table[:, size:]
    source = me ^ lax.broadcasted_iota(jnp.int32, (size, 1), 0)
    before = jnp.sum(jnp.where(source < me, counts, 0), axis=0, keepdims=True)
    total = jnp.sum(counts, axis=0, keepdims=True)
    owners = lax.broadcasted_iota(jnp.int32, (size, size), 1) == source

    def by_key(row):
        return jnp.sum(jnp.where(owners, row, 0), axis=1, keepdims=True)

    begin, here = by_key(before), by_key(counts[:1])
    place = lax.broadcasted_iota(jnp.int32, (size, rows), 1)
    token = jnp.full((size, rows), ABSENT, jnp.int32)
    for c in range(picks_ref.shape[0]):
        own = (place == begin + c) & (here > c)
        token = jnp.where(own, by_key(picks_ref[c : c + 1]), token)
    token = jnp.where(place < by_key(total), token, KEPT)
    latent = lax.broadcasted_iota(jnp.int32, (size * rows, 1), 0)
    keys = lax.broadcasted_iota(jnp.int32, (size * rows, size), 1)
    spread = (keys == (me ^ (latent // rows))).astype(jnp.float32)

    def by_row(values):
        return jnp.dot(spread, values.astype(jnp.float32), precision=lax.Precision.HIGHEST)

    is_latent = by_row(order) == (latent % rows).astype(jnp.float32)
    code = jnp.sum(jnp.where(is_latent, by_row(token), 0.0), axis=1, keepdims=True)
    return (code + jnp.where(code < 0, -0.5, 0.5)).astype(jnp.int32)


def stream_kernel(size, rows, coef_hbm, right_hbm, *refs):
    outs, near_left, refs = refs[:2], refs[2], refs[3:]
    coef, right, by_latent, left, near_rows, total, stage, sems_left, sems_in, sems_out = refs
    tokens, width = right.shape
    part = outs[0].shape[0]
    cuts, pieces, passes = sems_in.shape[0], sems_out.shape[0], 2
    tile, height, depth = width // pieces, tokens // cuts, tokens // passes
    reads, writes = [], []
    for cut in range(cuts):
        span = pl.ds(cut * height, height)
        reads.append(pltpu.make_async_copy(right_hbm.at[span], right.at[span], sems_in.at[cut]))
    for i in range(pieces):
        columns = pl.ds(i * tile, tile)
        for group, out in enumerate(outs):
            source = stage.at[pl.ds(group * part, part), columns]
            writes.append(pltpu.make_async_copy(source, out.at[:, columns], sems_out.at[i, group]))
    read_coef = pltpu.make_async_copy(coef_hbm, coef, sems_left.at[0])
    write_near = pltpu.make_async_copy(near_rows, near_left, sems_left.at[1])
    read_coef.start()
    for read in reads:
        read.start()
    read_coef.wait()
    by_latent[...] = coef[...].T
    ordered_rows(size, rows, by_latent, (left, near_rows))
    write_near.start()
    for step in range(passes):
        for read in reads[step * cuts // passes : (step + 1) * cuts // passes]:
            read.wait()
        span = slice(step * depth, (step + 1) * depth)
        for i in range(pieces):
            columns = slice(i * tile, (i + 1) * tile)
            out = jnp.dot(left[:, span], right[span, columns], preferred_element_type=jnp.float32)
            if step > 0:
                out = out + total[:, columns]
            if step < passes - 1:
                total[:, columns] = out
            else:
                stage[:, columns] = out.astype(stage.dtype)
                for write in writes[2 * i : 2 * i + 2]:
                    write.start()
    for write in writes + [write_near]:
        write.wait()


def stream_far_product(coef, right, size, rows):
    tokens, latents = coef.shape
    width = right.shape[1]
    part, half = latents // 4, latents // 2
    pieces, cuts = 4, 8
    anywhere = pl.BlockSpec(memory_space=pl.ANY)
    return pl.pallas_call(
        functools.partial(stream_kernel, size, rows),
        in_specs=[anywhere] * 2,
        out_specs=[anywhere] * 3,
        out_shape=[jax.ShapeDtypeStruct((part, width), coef.dtype)] * 2
        + [jax.ShapeDtypeStruct((half, tokens), coef.dtype)],
        scratch_shapes=[
            pltpu.VMEM((tokens, latents), coef.dtype),
            pltpu.VMEM((tokens, width), coef.dtype),
            pltpu.VMEM((latents, tokens), coef.dtype),
            pltpu.VMEM((half, tokens), coef.dtype),
            pltpu.VMEM((half, tokens), coef.dtype),
            pltpu.VMEM((half, width), jnp.float32),
            pltpu.VMEM((half, width), coef.dtype),
            pltpu.SemaphoreType.DMA((2,)),
            pltpu.SemaphoreType.DMA((cuts,)),
            pltpu.SemaphoreType.DMA((pieces, 2)),
        ],
        compiler_params=params(52),
        cost_estimate=cost(
            latents * tokens * width, 2 * (tokens * width + latents * tokens) + latents * width
        ),
        name="stream_far_product",
    )(coef, right)


def multiply(left_ref, right_ref, outs):
    out = jnp.dot(left_ref[...], right_ref[...], preferred_element_type=jnp.float32)
    part = outs[0].shape[0]
    for i, ref in enumerate(outs):
        ref[...] = out[i * part : (i + 1) * part].astype(ref.dtype)


def select_far_kernel(size, rows, count, coef_ref, right_ref, picks_ref, *refs):
    pieces, refs = refs[:count], refs[count:]
    outs, near_left, own_code, (by_latent, left, table, codes) = refs[:2], refs[2], refs[3], refs[4:]

    @pl.when(pl.program_id(0) == 0)
    def _():
        height = size // count
        for i, piece in enumerate(pieces):
            table[i * height : (i + 1) * height] = piece[...]
        code = row_codes(size, rows, table[...], picks_ref)
        codes[...] = code
        own_code[...] = codes[pl.ds(pl.multiple_of(lax.axis_index("latent") * rows, rows), rows)]
        tokens = lax.broadcasted_iota(jnp.int32, by_latent.shape, 1)
        by_latent[...] = jnp.where(
            code == KEPT, coef_ref[...].T, (tokens == code).astype(by_latent.dtype)
        )
        ordered_rows(size, rows, by_latent, (left, near_left))

    multiply(left, right_ref, outs)


def near_kernel(left_ref, right_ref, *outs):
    multiply(left_ref, right_ref, outs)


def product(kernel, left, right, others, out_more, scratch, name):
    tokens, width = right.shape
    tile = 512
    part = left.size // tokens // (4 if out_more else 2)
    fixed = lambda j: (0, 0)
    in_specs = [pl.BlockSpec(left.shape, fixed), pl.BlockSpec((tokens, tile), lambda j: (0, j))]
    return pl.pallas_call(
        kernel,
        grid=(width // tile,),
        in_specs=in_specs + [pl.BlockSpec(value.shape, fixed) for value in others],
        out_specs=[pl.BlockSpec((part, tile), lambda j: (0, j))] * 2
        + [pl.BlockSpec(value.shape, fixed) for value in out_more],
        out_shape=[jax.ShapeDtypeStruct((part, width), left.dtype)] * 2 + list(out_more),
        scratch_shapes=scratch,
        compiler_params=params(20),
        cost_estimate=cost(
            12 * part * tokens * width, 2 * (tokens * width + 2 * part * (tokens + width))
        ),
        name=name,
    )(left, right, *others)


def far_product(coef, right, size, rows, picks, table):
    tokens, latents = coef.shape
    near_left = jax.ShapeDtypeStruct((latents // 2, tokens), coef.dtype)
    code = jax.ShapeDtypeStruct((rows, 1), jnp.int32)
    scratch = [
        pltpu.VMEM((latents, tokens), coef.dtype),
        pltpu.VMEM((latents // 2, tokens), coef.dtype),
        pltpu.VMEM((size, table[0].shape[1]), jnp.int32),
        pltpu.VMEM((latents, 1), jnp.int32),
    ]
    kernel = functools.partial(select_far_kernel, size, rows, len(table))
    others = [picks] + list(table)
    return product(kernel, coef, right, others, [near_left, code], scratch, "far_product")


def near_product(left, right):
    return product(near_kernel, left, right, [], [], [], "near_product")


def term(kept, from_core, slot, rows):
    slots = kept[0].shape[0] // rows
    group, begin = slot // slots, slot % slots * rows
    pair = (kept[group], from_core[group])
    return sum(value[begin : begin + rows].astype(jnp.float32) for value in pair)


def updated(refs):
    code, states, terms = refs[0], refs[1:7], refs[7:15]
    reset = code[...] != KEPT
    enc_grad, dec_grad = (
        sum(ref[...].astype(jnp.float32) for ref in half) for half in (terms[:4], terms[4:])
    )
    enc = adam_update(*(ref[...] for ref in states[:3]), enc_grad)
    dec = adam_update(*(ref[...] for ref in states[3:]), dec_grad)
    enc_w = jnp.where(reset, reset_gain * enc_grad * inverse_rms(enc_grad), enc[0])
    dec_w = jnp.where(reset, enc_grad, dec[0])
    dec_w = dec_w * inverse_rms(dec_w)
    moments = [jnp.where(reset, 0.0, value) for value in enc[1:] + dec[1:]]
    return [enc_w] + moments[:2] + [dec_w] + moments[2:]


def blocks_kernel(*refs):
    results, blocks = updated(refs), refs[-1]
    blocks[0] = results[0].astype(blocks.dtype)
    blocks[1] = results[3].astype(blocks.dtype)


def states_kernel(*refs):
    for ref, value in zip(refs[-6:], updated(refs)):
        ref[...] = value


def update(code, states, enc_parts, dec_parts, came, blocks_only):
    rows, width = states[0].shape
    tile = 16

    def row_tile(value, skipped):
        return pl.BlockSpec((tile, value.shape[1]), lambda i: (i + skipped // tile, 0))

    operands = [(value, 0) for value in [code] + list(states)]
    for parts, first in ((enc_parts, 0), (dec_parts, rows)):
        operands += [(value, value.shape[0] - rows) for value in parts]
        operands += [(value, first) for value in came]
    if blocks_only:
        out_shape = [jax.ShapeDtypeStruct((2, rows, width), jnp.bfloat16)]
        out_specs = [pl.BlockSpec((2, tile, width), lambda i: (0, i, 0))]
    else:
        out_shape = [jax.ShapeDtypeStruct((rows, width), jnp.float32)] * 6
        out_specs = [pl.BlockSpec((tile, width), lambda i: (i, 0))] * 6
    return pl.pallas_call(
        blocks_kernel if blocks_only else states_kernel,
        grid=(rows // tile,),
        in_specs=[row_tile(*operand) for operand in operands],
        out_specs=out_specs,
        out_shape=out_shape,
        cost_estimate=cost(10 * rows * width, 10 * rows * width),
        compiler_params=params(20),
        name="blocks" if blocks_only else "states",
    )(*(value for value, _ in operands))


def place_kernel(plan, size, rows, count, *refs):
    pieces, outs, sems = refs[:count], refs[-3:-1], refs[-1]
    copies = []
    for i, (offset, other_core, column) in enumerate(plan):
        start = pl.multiple_of(owner_at(offset, other_core, size) * rows, rows)
        for whole, out in enumerate(outs):
            source = pieces[i].at[pl.ds(whole * rows, rows)]
            target = out.at[pl.ds(start, rows), pl.ds(column, pieces[i].shape[1])]
            copies.append(pltpu.make_async_copy(source, target, sems.at[i, whole]))
    for copy in copies:
        copy.start()
    for copy in copies:
        copy.wait()


def place(pieces, wholes, size, rows, width):
    operands = [value for _, _, _, value in pieces]
    plan = [piece[:3] for piece in pieces]
    count = len(operands)
    first = wholes is None
    if not first:
        operands += list(wholes)
    anywhere = pl.BlockSpec(memory_space=pl.ANY)
    return pl.pallas_call(
        functools.partial(place_kernel, plan, size, rows, count),
        out_shape=[jax.ShapeDtypeStruct((size * rows, width), operands[0].dtype)] * 2,
        in_specs=[anywhere] * len(operands),
        out_specs=[anywhere] * 2,
        scratch_shapes=[pltpu.SemaphoreType.DMA((count, 2))],
        input_output_aliases={} if first else {count: 0, count + 1: 1},
        compiler_params=params(4),
        cost_estimate=cost(0, 8 * count * rows * width),
        name="place",
    )(*operands)


def gathered(block, order, size, rows):
    chips = size // 2
    width = block.shape[1]
    half = width // 2
    hops = chips // 2
    right = left = block
    near, far, wholes = [(0, 0, 0, after(block, order))], [], None
    for hop in range(1, hops + 1):
        if hop == hops:
            right, left = right[:, :half], left[:, half:]
        right, left = shift(right, 1, size), shift(left, -1, size)
        sent = [(offset, 1, column, swap(value, 1, size)) for offset, _, column, value in near]
        wholes = place(near + far, wholes, size, rows, width)
        far = sent
        right, wholes = tied(right, wholes)
        left = after(left, right)
        near = [(-hop, 0, 0, right), (hop, 0, half if hop == hops else 0, left)]
    sent = [(offset, 1, column, swap(value, 1, size)) for offset, _, column, value in near]
    wholes = place(near, wholes, size, rows, width)
    return place(far + sent, wholes, size, rows, width)


def shards(
    x_rows,
    out_grad,
    enc_coef,
    latent_act,
    enc_w,
    enc_m,
    enc_v,
    dec_w,
    dec_m,
    dec_v,
    dead_order,
    pick_rows,
    send_count,
):
    rows, width = enc_w.shape
    half = width // 2
    size = lax.axis_size("latent")
    chips = size // 2
    stages = gather_table(jnp.concatenate([send_count, dead_order], axis=1), size)
    table = stages[-1]
    dec_sent, kept, dec_left = stream_far_product(latent_act, out_grad, size, rows)
    dec_sent = after(dec_sent, *stages[0])
    dec_kept, dec_core = [kept], [swap(dec_sent, 1, size)]
    enc_sent, kept, enc_left, code = far_product(
        after(enc_coef, dec_sent), x_rows, size, rows, pick_rows[0].T, table
    )
    enc_kept, enc_core = [kept], [swap(enc_sent, 1, size)]

    def both(slot):
        terms = [term(*pair, slot, rows) for pair in ((enc_kept, enc_core), (dec_kept, dec_core))]
        return jnp.concatenate(terms, axis=0)

    def travel(moving):
        return [shift(moving[0], 1, size), shift(moving[1], -1, size)]

    far = both(0).astype(jnp.bfloat16)
    moving = [far[:, :half], far[:, half:]]
    enc_sent, kept = near_product(after(enc_left, *moving), x_rows)
    came, enc_sent = tied(travel(moving), enc_sent)
    enc_kept.append(kept)
    enc_core.append(swap(enc_sent, 1, size))
    for hop in range(1, chips // 2):
        moving = []
        for side, value in enumerate(came):
            value = value.astype(jnp.float32)
            if value.shape[1] < width:
                pads = ((0, 0, 0), (0, half, 0) if side == 0 else (half, 0, 0))
                value = lax.pad(value, jnp.float32(0), pads)
            moving.append((value + both(2 * hop - side)).astype(jnp.bfloat16))
        came = travel(moving)
        if hop == 1:
            dec_sent, kept = near_product(after(dec_left, *moving), out_grad)
            dec_kept.append(kept)
            dec_core.append(swap(dec_sent, 1, size))
    states = (enc_w, enc_m, enc_v, dec_w, dec_m, dec_v)
    parts = ([enc_kept[1], enc_core[1]], [dec_kept[1], dec_core[1]], came)
    (blocks,) = update(code, states, *parts, True)
    results = update(code, after(states, blocks), *parts, False)
    enc_full, dec_full = gathered(blocks.reshape(2 * rows, width), results[0], size, rows)
    return (*results, enc_full, dec_full)


def solution(mesh):
    split = P(("groups", "latent"), None)
    placed = (split,) * 11 + (P(("groups", "latent"), None, None), split)
    return jax.shard_map(
        shards,
        mesh=mesh,
        in_specs=placed,
        out_specs=(split,) * 6 + (P("groups", None),) * 2,
        check_vma=False,
    )
```

```python
import functools

import jax
import jax.numpy as jnp
from jax import lax
from jax.experimental import pallas as pl
from jax.experimental.pallas import tpu as pltpu
from jax.sharding import PartitionSpec as P

beta_one = 0.9
beta_two = 0.99
first_fix = 1.0 - 0.9**4
second_fix = 1.0 - 0.99**4
learn_rate = 0.02
adam_eps = 1e-08
reset_gain = 0.01
norm_eps = 1e-06

KEPT = -1
ABSENT = -2


def adam_update(weight, moment, second, gradient):
    moment_new = beta_one * moment + (1.0 - beta_one) * gradient
    second_new = beta_two * second + (1.0 - beta_two) * gradient * gradient
    weight_new = weight - learn_rate * (moment_new / first_fix) / (
        jnp.sqrt(second_new / second_fix) + adam_eps
    )
    return (weight_new, moment_new, second_new)


def inverse_rms(value):
    return lax.rsqrt(jnp.mean(value * value, axis=1, keepdims=True) + norm_eps)


def swap(value, bits, size):
    return lax.ppermute(value, "latent", [(i, i ^ bits) for i in range(size)])


def after(value, *others):
    return lax.optimization_barrier((value,) + others)[0]


def tied(*values):
    return lax.optimization_barrier(values)


def params(mebibytes):
    return pltpu.CompilerParams(vmem_limit_bytes=mebibytes * 2**20)


def cost(flops, moved):
    return pl.CostEstimate(flops=int(flops), bytes_accessed=int(moved), transcendentals=0)


def chip_at(position, chips):
    return jnp.where(position < chips // 2, 2 * position, 2 * (chips - 1 - position) + 1)


def position_of(chip, chips):
    return jnp.where(chip % 2 == 0, chip // 2, chips - 1 - chip // 2)


def owner_at(offset, other_core, size):
    me = lax.axis_index("latent")
    chips = size // 2
    position = lax.rem(position_of(me // 2, chips) + offset + chips, chips)
    return 2 * chip_at(position, chips) + ((me % 2) ^ other_core)


def shift(value, step, size):
    chips = size // 2
    ring = [2 * q for q in range(chips // 2)] + [2 * q + 1 for q in reversed(range(chips // 2))]
    pairs = [
        (2 * ring[p] + core, 2 * ring[(p + step) % chips] + core)
        for p in range(chips)
        for core in range(2)
    ]
    return lax.ppermute(value, "latent", pairs)


def gather_table(row, size):
    pieces, step = [row], 1
    while step < size:
        if step > 1:
            pieces = [jnp.concatenate(pieces, axis=0)]
        pieces += [swap(pieces[0], step * k, size) for k in range(1, min(4, size // step))]
        step *= len(pieces)
    return pieces


def ordered_rows(size, rows, by_latent, groups):
    chips = size // 2
    for block in range(size):
        group, inside = block // chips, block % chips
        slot = group * (chips // 2) + inside % (chips // 2)
        far = chips // 2 - slot // 2
        offset = far if slot % 2 == 0 else 1 - far
        owner = owner_at(offset, 1 - inside // (chips // 2), size)
        begin = pl.multiple_of(owner * rows, rows)
        groups[group][inside * rows : (inside + 1) * rows] = by_latent[pl.ds(begin, rows)]


def row_codes(size, rows, table, picks_ref):
    me = lax.axis_index("latent")
    counts = table[:, :size]
    order = table[:, size:]
    source = me ^ lax.broadcasted_iota(jnp.int32, (size, 1), 0)
    before = jnp.sum(jnp.where(source < me, counts, 0), axis=0, keepdims=True)
    total = jnp.sum(counts, axis=0, keepdims=True)
    owners = lax.broadcasted_iota(jnp.int32, (size, size), 1) == source

    def by_key(row):
        return jnp.sum(jnp.where(owners, row, 0), axis=1, keepdims=True)

    begin, here = by_key(before), by_key(counts[:1])
    place = lax.broadcasted_iota(jnp.int32, (size, rows), 1)
    token = jnp.full((size, rows), ABSENT, jnp.int32)
    for c in range(picks_ref.shape[0]):
        own = (place == begin + c) & (here > c)
        token = jnp.where(own, by_key(picks_ref[c : c + 1]), token)
    token = jnp.where(place < by_key(total), token, KEPT)
    latent = lax.broadcasted_iota(jnp.int32, (size * rows, 1), 0)
    keys = lax.broadcasted_iota(jnp.int32, (size * rows, size), 1)
    spread = (keys == (me ^ (latent // rows))).astype(jnp.float32)

    def by_row(values):
        return jnp.dot(spread, values.astype(jnp.float32), precision=lax.Precision.HIGHEST)

    is_latent = by_row(order) == (latent % rows).astype(jnp.float32)
    code = jnp.sum(jnp.where(is_latent, by_row(token), 0.0), axis=1, keepdims=True)
    return (code + jnp.where(code < 0, -0.5, 0.5)).astype(jnp.int32)


def stream_kernel(size, rows, coef_hbm, right_hbm, *refs):
    outs, near_left, refs = refs[:2], refs[2], refs[3:]
    coef, right, by_latent, left, near_rows, total, stage, sems_left, sems_in, sems_out = refs
    tokens, width = right.shape
    part = outs[0].shape[0]
    cuts, pieces, passes = sems_in.shape[0], sems_out.shape[0], 2
    tile, height, depth = width // pieces, tokens // cuts, tokens // passes
    reads, writes = [], []
    for cut in range(cuts):
        span = pl.ds(cut * height, height)
        reads.append(pltpu.make_async_copy(right_hbm.at[span], right.at[span], sems_in.at[cut]))
    for i in range(pieces):
        columns = pl.ds(i * tile, tile)
        for group, out in enumerate(outs):
            source = stage.at[pl.ds(group * part, part), columns]
            writes.append(pltpu.make_async_copy(source, out.at[:, columns], sems_out.at[i, group]))
    read_coef = pltpu.make_async_copy(coef_hbm, coef, sems_left.at[0])
    write_near = pltpu.make_async_copy(near_rows, near_left, sems_left.at[1])
    read_coef.start()
    for read in reads:
        read.start()
    read_coef.wait()
    by_latent[...] = coef[...].T
    ordered_rows(size, rows, by_latent, (left, near_rows))
    write_near.start()
    for step in range(passes):
        for read in reads[step * cuts // passes : (step + 1) * cuts // passes]:
            read.wait()
        span = slice(step * depth, (step + 1) * depth)
        for i in range(pieces):
            columns = slice(i * tile, (i + 1) * tile)
            out = jnp.dot(left[:, span], right[span, columns], preferred_element_type=jnp.float32)
            if step > 0:
                out = out + total[:, columns]
            if step < passes - 1:
                total[:, columns] = out
            else:
                stage[:, columns] = out.astype(stage.dtype)
                for write in writes[2 * i : 2 * i + 2]:
                    write.start()
    for write in writes + [write_near]:
        write.wait()


def stream_far_product(coef, right, size, rows):
    tokens, latents = coef.shape
    width = right.shape[1]
    part, half = latents // 4, latents // 2
    pieces, cuts = 4, 8
    anywhere = pl.BlockSpec(memory_space=pl.ANY)
    return pl.pallas_call(
        functools.partial(stream_kernel, size, rows),
        in_specs=[anywhere] * 2,
        out_specs=[anywhere] * 3,
        out_shape=[jax.ShapeDtypeStruct((part, width), coef.dtype)] * 2
        + [jax.ShapeDtypeStruct((half, tokens), coef.dtype)],
        scratch_shapes=[
            pltpu.VMEM((tokens, latents), coef.dtype),
            pltpu.VMEM((tokens, width), coef.dtype),
            pltpu.VMEM((latents, tokens), coef.dtype),
            pltpu.VMEM((half, tokens), coef.dtype),
            pltpu.VMEM((half, tokens), coef.dtype),
            pltpu.VMEM((half, width), jnp.float32),
            pltpu.VMEM((half, width), coef.dtype),
            pltpu.SemaphoreType.DMA((2,)),
            pltpu.SemaphoreType.DMA((cuts,)),
            pltpu.SemaphoreType.DMA((pieces, 2)),
        ],
        compiler_params=params(52),
        cost_estimate=cost(
            latents * tokens * width, 2 * (tokens * width + latents * tokens) + latents * width
        ),
        name="stream_far_product",
    )(coef, right)


def multiply(left_ref, right_ref, outs):
    out = jnp.dot(left_ref[...], right_ref[...], preferred_element_type=jnp.float32)
    part = outs[0].shape[0]
    for i, ref in enumerate(outs):
        ref[...] = out[i * part : (i + 1) * part].astype(ref.dtype)


def select_far_kernel(size, rows, count, coef_ref, right_ref, picks_ref, *refs):
    pieces, refs = refs[:count], refs[count:]
    outs, near_left, own_code, (by_latent, left, table, codes) = refs[:2], refs[2], refs[3], refs[4:]

    @pl.when(pl.program_id(0) == 0)
    def _():
        height = size // count
        for i, piece in enumerate(pieces):
            table[i * height : (i + 1) * height] = piece[...]
        code = row_codes(size, rows, table[...], picks_ref)
        codes[...] = code
        own_code[...] = codes[pl.ds(pl.multiple_of(lax.axis_index("latent") * rows, rows), rows)]
        tokens = lax.broadcasted_iota(jnp.int32, by_latent.shape, 1)
        by_latent[...] = jnp.where(
            code == KEPT, coef_ref[...].T, (tokens == code).astype(by_latent.dtype)
        )
        ordered_rows(size, rows, by_latent, (left, near_left))

    multiply(left, right_ref, outs)


def near_kernel(left_ref, right_ref, *outs):
    multiply(left_ref, right_ref, outs)


def product(kernel, left, right, others, out_more, scratch, name):
    tokens, width = right.shape
    tile = 512
    part = left.size // tokens // (4 if out_more else 2)
    fixed = lambda j: (0, 0)
    in_specs = [pl.BlockSpec(left.shape, fixed), pl.BlockSpec((tokens, tile), lambda j: (0, j))]
    return pl.pallas_call(
        kernel,
        grid=(width // tile,),
        in_specs=in_specs + [pl.BlockSpec(value.shape, fixed) for value in others],
        out_specs=[pl.BlockSpec((part, tile), lambda j: (0, j))] * 2
        + [pl.BlockSpec(value.shape, fixed) for value in out_more],
        out_shape=[jax.ShapeDtypeStruct((part, width), left.dtype)] * 2 + list(out_more),
        scratch_shapes=scratch,
        compiler_params=params(20),
        cost_estimate=cost(
            12 * part * tokens * width, 2 * (tokens * width + 2 * part * (tokens + width))
        ),
        name=name,
    )(left, right, *others)


def far_product(coef, right, size, rows, picks, table):
    tokens, latents = coef.shape
    near_left = jax.ShapeDtypeStruct((latents // 2, tokens), coef.dtype)
    code = jax.ShapeDtypeStruct((rows, 1), jnp.int32)
    scratch = [
        pltpu.VMEM((latents, tokens), coef.dtype),
        pltpu.VMEM((latents // 2, tokens), coef.dtype),
        pltpu.VMEM((size, table[0].shape[1]), jnp.int32),
        pltpu.VMEM((latents, 1), jnp.int32),
    ]
    kernel = functools.partial(select_far_kernel, size, rows, len(table))
    others = [picks] + list(table)
    return product(kernel, coef, right, others, [near_left, code], scratch, "far_product")


def near_product(left, right):
    return product(near_kernel, left, right, [], [], [], "near_product")


def term(kept, from_core, slot, rows):
    slots = kept[0].shape[0] // rows
    group, begin = slot // slots, slot % slots * rows
    pair = (kept[group], from_core[group])
    return sum(value[begin : begin + rows].astype(jnp.float32) for value in pair)


def updated(refs):
    code, states, terms = refs[0], refs[1:7], refs[7:15]
    reset = code[...] != KEPT
    enc_grad, dec_grad = (
        sum(ref[...].astype(jnp.float32) for ref in half) for half in (terms[:4], terms[4:])
    )
    enc = adam_update(*(ref[...] for ref in states[:3]), enc_grad)
    dec = adam_update(*(ref[...] for ref in states[3:]), dec_grad)
    enc_w = jnp.where(reset, reset_gain * enc_grad * inverse_rms(enc_grad), enc[0])
    dec_w = jnp.where(reset, enc_grad, dec[0])
    dec_w = dec_w * inverse_rms(dec_w)
    moments = [jnp.where(reset, 0.0, value) for value in enc[1:] + dec[1:]]
    return [enc_w] + moments[:2] + [dec_w] + moments[2:]


def blocks_kernel(*refs):
    results, blocks = updated(refs), refs[-1]
    blocks[0] = results[0].astype(blocks.dtype)
    blocks[1] = results[3].astype(blocks.dtype)


def states_kernel(*refs):
    for ref, value in zip(refs[-6:], updated(refs)):
        ref[...] = value


def update(code, states, enc_parts, dec_parts, came, blocks_only):
    rows, width = states[0].shape
    tile = 16

    def row_tile(value, skipped):
        return pl.BlockSpec((tile, value.shape[1]), lambda i: (i + skipped // tile, 0))

    operands = [(value, 0) for value in [code] + list(states)]
    for parts, first in ((enc_parts, 0), (dec_parts, rows)):
        operands += [(value, value.shape[0] - rows) for value in parts]
        operands += [(value, first) for value in came]
    if blocks_only:
        out_shape = [jax.ShapeDtypeStruct((2, rows, width), jnp.bfloat16)]
        out_specs = [pl.BlockSpec((2, tile, width), lambda i: (0, i, 0))]
    else:
        out_shape = [jax.ShapeDtypeStruct((rows, width), jnp.float32)] * 6
        out_specs = [pl.BlockSpec((tile, width), lambda i: (i, 0))] * 6
    return pl.pallas_call(
        blocks_kernel if blocks_only else states_kernel,
        grid=(rows // tile,),
        in_specs=[row_tile(*operand) for operand in operands],
        out_specs=out_specs,
        out_shape=out_shape,
        cost_estimate=cost(10 * rows * width, 10 * rows * width),
        compiler_params=params(20),
        name="blocks" if blocks_only else "states",
    )(*(value for value, _ in operands))


def place_kernel(plan, size, rows, count, *refs):
    pieces, outs, sems = refs[:count], refs[-3:-1], refs[-1]
    copies = []
    for i, (offset, other_core, column) in enumerate(plan):
        start = pl.multiple_of(owner_at(offset, other_core, size) * rows, rows)
        for whole, out in enumerate(outs):
            source = pieces[i].at[pl.ds(whole * rows, rows)]
            target = out.at[pl.ds(start, rows), pl.ds(column, pieces[i].shape[1])]
            copies.append(pltpu.make_async_copy(source, target, sems.at[i, whole]))
    for copy in copies:
        copy.start()
    for copy in copies:
        copy.wait()


def place(pieces, wholes, size, rows, width):
    operands = [value for _, _, _, value in pieces]
    plan = [piece[:3] for piece in pieces]
    count = len(operands)
    first = wholes is None
    if not first:
        operands += list(wholes)
    anywhere = pl.BlockSpec(memory_space=pl.ANY)
    return pl.pallas_call(
        functools.partial(place_kernel, plan, size, rows, count),
        out_shape=[jax.ShapeDtypeStruct((size * rows, width), operands[0].dtype)] * 2,
        in_specs=[anywhere] * len(operands),
        out_specs=[anywhere] * 2,
        scratch_shapes=[pltpu.SemaphoreType.DMA((count, 2))],
        input_output_aliases={} if first else {count: 0, count + 1: 1},
        compiler_params=params(4),
        cost_estimate=cost(0, 8 * count * rows * width),
        name="place",
    )(*operands)


def gathered(block, order, size, rows):
    chips = size // 2
    width = block.shape[1]
    half = width // 2
    hops = chips // 2
    right = left = block
    near, far, wholes = [(0, 0, 0, after(block, order))], [], None
    for hop in range(1, hops + 1):
        if hop == hops:
            right, left = right[:, :half], left[:, half:]
        right, left = shift(right, 1, size), shift(left, -1, size)
        sent = [(offset, 1, column, swap(value, 1, size)) for offset, _, column, value in near]
        wholes = place(near + far, wholes, size, rows, width)
        far = sent
        right, wholes = tied(right, wholes)
        left = after(left, right)
        near = [(-hop, 0, 0, right), (hop, 0, half if hop == hops else 0, left)]
    sent = [(offset, 1, column, swap(value, 1, size)) for offset, _, column, value in near]
    wholes = place(near, wholes, size, rows, width)
    return place(far + sent, wholes, size, rows, width)


def shards(
    x_rows,
    out_grad,
    enc_coef,
    latent_act,
    enc_w,
    enc_m,
    enc_v,
    dec_w,
    dec_m,
    dec_v,
    dead_order,
    pick_rows,
    send_count,
):
    rows, width = enc_w.shape
    half = width // 2
    size = lax.axis_size("latent")
    chips = size // 2
    table = gather_table(jnp.concatenate([send_count, dead_order], axis=1), size)
    dec_sent, kept, dec_left = stream_far_product(
        after(latent_act, table[0]), out_grad, size, rows
    )
    dec_sent = after(dec_sent, *table)
    dec_kept, dec_core = [kept], [swap(dec_sent, 1, size)]
    enc_sent, kept, enc_left, code = far_product(
        after(enc_coef, dec_sent), x_rows, size, rows, pick_rows[0].T, table
    )
    enc_kept, enc_core = [kept], [swap(enc_sent, 1, size)]

    def both(slot):
        terms = [term(*pair, slot, rows) for pair in ((enc_kept, enc_core), (dec_kept, dec_core))]
        return jnp.concatenate(terms, axis=0)

    def travel(moving):
        return [shift(moving[0], 1, size), shift(moving[1], -1, size)]

    far = both(0).astype(jnp.bfloat16)
    moving = [far[:, :half], far[:, half:]]
    enc_sent, kept = near_product(after(enc_left, *moving), x_rows)
    came, enc_sent = tied(travel(moving), enc_sent)
    enc_kept.append(kept)
    enc_core.append(swap(enc_sent, 1, size))
    for hop in range(1, chips // 2):
        moving = []
        for side, value in enumerate(came):
            value = value.astype(jnp.float32)
            if value.shape[1] < width:
                pads = ((0, 0, 0), (0, half, 0) if side == 0 else (half, 0, 0))
                value = lax.pad(value, jnp.float32(0), pads)
            moving.append((value + both(2 * hop - side)).astype(jnp.bfloat16))
        came = travel(moving)
        if hop == 1:
            dec_sent, kept = near_product(after(dec_left, *moving), out_grad)
            dec_kept.append(kept)
            dec_core.append(swap(dec_sent, 1, size))
    states = (enc_w, enc_m, enc_v, dec_w, dec_m, dec_v)
    parts = ([enc_kept[1], enc_core[1]], [dec_kept[1], dec_core[1]], came)
    (blocks,) = update(code, states, *parts, True)
    results = update(code, after(states, blocks), *parts, False)
    enc_full, dec_full = gathered(blocks.reshape(2 * rows, width), results[0], size, rows)
    return (*results, enc_full, dec_full)


def solution(mesh):
    split = P(("groups", "latent"), None)
    placed = (split,) * 11 + (P(("groups", "latent"), None, None), split)
    return jax.shard_map(
        shards,
        mesh=mesh,
        in_specs=placed,
        out_specs=(split,) * 6 + (P("groups", None),) * 2,
        check_vma=False,
    )
```

```python
import functools

import jax
import jax.numpy as jnp
from jax import lax
from jax.experimental import pallas as pl
from jax.experimental.pallas import tpu as pltpu
from jax.sharding import PartitionSpec as P

beta_one = 0.9
beta_two = 0.99
first_fix = 1.0 - 0.9**4
second_fix = 1.0 - 0.99**4
learn_rate = 0.02
adam_eps = 1e-08
reset_gain = 0.01
norm_eps = 1e-06

KEPT = -1
ABSENT = -2


def adam_update(weight, moment, second, gradient):
    moment_new = beta_one * moment + (1.0 - beta_one) * gradient
    second_new = beta_two * second + (1.0 - beta_two) * gradient * gradient
    weight_new = weight - learn_rate * (moment_new / first_fix) / (
        jnp.sqrt(second_new / second_fix) + adam_eps
    )
    return (weight_new, moment_new, second_new)


def inverse_rms(value):
    return lax.rsqrt(jnp.mean(value * value, axis=1, keepdims=True) + norm_eps)


def swap(value, bits, size):
    return lax.ppermute(value, "latent", [(i, i ^ bits) for i in range(size)])


def after(value, *others):
    return lax.optimization_barrier((value,) + others)[0]


def tied(*values):
    return lax.optimization_barrier(values)


def params(mebibytes):
    return pltpu.CompilerParams(vmem_limit_bytes=mebibytes * 2**20)


def cost(flops, moved):
    return pl.CostEstimate(flops=int(flops), bytes_accessed=int(moved), transcendentals=0)


def chip_at(position, chips):
    return jnp.where(position < chips // 2, 2 * position, 2 * (chips - 1 - position) + 1)


def position_of(chip, chips):
    return jnp.where(chip % 2 == 0, chip // 2, chips - 1 - chip // 2)


def owner_at(offset, other_core, size):
    me = lax.axis_index("latent")
    chips = size // 2
    position = lax.rem(position_of(me // 2, chips) + offset + chips, chips)
    return 2 * chip_at(position, chips) + ((me % 2) ^ other_core)


def shift(value, step, size):
    chips = size // 2
    ring = [2 * q for q in range(chips // 2)] + [2 * q + 1 for q in reversed(range(chips // 2))]
    pairs = [
        (2 * ring[p] + core, 2 * ring[(p + step) % chips] + core)
        for p in range(chips)
        for core in range(2)
    ]
    return lax.ppermute(value, "latent", pairs)


def gather_table(row, size):
    stages, step = [], 1
    pieces = [row]
    while step < size:
        if step > 1:
            pieces = [jnp.concatenate(pieces, axis=0)]
        pieces += [swap(pieces[0], step * k, size) for k in range(1, min(4, size // step))]
        stages.append(pieces)
        step *= len(pieces)
    return stages


def ordered_rows(size, rows, by_latent, groups):
    chips = size // 2
    for block in range(size):
        group, inside = block // chips, block % chips
        slot = group * (chips // 2) + inside % (chips // 2)
        far = chips // 2 - slot // 2
        offset = far if slot % 2 == 0 else 1 - far
        owner = owner_at(offset, 1 - inside // (chips // 2), size)
        begin = pl.multiple_of(owner * rows, rows)
        groups[group][inside * rows : (inside + 1) * rows] = by_latent[pl.ds(begin, rows)]


def row_codes(size, rows, table, picks_ref):
    me = lax.axis_index("latent")
    counts = table[:, :size]
    order = table[:, size:]
    source = me ^ lax.broadcasted_iota(jnp.int32, (size, 1), 0)
    before = jnp.sum(jnp.where(source < me, counts, 0), axis=0, keepdims=True)
    total = jnp.sum(counts, axis=0, keepdims=True)
    owners = lax.broadcasted_iota(jnp.int32, (size, size), 1) == source

    def by_key(row):
        return jnp.sum(jnp.where(owners, row, 0), axis=1, keepdims=True)

    begin, here = by_key(before), by_key(counts[:1])
    place = lax.broadcasted_iota(jnp.int32, (size, rows), 1)
    token = jnp.full((size, rows), ABSENT, jnp.int32)
    for c in range(picks_ref.shape[0]):
        own = (place == begin + c) & (here > c)
        token = jnp.where(own, by_key(picks_ref[c : c + 1]), token)
    token = jnp.where(place < by_key(total), token, KEPT)
    latent = lax.broadcasted_iota(jnp.int32, (size * rows, 1), 0)
    keys = lax.broadcasted_iota(jnp.int32, (size * rows, size), 1)
    spread = (keys == (me ^ (latent // rows))).astype(jnp.float32)

    def by_row(values):
        return jnp.dot(spread, values.astype(jnp.float32), precision=lax.Precision.HIGHEST)

    is_latent = by_row(order) == (latent % rows).astype(jnp.float32)
    code = jnp.sum(jnp.where(is_latent, by_row(token), 0.0), axis=1, keepdims=True)
    return (code + jnp.where(code < 0, -0.5, 0.5)).astype(jnp.int32)


def stream_kernel(size, rows, coef_hbm, right_hbm, *refs):
    outs, near_left, refs = refs[:2], refs[2], refs[3:]
    coef, right, by_latent, left, near_rows, total, stage, sems_left, sems_in, sems_out = refs
    tokens, width = right.shape
    part = outs[0].shape[0]
    cuts, pieces, passes = sems_in.shape[0], sems_out.shape[0], 2
    tile, height, depth = width // pieces, tokens // cuts, tokens // passes
    reads, writes = [], []
    for cut in range(cuts):
        span = pl.ds(cut * height, height)
        reads.append(pltpu.make_async_copy(right_hbm.at[span], right.at[span], sems_in.at[cut]))
    for i in range(pieces):
        columns = pl.ds(i * tile, tile)
        for group, out in enumerate(outs):
            source = stage.at[pl.ds(group * part, part), columns]
            writes.append(pltpu.make_async_copy(source, out.at[:, columns], sems_out.at[i, group]))
    read_coef = pltpu.make_async_copy(coef_hbm, coef, sems_left.at[0])
    write_near = pltpu.make_async_copy(near_rows, near_left, sems_left.at[1])
    read_coef.start()
    for read in reads:
        read.start()
    read_coef.wait()
    by_latent[...] = coef[...].T
    ordered_rows(size, rows, by_latent, (left, near_rows))
    write_near.start()
    for step in range(passes):
        for read in reads[step * cuts // passes : (step + 1) * cuts // passes]:
            read.wait()
        span = slice(step * depth, (step + 1) * depth)
        for i in range(pieces):
            columns = slice(i * tile, (i + 1) * tile)
            out = jnp.dot(left[:, span], right[span, columns], preferred_element_type=jnp.float32)
            if step > 0:
                out = out + total[:, columns]
            if step < passes - 1:
                total[:, columns] = out
            else:
                stage[:, columns] = out.astype(stage.dtype)
                for write in writes[2 * i : 2 * i + 2]:
                    write.start()
    for write in writes + [write_near]:
        write.wait()


def stream_far_product(coef, right, size, rows):
    tokens, latents = coef.shape
    width = right.shape[1]
    part, half = latents // 4, latents // 2
    pieces, cuts = 4, 8
    anywhere = pl.BlockSpec(memory_space=pl.ANY)
    return pl.pallas_call(
        functools.partial(stream_kernel, size, rows),
        in_specs=[anywhere] * 2,
        out_specs=[anywhere] * 3,
        out_shape=[jax.ShapeDtypeStruct((part, width), coef.dtype)] * 2
        + [jax.ShapeDtypeStruct((half, tokens), coef.dtype)],
        scratch_shapes=[
            pltpu.VMEM((tokens, latents), coef.dtype),
            pltpu.VMEM((tokens, width), coef.dtype),
            pltpu.VMEM((latents, tokens), coef.dtype),
            pltpu.VMEM((half, tokens), coef.dtype),
            pltpu.VMEM((half, tokens), coef.dtype),
            pltpu.VMEM((half, width), jnp.float32),
            pltpu.VMEM((half, width), coef.dtype),
            pltpu.SemaphoreType.DMA((2,)),
            pltpu.SemaphoreType.DMA((cuts,)),
            pltpu.SemaphoreType.DMA((pieces, 2)),
        ],
        compiler_params=params(52),
        cost_estimate=cost(
            latents * tokens * width, 2 * (tokens * width + latents * tokens) + latents * width
        ),
        name="stream_far_product",
    )(coef, right)


def multiply(left_ref, right_ref, outs):
    out = jnp.dot(left_ref[...], right_ref[...], preferred_element_type=jnp.float32)
    part = outs[0].shape[0]
    for i, ref in enumerate(outs):
        ref[...] = out[i * part : (i + 1) * part].astype(ref.dtype)


def select_far_kernel(size, rows, count, coef_ref, right_ref, picks_ref, *refs):
    pieces, refs = refs[:count], refs[count:]
    outs, near_left, own_code, (by_latent, left, table, codes) = refs[:2], refs[2], refs[3], refs[4:]

    @pl.when(pl.program_id(0) == 0)
    def _():
        height = size // count
        for i, piece in enumerate(pieces):
            table[i * height : (i + 1) * height] = piece[...]
        code = row_codes(size, rows, table[...], picks_ref)
        codes[...] = code
        own_code[...] = codes[pl.ds(pl.multiple_of(lax.axis_index("latent") * rows, rows), rows)]
        tokens = lax.broadcasted_iota(jnp.int32, by_latent.shape, 1)
        by_latent[...] = jnp.where(
            code == KEPT, coef_ref[...].T, (tokens == code).astype(by_latent.dtype)
        )
        ordered_rows(size, rows, by_latent, (left, near_left))

    multiply(left, right_ref, outs)


def near_kernel(left_ref, right_ref, *outs):
    multiply(left_ref, right_ref, outs)


def product(kernel, left, right, others, out_more, scratch, name):
    tokens, width = right.shape
    tile = 512
    part = left.size // tokens // (4 if out_more else 2)
    fixed = lambda j: (0, 0)
    in_specs = [pl.BlockSpec(left.shape, fixed), pl.BlockSpec((tokens, tile), lambda j: (0, j))]
    return pl.pallas_call(
        kernel,
        grid=(width // tile,),
        in_specs=in_specs + [pl.BlockSpec(value.shape, fixed) for value in others],
        out_specs=[pl.BlockSpec((part, tile), lambda j: (0, j))] * 2
        + [pl.BlockSpec(value.shape, fixed) for value in out_more],
        out_shape=[jax.ShapeDtypeStruct((part, width), left.dtype)] * 2 + list(out_more),
        scratch_shapes=scratch,
        compiler_params=params(20),
        cost_estimate=cost(
            12 * part * tokens * width, 2 * (tokens * width + 2 * part * (tokens + width))
        ),
        name=name,
    )(left, right, *others)


def far_product(coef, right, size, rows, picks, table):
    tokens, latents = coef.shape
    near_left = jax.ShapeDtypeStruct((latents // 2, tokens), coef.dtype)
    code = jax.ShapeDtypeStruct((rows, 1), jnp.int32)
    scratch = [
        pltpu.VMEM((latents, tokens), coef.dtype),
        pltpu.VMEM((latents // 2, tokens), coef.dtype),
        pltpu.VMEM((size, table[0].shape[1]), jnp.int32),
        pltpu.VMEM((latents, 1), jnp.int32),
    ]
    kernel = functools.partial(select_far_kernel, size, rows, len(table))
    others = [picks] + list(table)
    return product(kernel, coef, right, others, [near_left, code], scratch, "far_product")


def near_product(left, right):
    return product(near_kernel, left, right, [], [], [], "near_product")


def term(kept, from_core, slot, rows):
    slots = kept[0].shape[0] // rows
    group, begin = slot // slots, slot % slots * rows
    pair = (kept[group], from_core[group])
    return sum(value[begin : begin + rows].astype(jnp.float32) for value in pair)


def updated(refs):
    code, states, terms = refs[0], refs[1:7], refs[7:15]
    reset = code[...] != KEPT
    enc_grad, dec_grad = (
        sum(ref[...].astype(jnp.float32) for ref in half) for half in (terms[:4], terms[4:])
    )
    enc = adam_update(*(ref[...] for ref in states[:3]), enc_grad)
    dec = adam_update(*(ref[...] for ref in states[3:]), dec_grad)
    enc_w = jnp.where(reset, reset_gain * enc_grad * inverse_rms(enc_grad), enc[0])
    dec_w = jnp.where(reset, enc_grad, dec[0])
    dec_w = dec_w * inverse_rms(dec_w)
    moments = [jnp.where(reset, 0.0, value) for value in enc[1:] + dec[1:]]
    return [enc_w] + moments[:2] + [dec_w] + moments[2:]


def blocks_kernel(*refs):
    results, blocks = updated(refs), refs[-1]
    blocks[0] = results[0].astype(blocks.dtype)
    blocks[1] = results[3].astype(blocks.dtype)


def states_kernel(*refs):
    for ref, value in zip(refs[-6:], updated(refs)):
        ref[...] = value


def update(code, states, enc_parts, dec_parts, blocks_only):
    rows, width = states[0].shape
    tile = 16

    def row_tile(value, skipped):
        return pl.BlockSpec((tile, value.shape[1]), lambda i: (i + skipped // tile, 0))

    operands = [(value, 0) for value in [code] + list(states)]
    operands += [(value, value.shape[0] - rows) for value in enc_parts + dec_parts]
    if blocks_only:
        out_shape = [jax.ShapeDtypeStruct((2, rows, width), jnp.bfloat16)]
        out_specs = [pl.BlockSpec((2, tile, width), lambda i: (0, i, 0))]
    else:
        out_shape = [jax.ShapeDtypeStruct((rows, width), jnp.float32)] * 6
        out_specs = [pl.BlockSpec((tile, width), lambda i: (i, 0))] * 6
    return pl.pallas_call(
        blocks_kernel if blocks_only else states_kernel,
        grid=(rows // tile,),
        in_specs=[row_tile(*operand) for operand in operands],
        out_specs=out_specs,
        out_shape=out_shape,
        cost_estimate=cost(10 * rows * width, 10 * rows * width),
        compiler_params=params(20),
        name="blocks" if blocks_only else "states",
    )(*(value for value, _ in operands))


def place_kernel(plan, size, rows, count, *refs):
    pieces, outs, sems = refs[:count], refs[-3:-1], refs[-1]
    copies = []
    for i, (offset, other_core, column) in enumerate(plan):
        start = pl.multiple_of(owner_at(offset, other_core, size) * rows, rows)
        for whole, out in enumerate(outs):
            source = pieces[i].at[pl.ds(whole * rows, rows)]
            target = out.at[pl.ds(start, rows), pl.ds(column, pieces[i].shape[1])]
            copies.append(pltpu.make_async_copy(source, target, sems.at[i, whole]))
    for copy in copies:
        copy.start()
    for copy in copies:
        copy.wait()


def place(pieces, wholes, size, rows, width):
    operands = [value for _, _, _, value in pieces]
    plan = [piece[:3] for piece in pieces]
    count = len(operands)
    first = wholes is None
    if not first:
        operands += list(wholes)
    anywhere = pl.BlockSpec(memory_space=pl.ANY)
    return pl.pallas_call(
        functools.partial(place_kernel, plan, size, rows, count),
        out_shape=[jax.ShapeDtypeStruct((size * rows, width), operands[0].dtype)] * 2,
        in_specs=[anywhere] * len(operands),
        out_specs=[anywhere] * 2,
        scratch_shapes=[pltpu.SemaphoreType.DMA((count, 2))],
        input_output_aliases={} if first else {count: 0, count + 1: 1},
        compiler_params=params(4),
        cost_estimate=cost(0, 8 * count * rows * width),
        name="place",
    )(*operands)


def gathered(block, order, size, rows):
    chips = size // 2
    width = block.shape[1]
    half = width // 2
    hops = chips // 2
    right = left = block
    near, far, wholes = [(0, 0, 0, after(block, order))], [], None
    for hop in range(1, hops + 1):
        if hop == hops:
            right, left = right[:, :half], left[:, half:]
        right, left = shift(right, 1, size), shift(left, -1, size)
        sent = [(offset, 1, column, swap(value, 1, size)) for offset, _, column, value in near]
        wholes = place(near + far, wholes, size, rows, width)
        far = sent
        right, wholes = tied(right, wholes)
        left = after(left, right)
        near = [(-hop, 0, 0, right), (hop, 0, half if hop == hops else 0, left)]
    sent = [(offset, 1, column, swap(value, 1, size)) for offset, _, column, value in near]
    wholes = place(near, wholes, size, rows, width)
    return place(far + sent, wholes, size, rows, width)


def shards(
    x_rows,
    out_grad,
    enc_coef,
    latent_act,
    enc_w,
    enc_m,
    enc_v,
    dec_w,
    dec_m,
    dec_v,
    dead_order,
    pick_rows,
    send_count,
):
    rows, width = enc_w.shape
    half = width // 2
    size = lax.axis_size("latent")
    chips = size // 2
    stages = gather_table(jnp.concatenate([send_count, dead_order], axis=1), size)
    table = stages[-1]
    dec_sent, kept, dec_left = stream_far_product(latent_act, out_grad, size, rows)
    dec_sent = after(dec_sent, *stages[0])
    dec_kept, dec_core = [kept], [swap(dec_sent, 1, size)]
    enc_sent, kept, enc_left, code = far_product(
        after(enc_coef, dec_sent), x_rows, size, rows, pick_rows[0].T, table
    )
    enc_kept, enc_core = [kept], [swap(enc_sent, 1, size)]

    def begin(kept, from_core):
        far = term(kept, from_core, 0, rows).astype(jnp.bfloat16)
        return [far[:, :half], far[:, half:]]

    def travel(moving):
        return [shift(moving[0], 1, size), shift(moving[1], -1, size)]

    def advance(came, kept, from_core, hop, order):
        moving = []
        for side, value in enumerate(after(came, order)):
            value = value.astype(jnp.float32)
            if value.shape[1] < width:
                pads = ((0, 0, 0), (0, half, 0) if side == 0 else (half, 0, 0))
                value = lax.pad(value, jnp.float32(0), pads)
            value = value + term(kept, from_core, 2 * hop - side, rows)
            moving.append(value.astype(jnp.bfloat16))
        return travel(moving), moving

    dec_moving = begin(dec_kept, dec_core)
    dec_came = travel(dec_moving)
    enc_moving = begin(enc_kept, after(enc_core, *dec_moving))
    enc_sent, kept = near_product(after(enc_left, *enc_moving), x_rows)
    enc_came, enc_sent = tied(travel(enc_moving), enc_sent)
    enc_kept.append(kept)
    enc_core.append(swap(enc_sent, 1, size))
    dec_came, order = advance(dec_came, dec_kept, dec_core, 1, enc_sent)
    enc_came, order = advance(enc_came, enc_kept, enc_core, 1, order)
    dec_sent, kept = near_product(after(dec_left, *order), out_grad)
    dec_kept.append(kept)
    dec_core.append(swap(dec_sent, 1, size))
    order = dec_sent
    for hop in range(2, chips // 2):
        dec_came, order = advance(dec_came, dec_kept, dec_core, hop, order)
        if hop == chips // 2 - 1:
            order = (order, dec_came)
        enc_came, order = advance(enc_came, enc_kept, enc_core, hop, order)
    states = (enc_w, enc_m, enc_v, dec_w, dec_m, dec_v)
    parts = ([enc_kept[1], enc_core[1]] + enc_came, [dec_kept[1], dec_core[1]] + dec_came)
    (blocks,) = update(code, states, *parts, True)
    results = update(code, after(states, blocks), *parts, False)
    enc_full, dec_full = gathered(blocks.reshape(2 * rows, width), results[0], size, rows)
    return (*results, enc_full, dec_full)


def solution(mesh):
    split = P(("groups", "latent"), None)
    placed = (split,) * 11 + (P(("groups", "latent"), None, None), split)
    return jax.shard_map(
        shards,
        mesh=mesh,
        in_specs=placed,
        out_specs=(split,) * 6 + (P("groups", None),) * 2,
        check_vma=False,
    )
```

```python
import functools

import jax
import jax.numpy as jnp
from jax import lax
from jax.experimental import pallas as pl
from jax.experimental.pallas import tpu as pltpu
from jax.sharding import PartitionSpec as P

beta_one = 0.9
beta_two = 0.99
first_fix = 1.0 - 0.9**4
second_fix = 1.0 - 0.99**4
learn_rate = 0.02
adam_eps = 1e-08
reset_gain = 0.01
norm_eps = 1e-06

KEPT = -1
ABSENT = -2


def adam_update(weight, moment, second, gradient):
    moment_new = beta_one * moment + (1.0 - beta_one) * gradient
    second_new = beta_two * second + (1.0 - beta_two) * gradient * gradient
    weight_new = weight - learn_rate * (moment_new / first_fix) / (
        jnp.sqrt(second_new / second_fix) + adam_eps
    )
    return (weight_new, moment_new, second_new)


def inverse_rms(value):
    return lax.rsqrt(jnp.mean(value * value, axis=1, keepdims=True) + norm_eps)


def swap(value, bits, size):
    return lax.ppermute(value, "latent", [(i, i ^ bits) for i in range(size)])


def after(value, *others):
    return lax.optimization_barrier((value,) + others)[0]


def tied(*values):
    return lax.optimization_barrier(values)


def params(mebibytes):
    return pltpu.CompilerParams(vmem_limit_bytes=mebibytes * 2**20)


def cost(flops, moved):
    return pl.CostEstimate(flops=int(flops), bytes_accessed=int(moved), transcendentals=0)


def chip_at(position, chips):
    return jnp.where(position < chips // 2, 2 * position, 2 * (chips - 1 - position) + 1)


def position_of(chip, chips):
    return jnp.where(chip % 2 == 0, chip // 2, chips - 1 - chip // 2)


def owner_at(offset, other_core, size):
    me = lax.axis_index("latent")
    chips = size // 2
    position = lax.rem(position_of(me // 2, chips) + offset + chips, chips)
    return 2 * chip_at(position, chips) + ((me % 2) ^ other_core)


def shift(value, step, size):
    chips = size // 2
    ring = [2 * q for q in range(chips // 2)] + [2 * q + 1 for q in reversed(range(chips // 2))]
    pairs = [
        (2 * ring[p] + core, 2 * ring[(p + step) % chips] + core)
        for p in range(chips)
        for core in range(2)
    ]
    return lax.ppermute(value, "latent", pairs)


def gather_table(row, size):
    stages, step = [], 4
    pieces = [row]
    while step < size:
        pieces = [row if len(pieces) == 1 else jnp.concatenate(pieces, axis=0)]
        pieces += [swap(pieces[0], step * k, size) for k in range(1, min(4, size // step))]
        stages.append(pieces)
        step *= len(pieces)
    table = jnp.concatenate(pieces, axis=0)
    stages.append([table] + [swap(table, k, size) for k in range(1, 4)])
    return stages


def table_key(row, size):
    height = size // 4
    return 4 * (row % height) + row // height


def ordered_rows(size, rows, by_latent, groups):
    chips = size // 2
    for block in range(size):
        group, inside = block // chips, block % chips
        slot = group * (chips // 2) + inside % (chips // 2)
        far = chips // 2 - slot // 2
        offset = far if slot % 2 == 0 else 1 - far
        owner = owner_at(offset, 1 - inside // (chips // 2), size)
        begin = pl.multiple_of(owner * rows, rows)
        groups[group][inside * rows : (inside + 1) * rows] = by_latent[pl.ds(begin, rows)]


def row_codes(size, rows, table, picks_ref):
    me = lax.axis_index("latent")
    counts = table[:, :size]
    order = table[:, size:]
    source = me ^ table_key(lax.broadcasted_iota(jnp.int32, (size, 1), 0), size)
    before = jnp.sum(jnp.where(source < me, counts, 0), axis=0, keepdims=True)
    total = jnp.sum(counts, axis=0, keepdims=True)
    owners = lax.broadcasted_iota(jnp.int32, (size, size), 1) == source

    def by_key(row):
        return jnp.sum(jnp.where(owners, row, 0), axis=1, keepdims=True)

    begin, here = by_key(before), by_key(counts[:1])
    place = lax.broadcasted_iota(jnp.int32, (size, rows), 1)
    token = jnp.full((size, rows), ABSENT, jnp.int32)
    for c in range(picks_ref.shape[0]):
        own = (place == begin + c) & (here > c)
        token = jnp.where(own, by_key(picks_ref[c : c + 1]), token)
    token = jnp.where(place < by_key(total), token, KEPT)
    latent = lax.broadcasted_iota(jnp.int32, (size * rows, 1), 0)
    keys = table_key(lax.broadcasted_iota(jnp.int32, (size * rows, size), 1), size)
    spread = (keys == (me ^ (latent // rows))).astype(jnp.float32)

    def by_row(values):
        return jnp.dot(spread, values.astype(jnp.float32), precision=lax.Precision.HIGHEST)

    is_latent = by_row(order) == (latent % rows).astype(jnp.float32)
    code = jnp.sum(jnp.where(is_latent, by_row(token), 0.0), axis=1, keepdims=True)
    return (code + jnp.where(code < 0, -0.5, 0.5)).astype(jnp.int32)


def stream_kernel(size, rows, coef_hbm, right_hbm, *refs):
    outs, near_left, refs = refs[:2], refs[2], refs[3:]
    coef, right, by_latent, left, near_rows, total, stage, sems_left, sems_in, sems_out = refs
    tokens, width = right.shape
    part = outs[0].shape[0]
    cuts, pieces, passes = sems_in.shape[0], sems_out.shape[0], 2
    tile, height, depth = width // pieces, tokens // cuts, tokens // passes
    reads, writes = [], []
    for cut in range(cuts):
        span = pl.ds(cut * height, height)
        reads.append(pltpu.make_async_copy(right_hbm.at[span], right.at[span], sems_in.at[cut]))
    for i in range(pieces):
        columns = pl.ds(i * tile, tile)
        for group, out in enumerate(outs):
            source = stage.at[pl.ds(group * part, part), columns]
            writes.append(pltpu.make_async_copy(source, out.at[:, columns], sems_out.at[i, group]))
    read_coef = pltpu.make_async_copy(coef_hbm, coef, sems_left.at[0])
    write_near = pltpu.make_async_copy(near_rows, near_left, sems_left.at[1])
    read_coef.start()
    for read in reads:
        read.start()
    read_coef.wait()
    by_latent[...] = coef[...].T
    ordered_rows(size, rows, by_latent, (left, near_rows))
    write_near.start()
    for step in range(passes):
        for read in reads[step * cuts // passes : (step + 1) * cuts // passes]:
            read.wait()
        span = slice(step * depth, (step + 1) * depth)
        for i in range(pieces):
            columns = slice(i * tile, (i + 1) * tile)
            out = jnp.dot(left[:, span], right[span, columns], preferred_element_type=jnp.float32)
            if step > 0:
                out = out + total[:, columns]
            if step < passes - 1:
                total[:, columns] = out
            else:
                stage[:, columns] = out.astype(stage.dtype)
                for write in writes[2 * i : 2 * i + 2]:
                    write.start()
    for write in writes + [write_near]:
        write.wait()


def stream_far_product(coef, right, size, rows):
    tokens, latents = coef.shape
    width = right.shape[1]
    part, half = latents // 4, latents // 2
    pieces, cuts = 4, 8
    anywhere = pl.BlockSpec(memory_space=pl.ANY)
    return pl.pallas_call(
        functools.partial(stream_kernel, size, rows),
        in_specs=[anywhere] * 2,
        out_specs=[anywhere] * 3,
        out_shape=[jax.ShapeDtypeStruct((part, width), coef.dtype)] * 2
        + [jax.ShapeDtypeStruct((half, tokens), coef.dtype)],
        scratch_shapes=[
            pltpu.VMEM((tokens, latents), coef.dtype),
            pltpu.VMEM((tokens, width), coef.dtype),
            pltpu.VMEM((latents, tokens), coef.dtype),
            pltpu.VMEM((half, tokens), coef.dtype),
            pltpu.VMEM((half, tokens), coef.dtype),
            pltpu.VMEM((half, width), jnp.float32),
            pltpu.VMEM((half, width), coef.dtype),
            pltpu.SemaphoreType.DMA((2,)),
            pltpu.SemaphoreType.DMA((cuts,)),
            pltpu.SemaphoreType.DMA((pieces, 2)),
        ],
        compiler_params=params(52),
        cost_estimate=cost(
            latents * tokens * width, 2 * (tokens * width + latents * tokens) + latents * width
        ),
        name="stream_far_product",
    )(coef, right)


def multiply(left_ref, right_ref, outs):
    out = jnp.dot(left_ref[...], right_ref[...], preferred_element_type=jnp.float32)
    part = outs[0].shape[0]
    for i, ref in enumerate(outs):
        ref[...] = out[i * part : (i + 1) * part].astype(ref.dtype)


def select_far_kernel(size, rows, count, coef_ref, right_ref, picks_ref, *refs):
    pieces, refs = refs[:count], refs[count:]
    outs, near_left, own_code, (by_latent, left, table, codes) = refs[:2], refs[2], refs[3], refs[4:]

    @pl.when(pl.program_id(0) == 0)
    def _():
        height = size // count
        for i, piece in enumerate(pieces):
            table[i * height : (i + 1) * height] = piece[...]
        code = row_codes(size, rows, table[...], picks_ref)
        codes[...] = code
        own_code[...] = codes[pl.ds(pl.multiple_of(lax.axis_index("latent") * rows, rows), rows)]
        tokens = lax.broadcasted_iota(jnp.int32, by_latent.shape, 1)
        by_latent[...] = jnp.where(
            code == KEPT, coef_ref[...].T, (tokens == code).astype(by_latent.dtype)
        )
        ordered_rows(size, rows, by_latent, (left, near_left))

    multiply(left, right_ref, outs)


def near_kernel(left_ref, right_ref, *outs):
    multiply(left_ref, right_ref, outs)


def product(kernel, left, right, others, out_more, scratch, name):
    tokens, width = right.shape
    tile = 512
    part = left.size // tokens // (4 if out_more else 2)
    fixed = lambda j: (0, 0)
    in_specs = [pl.BlockSpec(left.shape, fixed), pl.BlockSpec((tokens, tile), lambda j: (0, j))]
    return pl.pallas_call(
        kernel,
        grid=(width // tile,),
        in_specs=in_specs + [pl.BlockSpec(value.shape, fixed) for value in others],
        out_specs=[pl.BlockSpec((part, tile), lambda j: (0, j))] * 2
        + [pl.BlockSpec(value.shape, fixed) for value in out_more],
        out_shape=[jax.ShapeDtypeStruct((part, width), left.dtype)] * 2 + list(out_more),
        scratch_shapes=scratch,
        compiler_params=params(20),
        cost_estimate=cost(
            12 * part * tokens * width, 2 * (tokens * width + 2 * part * (tokens + width))
        ),
        name=name,
    )(left, right, *others)


def far_product(coef, right, size, rows, picks, table):
    tokens, latents = coef.shape
    near_left = jax.ShapeDtypeStruct((latents // 2, tokens), coef.dtype)
    code = jax.ShapeDtypeStruct((rows, 1), jnp.int32)
    scratch = [
        pltpu.VMEM((latents, tokens), coef.dtype),
        pltpu.VMEM((latents // 2, tokens), coef.dtype),
        pltpu.VMEM((size, table[0].shape[1]), jnp.int32),
        pltpu.VMEM((latents, 1), jnp.int32),
    ]
    kernel = functools.partial(select_far_kernel, size, rows, len(table))
    others = [picks] + list(table)
    return product(kernel, coef, right, others, [near_left, code], scratch, "far_product")


def near_product(left, right):
    return product(near_kernel, left, right, [], [], [], "near_product")


def term(kept, from_core, slot, rows):
    slots = kept[0].shape[0] // rows
    group, begin = slot // slots, slot % slots * rows
    pair = (kept[group], from_core[group])
    return sum(value[begin : begin + rows].astype(jnp.float32) for value in pair)


def updated(refs):
    code, states, terms = refs[0], refs[1:7], refs[7:15]
    reset = code[...] != KEPT
    enc_grad, dec_grad = (
        sum(ref[...].astype(jnp.float32) for ref in half) for half in (terms[:4], terms[4:])
    )
    enc = adam_update(*(ref[...] for ref in states[:3]), enc_grad)
    dec = adam_update(*(ref[...] for ref in states[3:]), dec_grad)
    enc_w = jnp.where(reset, reset_gain * enc_grad * inverse_rms(enc_grad), enc[0])
    dec_w = jnp.where(reset, enc_grad, dec[0])
    dec_w = dec_w * inverse_rms(dec_w)
    moments = [jnp.where(reset, 0.0, value) for value in enc[1:] + dec[1:]]
    return [enc_w] + moments[:2] + [dec_w] + moments[2:]


def blocks_kernel(*refs):
    results, blocks = updated(refs), refs[-1]
    blocks[0] = results[0].astype(blocks.dtype)
    blocks[1] = results[3].astype(blocks.dtype)


def states_kernel(*refs):
    for ref, value in zip(refs[-6:], updated(refs)):
        ref[...] = value


def update(code, states, enc_parts, dec_parts, came, blocks_only):
    rows, width = states[0].shape
    tile = 16

    def row_tile(value, skipped):
        return pl.BlockSpec((tile, value.shape[1]), lambda i: (i + skipped // tile, 0))

    operands = [(value, 0) for value in [code] + list(states)]
    for parts, first in ((enc_parts, 0), (dec_parts, rows)):
        operands += [(value, value.shape[0] - rows) for value in parts]
        operands += [(value, first) for value in came]
    if blocks_only:
        out_shape = [jax.ShapeDtypeStruct((2, rows, width), jnp.bfloat16)]
        out_specs = [pl.BlockSpec((2, tile, width), lambda i: (0, i, 0))]
    else:
        out_shape = [jax.ShapeDtypeStruct((rows, width), jnp.float32)] * 6
        out_specs = [pl.BlockSpec((tile, width), lambda i: (i, 0))] * 6
    return pl.pallas_call(
        blocks_kernel if blocks_only else states_kernel,
        grid=(rows // tile,),
        in_specs=[row_tile(*operand) for operand in operands],
        out_specs=out_specs,
        out_shape=out_shape,
        cost_estimate=cost(10 * rows * width, 10 * rows * width),
        compiler_params=params(20),
        name="blocks" if blocks_only else "states",
    )(*(value for value, _ in operands))


def place_kernel(plan, size, rows, count, *refs):
    pieces, outs, sems = refs[:count], refs[-3:-1], refs[-1]
    copies = []
    for i, (offset, other_core, column) in enumerate(plan):
        start = pl.multiple_of(owner_at(offset, other_core, size) * rows, rows)
        for whole, out in enumerate(outs):
            source = pieces[i].at[pl.ds(whole * rows, rows)]
            target = out.at[pl.ds(start, rows), pl.ds(column, pieces[i].shape[1])]
            copies.append(pltpu.make_async_copy(source, target, sems.at[i, whole]))
    for copy in copies:
        copy.start()
    for copy in copies:
        copy.wait()


def place(pieces, wholes, size, rows, width):
    operands = [value for _, _, _, value in pieces]
    plan = [piece[:3] for piece in pieces]
    count = len(operands)
    first = wholes is None
    if not first:
        operands += list(wholes)
    anywhere = pl.BlockSpec(memory_space=pl.ANY)
    return pl.pallas_call(
        functools.partial(place_kernel, plan, size, rows, count),
        out_shape=[jax.ShapeDtypeStruct((size * rows, width), operands[0].dtype)] * 2,
        in_specs=[anywhere] * len(operands),
        out_specs=[anywhere] * 2,
        scratch_shapes=[pltpu.SemaphoreType.DMA((count, 2))],
        input_output_aliases={} if first else {count: 0, count + 1: 1},
        compiler_params=params(4),
        cost_estimate=cost(0, 8 * count * rows * width),
        name="place",
    )(*operands)


def gathered(block, order, size, rows):
    chips = size // 2
    width = block.shape[1]
    half = width // 2
    hops = chips // 2
    right = left = block
    near, far, wholes = [(0, 0, 0, after(block, order))], [], None
    for hop in range(1, hops + 1):
        if hop == hops:
            right, left = right[:, :half], left[:, half:]
        right, left = shift(right, 1, size), shift(left, -1, size)
        sent = [(offset, 1, column, swap(value, 1, size)) for offset, _, column, value in near]
        wholes = place(near + far, wholes, size, rows, width)
        far = sent
        right, wholes = tied(right, wholes)
        left = after(left, right)
        near = [(-hop, 0, 0, right), (hop, 0, half if hop == hops else 0, left)]
    sent = [(offset, 1, column, swap(value, 1, size)) for offset, _, column, value in near]
    wholes = place(near, wholes, size, rows, width)
    return place(far + sent, wholes, size, rows, width)


def shards(
    x_rows,
    out_grad,
    enc_coef,
    latent_act,
    enc_w,
    enc_m,
    enc_v,
    dec_w,
    dec_m,
    dec_v,
    dead_order,
    pick_rows,
    send_count,
):
    rows, width = enc_w.shape
    half = width // 2
    size = lax.axis_size("latent")
    chips = size // 2
    stages = gather_table(jnp.concatenate([send_count, dead_order], axis=1), size)
    table = stages[-1]
    dec_sent, kept, dec_left = stream_far_product(latent_act, out_grad, size, rows)
    dec_sent = after(dec_sent, *stages[0])
    dec_kept, dec_core = [kept], [swap(dec_sent, 1, size)]
    enc_sent, kept, enc_left, code = far_product(
        after(enc_coef, dec_sent), x_rows, size, rows, pick_rows[0].T, table
    )
    enc_kept, enc_core = [kept], [swap(enc_sent, 1, size)]

    def both(slot):
        terms = [term(*pair, slot, rows) for pair in ((enc_kept, enc_core), (dec_kept, dec_core))]
        return jnp.concatenate(terms, axis=0)

    def travel(moving):
        return [shift(moving[0], 1, size), shift(moving[1], -1, size)]

    far = both(0).astype(jnp.bfloat16)
    moving = [far[:, :half], far[:, half:]]
    enc_sent, kept = near_product(after(enc_left, *moving), x_rows)
    came, enc_sent = tied(travel(moving), enc_sent)
    enc_kept.append(kept)
    enc_core.append(swap(enc_sent, 1, size))
    for hop in range(1, chips // 2):
        moving = []
        for side, value in enumerate(came):
            value = value.astype(jnp.float32)
            if value.shape[1] < width:
                pads = ((0, 0, 0), (0, half, 0) if side == 0 else (half, 0, 0))
                value = lax.pad(value, jnp.float32(0), pads)
            moving.append((value + both(2 * hop - side)).astype(jnp.bfloat16))
        came = travel(moving)
        if hop == 1:
            dec_sent, kept = near_product(after(dec_left, *moving), out_grad)
            dec_kept.append(kept)
            dec_core.append(swap(dec_sent, 1, size))
    states = (enc_w, enc_m, enc_v, dec_w, dec_m, dec_v)
    parts = ([enc_kept[1], enc_core[1]], [dec_kept[1], dec_core[1]], came)
    (blocks,) = update(code, states, *parts, True)
    results = update(code, after(states, blocks), *parts, False)
    enc_full, dec_full = gathered(blocks.reshape(2 * rows, width), results[0], size, rows)
    return (*results, enc_full, dec_full)


def solution(mesh):
    split = P(("groups", "latent"), None)
    placed = (split,) * 11 + (P(("groups", "latent"), None, None), split)
    return jax.shard_map(
        shards,
        mesh=mesh,
        in_specs=placed,
        out_specs=(split,) * 6 + (P("groups", None),) * 2,
        check_vma=False,
    )
```

```python
import functools

import jax
import jax.numpy as jnp
from jax import lax
from jax.experimental import pallas as pl
from jax.experimental.pallas import tpu as pltpu
from jax.sharding import PartitionSpec as P

beta_one = 0.9
beta_two = 0.99
first_fix = 1.0 - 0.9**4
second_fix = 1.0 - 0.99**4
learn_rate = 0.02
adam_eps = 1e-08
reset_gain = 0.01
norm_eps = 1e-06

KEPT = -1
ABSENT = -2


def adam_update(weight, moment, second, gradient):
    moment_new = beta_one * moment + (1.0 - beta_one) * gradient
    second_new = beta_two * second + (1.0 - beta_two) * gradient * gradient
    weight_new = weight - learn_rate * (moment_new / first_fix) / (
        jnp.sqrt(second_new / second_fix) + adam_eps
    )
    return (weight_new, moment_new, second_new)


def inverse_rms(value):
    return lax.rsqrt(jnp.mean(value * value, axis=1, keepdims=True) + norm_eps)


def swap(value, bits, size):
    return lax.ppermute(value, "latent", [(i, i ^ bits) for i in range(size)])


def after(value, *others):
    return lax.optimization_barrier((value,) + others)[0]


def tied(*values):
    return lax.optimization_barrier(values)


def params(mebibytes):
    return pltpu.CompilerParams(vmem_limit_bytes=mebibytes * 2**20)


def cost(flops, moved):
    return pl.CostEstimate(flops=int(flops), bytes_accessed=int(moved), transcendentals=0)


def chip_at(position, chips):
    return jnp.where(position < chips // 2, 2 * position, 2 * (chips - 1 - position) + 1)


def position_of(chip, chips):
    return jnp.where(chip % 2 == 0, chip // 2, chips - 1 - chip // 2)


def owner_at(offset, other_core, size):
    me = lax.axis_index("latent")
    chips = size // 2
    position = lax.rem(position_of(me // 2, chips) + offset + chips, chips)
    return 2 * chip_at(position, chips) + ((me % 2) ^ other_core)


def shift(value, step, size):
    chips = size // 2
    ring = [2 * q for q in range(chips // 2)] + [2 * q + 1 for q in reversed(range(chips // 2))]
    pairs = [
        (2 * ring[p] + core, 2 * ring[(p + step) % chips] + core)
        for p in range(chips)
        for core in range(2)
    ]
    return lax.ppermute(value, "latent", pairs)


def gather_table(row, size):
    stages, step = [], 1
    pieces = [row]
    while step < size:
        if step > 1:
            pieces = [jnp.concatenate(pieces, axis=0)]
        pieces += [swap(pieces[0], step * k, size) for k in range(1, min(4, size // step))]
        stages.append(pieces)
        step *= len(pieces)
    return stages


def ordered_rows(size, rows, by_latent, groups):
    chips = size // 2
    for block in range(size):
        group, inside = block // chips, block % chips
        slot = group * (chips // 2) + inside % (chips // 2)
        far = chips // 2 - slot // 2
        offset = far if slot % 2 == 0 else 1 - far
        owner = owner_at(offset, 1 - inside // (chips // 2), size)
        begin = pl.multiple_of(owner * rows, rows)
        groups[group][inside * rows : (inside + 1) * rows] = by_latent[pl.ds(begin, rows)]


def row_codes(size, rows, table, picks_ref):
    me = lax.axis_index("latent")
    counts = table[:, :size]
    order = table[:, size:]
    source = me ^ lax.broadcasted_iota(jnp.int32, (size, 1), 0)
    before = jnp.sum(jnp.where(source < me, counts, 0), axis=0, keepdims=True)
    total = jnp.sum(counts, axis=0, keepdims=True)
    owners = lax.broadcasted_iota(jnp.int32, (size, size), 1) == source

    def by_key(row):
        return jnp.sum(jnp.where(owners, row, 0), axis=1, keepdims=True)

    begin, here = by_key(before), by_key(counts[:1])
    place = lax.broadcasted_iota(jnp.int32, (size, rows), 1)
    token = jnp.full((size, rows), ABSENT, jnp.int32)
    for c in range(picks_ref.shape[0]):
        own = (place == begin + c) & (here > c)
        token = jnp.where(own, by_key(picks_ref[c : c + 1]), token)
    token = jnp.where(place < by_key(total), token, KEPT)
    latent = lax.broadcasted_iota(jnp.int32, (size * rows, 1), 0)
    keys = lax.broadcasted_iota(jnp.int32, (size * rows, size), 1)
    spread = (keys == (me ^ (latent // rows))).astype(jnp.float32)

    def by_row(values):
        return jnp.dot(spread, values.astype(jnp.float32), precision=lax.Precision.HIGHEST)

    is_latent = by_row(order) == (latent % rows).astype(jnp.float32)
    code = jnp.sum(jnp.where(is_latent, by_row(token), 0.0), axis=1, keepdims=True)
    return (code + jnp.where(code < 0, -0.5, 0.5)).astype(jnp.int32)


def stream_kernel(size, rows, coef_ref, right_hbm, *refs):
    outs, (right, by_latent, by_slot, stage, sems_in, sems_out) = refs[:4], refs[4:]
    tokens, width = right.shape
    part = outs[0].shape[0]
    pieces, cuts = sems_in.shape
    tile, height = width // pieces, tokens // cuts
    reads, writes = [], []
    for i in range(pieces):
        columns = pl.ds(i * tile, tile)
        reads.append([])
        for cut in range(cuts):
            span = pl.ds(cut * height, height)
            reads[i].append(
                pltpu.make_async_copy(
                    right_hbm.at[span, columns], right.at[span, columns], sems_in.at[i, cut]
                )
            )
        for group, out in enumerate(outs):
            source = stage.at[pl.ds(group * part, part), columns]
            writes.append(pltpu.make_async_copy(source, out.at[:, columns], sems_out.at[i, group]))
    for read in sum(reads, []):
        read.start()
    by_latent[...] = coef_ref[...].T
    far_rows = by_slot.shape[0] // 2
    ordered_rows(
        size, rows, by_latent, (by_slot.at[pl.ds(0, far_rows)], by_slot.at[pl.ds(far_rows, far_rows)])
    )
    for i in range(pieces):
        for read in reads[i]:
            read.wait()
        columns = slice(i * tile, (i + 1) * tile)
        out = jnp.dot(by_slot[...], right[:, columns], preferred_element_type=jnp.float32)
        stage[:, columns] = out.astype(stage.dtype)
        for write in writes[4 * i : 4 * i + 4]:
            write.start()
    for write in writes:
        write.wait()


def stream_product(coef, right, size, rows):
    tokens, latents = coef.shape
    width = right.shape[1]
    part = latents // 4
    pieces, cuts = 4, 4
    anywhere = pl.BlockSpec(memory_space=pl.ANY)
    return pl.pallas_call(
        functools.partial(stream_kernel, size, rows),
        in_specs=[pl.BlockSpec(memory_space=pltpu.VMEM), anywhere],
        out_specs=[anywhere] * 4,
        out_shape=[jax.ShapeDtypeStruct((part, width), coef.dtype)] * 4,
        scratch_shapes=[
            pltpu.VMEM((tokens, width), coef.dtype),
            pltpu.VMEM((latents, tokens), coef.dtype),
            pltpu.VMEM((latents, tokens), coef.dtype),
            pltpu.VMEM((latents, width), coef.dtype),
            pltpu.SemaphoreType.DMA((pieces, cuts)),
            pltpu.SemaphoreType.DMA((pieces, 4)),
        ],
        compiler_params=params(50),
        cost_estimate=cost(
            2 * latents * tokens * width, 2 * (tokens * width + latents * (tokens + width))
        ),
        name="product",
    )(coef, right)


def multiply(left_ref, right_ref, outs):
    out = jnp.dot(left_ref[...], right_ref[...], preferred_element_type=jnp.float32)
    part = outs[0].shape[0]
    for i, ref in enumerate(outs):
        ref[...] = out[i * part : (i + 1) * part].astype(ref.dtype)


def select_far_kernel(size, rows, count, coef_ref, right_ref, picks_ref, *refs):
    pieces, refs = refs[:count], refs[count:]
    outs, near_left, own_code, (by_latent, left, table, codes) = refs[:2], refs[2], refs[3], refs[4:]

    @pl.when(pl.program_id(0) == 0)
    def _():
        height = size // count
        for i, piece in enumerate(pieces):
            table[i * height : (i + 1) * height] = piece[...]
        code = row_codes(size, rows, table[...], picks_ref)
        codes[...] = code
        own_code[...] = codes[pl.ds(pl.multiple_of(lax.axis_index("latent") * rows, rows), rows)]
        tokens = lax.broadcasted_iota(jnp.int32, by_latent.shape, 1)
        by_latent[...] = jnp.where(
            code == KEPT, coef_ref[...].T, (tokens == code).astype(by_latent.dtype)
        )
        ordered_rows(size, rows, by_latent, (left, near_left))

    multiply(left, right_ref, outs)


def near_kernel(left_ref, right_ref, *outs):
    multiply(left_ref, right_ref, outs)


def product(kernel, left, right, others, out_more, scratch, name):
    tokens, width = right.shape
    tile = 512
    part = left.size // tokens // (4 if out_more else 2)
    fixed = lambda j: (0, 0)
    in_specs = [pl.BlockSpec(left.shape, fixed), pl.BlockSpec((tokens, tile), lambda j: (0, j))]
    return pl.pallas_call(
        kernel,
        grid=(width // tile,),
        in_specs=in_specs + [pl.BlockSpec(value.shape, fixed) for value in others],
        out_specs=[pl.BlockSpec((part, tile), lambda j: (0, j))] * 2
        + [pl.BlockSpec(value.shape, fixed) for value in out_more],
        out_shape=[jax.ShapeDtypeStruct((part, width), left.dtype)] * 2 + list(out_more),
        scratch_shapes=scratch,
        compiler_params=params(20),
        cost_estimate=cost(
            4 * part * tokens * width, 2 * (tokens * width + 2 * part * (tokens + width))
        ),
        name=name,
    )(left, right, *others)


def far_product(coef, right, size, rows, picks, table):
    tokens, latents = coef.shape
    near_left = jax.ShapeDtypeStruct((latents // 2, tokens), coef.dtype)
    code = jax.ShapeDtypeStruct((rows, 1), jnp.int32)
    scratch = [
        pltpu.VMEM((latents, tokens), coef.dtype),
        pltpu.VMEM((latents // 2, tokens), coef.dtype),
        pltpu.VMEM((size, table[0].shape[1]), jnp.int32),
        pltpu.VMEM((latents, 1), jnp.int32),
    ]
    kernel = functools.partial(select_far_kernel, size, rows, len(table))
    others = [picks] + list(table)
    return product(kernel, coef, right, others, [near_left, code], scratch, "far_product")


def near_product(left, right):
    return product(near_kernel, left, right, [], [], [], "near_product")


def term(kept, from_core, slot, rows):
    slots = kept[0].shape[0] // rows
    group, begin = slot // slots, slot % slots * rows
    pair = (kept[group], from_core[group])
    return sum(value[begin : begin + rows].astype(jnp.float32) for value in pair)


def updated(refs):
    code, states, terms = refs[0], refs[1:7], refs[7:15]
    reset = code[...] != KEPT
    enc_grad, dec_grad = (
        sum(ref[...].astype(jnp.float32) for ref in half) for half in (terms[:4], terms[4:])
    )
    enc = adam_update(*(ref[...] for ref in states[:3]), enc_grad)
    dec = adam_update(*(ref[...] for ref in states[3:]), dec_grad)
    enc_w = jnp.where(reset, reset_gain * enc_grad * inverse_rms(enc_grad), enc[0])
    dec_w = jnp.where(reset, enc_grad, dec[0])
    dec_w = dec_w * inverse_rms(dec_w)
    moments = [jnp.where(reset, 0.0, value) for value in enc[1:] + dec[1:]]
    return [enc_w] + moments[:2] + [dec_w] + moments[2:]


def blocks_kernel(*refs):
    results, blocks = updated(refs), refs[-1]
    blocks[0] = results[0].astype(blocks.dtype)
    blocks[1] = results[3].astype(blocks.dtype)


def states_kernel(*refs):
    for ref, value in zip(refs[-6:], updated(refs)):
        ref[...] = value


def update(code, states, enc_parts, dec_parts, came, blocks_only):
    rows, width = states[0].shape
    tile = 16

    def row_tile(value, skipped):
        return pl.BlockSpec((tile, value.shape[1]), lambda i: (i + skipped // tile, 0))

    operands = [(value, 0) for value in [code] + list(states)]
    for parts, first in ((enc_parts, 0), (dec_parts, rows)):
        operands += [(value, value.shape[0] - rows) for value in parts]
        operands += [(value, first) for value in came]
    if blocks_only:
        out_shape = [jax.ShapeDtypeStruct((2, rows, width), jnp.bfloat16)]
        out_specs = [pl.BlockSpec((2, tile, width), lambda i: (0, i, 0))]
    else:
        out_shape = [jax.ShapeDtypeStruct((rows, width), jnp.float32)] * 6
        out_specs = [pl.BlockSpec((tile, width), lambda i: (i, 0))] * 6
    return pl.pallas_call(
        blocks_kernel if blocks_only else states_kernel,
        grid=(rows // tile,),
        in_specs=[row_tile(*operand) for operand in operands],
        out_specs=out_specs,
        out_shape=out_shape,
        cost_estimate=cost(10 * rows * width, 10 * rows * width),
        compiler_params=params(20),
        name="blocks" if blocks_only else "states",
    )(*(value for value, _ in operands))


def place_kernel(plan, size, rows, count, *refs):
    pieces, outs, sems = refs[:count], refs[-3:-1], refs[-1]
    copies = []
    for i, (offset, other_core, column) in enumerate(plan):
        start = pl.multiple_of(owner_at(offset, other_core, size) * rows, rows)
        for whole, out in enumerate(outs):
            source = pieces[i].at[pl.ds(whole * rows, rows)]
            target = out.at[pl.ds(start, rows), pl.ds(column, pieces[i].shape[1])]
            copies.append(pltpu.make_async_copy(source, target, sems.at[i, whole]))
    for copy in copies:
        copy.start()
    for copy in copies:
        copy.wait()


def place(pieces, wholes, size, rows, width):
    operands = [value for _, _, _, value in pieces]
    plan = [piece[:3] for piece in pieces]
    count = len(operands)
    first = wholes is None
    if not first:
        operands += list(wholes)
    anywhere = pl.BlockSpec(memory_space=pl.ANY)
    return pl.pallas_call(
        functools.partial(place_kernel, plan, size, rows, count),
        out_shape=[jax.ShapeDtypeStruct((size * rows, width), operands[0].dtype)] * 2,
        in_specs=[anywhere] * len(operands),
        out_specs=[anywhere] * 2,
        scratch_shapes=[pltpu.SemaphoreType.DMA((count, 2))],
        input_output_aliases={} if first else {count: 0, count + 1: 1},
        compiler_params=params(4),
        cost_estimate=cost(0, 8 * count * rows * width),
        name="place",
    )(*operands)


def gathered(block, order, size, rows):
    chips = size // 2
    width = block.shape[1]
    half = width // 2
    hops = chips // 2
    right = left = block
    near, far, wholes = [(0, 0, 0, after(block, order))], [], None
    for hop in range(1, hops + 1):
        if hop == hops:
            right, left = right[:, :half], left[:, half:]
        right, left = shift(right, 1, size), shift(left, -1, size)
        sent = [(offset, 1, column, swap(value, 1, size)) for offset, _, column, value in near]
        wholes = place(near + far, wholes, size, rows, width)
        far = sent
        right, wholes = tied(right, wholes)
        left = after(left, right)
        near = [(-hop, 0, 0, right), (hop, 0, half if hop == hops else 0, left)]
    sent = [(offset, 1, column, swap(value, 1, size)) for offset, _, column, value in near]
    wholes = place(near, wholes, size, rows, width)
    return place(far + sent, wholes, size, rows, width)


def shards(
    x_rows,
    out_grad,
    enc_coef,
    latent_act,
    enc_w,
    enc_m,
    enc_v,
    dec_w,
    dec_m,
    dec_v,
    dead_order,
    pick_rows,
    send_count,
):
    rows, width = enc_w.shape
    half = width // 2
    size = lax.axis_size("latent")
    chips = size // 2
    stages = gather_table(jnp.concatenate([send_count, dead_order], axis=1), size)
    table = stages[-1]
    dec = stream_product(latent_act, out_grad, size, rows)
    dec_far = after(dec[0], *stages[0])
    dec_kept = [dec[1], dec[3]]
    dec_core = [swap(dec_far, 1, size), swap(after(dec[2], table[0]), 1, size)]

    def travel(moving):
        return [shift(moving[0], 1, size), shift(moving[1], -1, size)]

    def begin(kept, from_core):
        far = term(kept, from_core, 0, rows).astype(jnp.bfloat16)
        return [far[:, :half], far[:, half:]]

    def second(came, kept, from_core, order):
        moving = []
        for side, value in enumerate(after(came, order)):
            pads = ((0, 0, 0), (0, half, 0) if side == 0 else (half, 0, 0))
            value = lax.pad(value.astype(jnp.float32), jnp.float32(0), pads)
            value = value + term(kept, from_core, 2 - side, rows)
            moving.append(value.astype(jnp.bfloat16))
        return moving

    dec_moving = begin(dec_kept, after(dec_core, table[0]))
    enc_sent, kept, enc_left, code = far_product(
        after(enc_coef, *dec_moving), x_rows, size, rows, pick_rows[0].T, table
    )
    dec_came, enc_sent = tied(travel(dec_moving), enc_sent)
    enc_kept, enc_core = [kept], [swap(enc_sent, 1, size)]
    dec_moving = second(dec_came, dec_kept, dec_core, enc_sent)
    enc_moving = begin(enc_kept, after(enc_core, *dec_moving))
    enc_sent, kept = near_product(after(enc_left, *enc_moving), x_rows)
    enc_came, dec_came, enc_sent = tied(travel(enc_moving), travel(dec_moving), enc_sent)
    enc_kept.append(kept)
    enc_core.append(swap(enc_sent, 1, size))
    enc_came = travel(second(enc_came, enc_kept, enc_core, enc_sent))
    came = [jnp.concatenate(pair, axis=0) for pair in zip(enc_came, dec_came)]
    for hop in range(2, chips // 2):
        moving = []
        for side, value in enumerate(came):
            slot = 2 * hop - side
            terms = [term(*pair, slot, rows) for pair in ((enc_kept, enc_core), (dec_kept, dec_core))]
            value = value.astype(jnp.float32) + jnp.concatenate(terms, axis=0)
            moving.append(value.astype(jnp.bfloat16))
        came = travel(moving)
    states = (enc_w, enc_m, enc_v, dec_w, dec_m, dec_v)
    parts = ([enc_kept[1], enc_core[1]], [dec_kept[1], dec_core[1]], came)
    (blocks,) = update(code, states, *parts, True)
    results = update(code, after(states, blocks), *parts, False)
    enc_full, dec_full = gathered(blocks.reshape(2 * rows, width), results[0], size, rows)
    return (*results, enc_full, dec_full)


def solution(mesh):
    split = P(("groups", "latent"), None)
    placed = (split,) * 11 + (P(("groups", "latent"), None, None), split)
    return jax.shard_map(
        shards,
        mesh=mesh,
        in_specs=placed,
        out_specs=(split,) * 6 + (P("groups", None),) * 2,
        check_vma=False,
    )
```

```python
import functools

import jax
import jax.numpy as jnp
from jax import lax
from jax.experimental import pallas as pl
from jax.experimental.pallas import tpu as pltpu
from jax.sharding import PartitionSpec as P

beta_one = 0.9
beta_two = 0.99
first_fix = 1.0 - 0.9**4
second_fix = 1.0 - 0.99**4
learn_rate = 0.02
adam_eps = 1e-08
reset_gain = 0.01
norm_eps = 1e-06

KEPT = -1
ABSENT = -2


def adam_update(weight, moment, second, gradient):
    moment_new = beta_one * moment + (1.0 - beta_one) * gradient
    second_new = beta_two * second + (1.0 - beta_two) * gradient * gradient
    weight_new = weight - learn_rate * (moment_new / first_fix) / (
        jnp.sqrt(second_new / second_fix) + adam_eps
    )
    return (weight_new, moment_new, second_new)


def inverse_rms(value):
    return lax.rsqrt(jnp.mean(value * value, axis=1, keepdims=True) + norm_eps)


def swap(value, bits, size):
    return lax.ppermute(value, "latent", [(i, i ^ bits) for i in range(size)])


def after(value, *others):
    return lax.optimization_barrier((value,) + others)[0]


def tied(*values):
    return lax.optimization_barrier(values)


def params(mebibytes):
    return pltpu.CompilerParams(vmem_limit_bytes=mebibytes * 2**20)


def cost(flops, moved):
    return pl.CostEstimate(flops=int(flops), bytes_accessed=int(moved), transcendentals=0)


def chip_at(position, chips):
    return jnp.where(position < chips // 2, 2 * position, 2 * (chips - 1 - position) + 1)


def position_of(chip, chips):
    return jnp.where(chip % 2 == 0, chip // 2, chips - 1 - chip // 2)


def owner_at(offset, other_core, size):
    me = lax.axis_index("latent")
    chips = size // 2
    position = lax.rem(position_of(me // 2, chips) + offset + chips, chips)
    return 2 * chip_at(position, chips) + ((me % 2) ^ other_core)


def shift(value, step, size):
    chips = size // 2
    ring = [2 * q for q in range(chips // 2)] + [2 * q + 1 for q in reversed(range(chips // 2))]
    pairs = [
        (2 * ring[p] + core, 2 * ring[(p + step) % chips] + core)
        for p in range(chips)
        for core in range(2)
    ]
    return lax.ppermute(value, "latent", pairs)


def gather_table(row, size):
    stages, step = [], 1
    pieces = [row]
    while step < size:
        if step > 1:
            pieces = [jnp.concatenate(pieces, axis=0)]
        pieces += [swap(pieces[0], step * k, size) for k in range(1, min(4, size // step))]
        stages.append(pieces)
        step *= len(pieces)
    return stages


def ordered_rows(size, rows, by_latent, by_slot):
    chips = size // 2
    for block in range(size):
        group, inside = block // chips, block % chips
        slot = group * (chips // 2) + inside % (chips // 2)
        far = chips // 2 - slot // 2
        offset = far if slot % 2 == 0 else 1 - far
        owner = owner_at(offset, 1 - inside // (chips // 2), size)
        begin = pl.multiple_of(owner * rows, rows)
        by_slot[block * rows : (block + 1) * rows] = by_latent[pl.ds(begin, rows)]


def row_codes(size, rows, table, picks_ref):
    me = lax.axis_index("latent")
    counts = table[:, :size]
    order = table[:, size:]
    source = me ^ lax.broadcasted_iota(jnp.int32, (size, 1), 0)
    before = jnp.sum(jnp.where(source < me, counts, 0), axis=0, keepdims=True)
    total = jnp.sum(counts, axis=0, keepdims=True)
    owners = lax.broadcasted_iota(jnp.int32, (size, size), 1) == source

    def by_key(row):
        return jnp.sum(jnp.where(owners, row, 0), axis=1, keepdims=True)

    begin, here = by_key(before), by_key(counts[:1])
    place = lax.broadcasted_iota(jnp.int32, (size, rows), 1)
    token = jnp.full((size, rows), ABSENT, jnp.int32)
    for c in range(picks_ref.shape[0]):
        own = (place == begin + c) & (here > c)
        token = jnp.where(own, by_key(picks_ref[c : c + 1]), token)
    token = jnp.where(place < by_key(total), token, KEPT)
    latent = lax.broadcasted_iota(jnp.int32, (size * rows, 1), 0)
    keys = lax.broadcasted_iota(jnp.int32, (size * rows, size), 1)
    spread = (keys == (me ^ (latent // rows))).astype(jnp.float32)

    def by_row(values):
        return jnp.dot(spread, values.astype(jnp.float32), precision=lax.Precision.HIGHEST)

    is_latent = by_row(order) == (latent % rows).astype(jnp.float32)
    code = jnp.sum(jnp.where(is_latent, by_row(token), 0.0), axis=1, keepdims=True)
    return (code + jnp.where(code < 0, -0.5, 0.5)).astype(jnp.int32)


def multiply(by_slot, right_ref, outs):
    out = jnp.dot(by_slot[...], right_ref[...], preferred_element_type=jnp.float32)
    part = outs[0].shape[0]
    for i, ref in enumerate(outs):
        ref[...] = out[i * part : (i + 1) * part].astype(ref.dtype)


def stream_kernel(size, rows, coef_ref, right_hbm, *refs):
    outs, (right, by_latent, by_slot, stage, sems_in, sems_out) = refs[:4], refs[4:]
    tokens, width = right.shape
    part = outs[0].shape[0]
    pieces, cuts = sems_in.shape
    tile, height = width // pieces, tokens // cuts
    reads, writes = [], []
    for i in range(pieces):
        columns = pl.ds(i * tile, tile)
        reads.append([])
        for cut in range(cuts):
            span = pl.ds(cut * height, height)
            reads[i].append(
                pltpu.make_async_copy(
                    right_hbm.at[span, columns], right.at[span, columns], sems_in.at[i, cut]
                )
            )
        for group, out in enumerate(outs):
            source = stage.at[pl.ds(group * part, part), columns]
            writes.append(pltpu.make_async_copy(source, out.at[:, columns], sems_out.at[i, group]))
    for read in sum(reads, []):
        read.start()
    by_latent[...] = coef_ref[...].T
    ordered_rows(size, rows, by_latent, by_slot)
    for i in range(pieces):
        for read in reads[i]:
            read.wait()
        columns = slice(i * tile, (i + 1) * tile)
        out = jnp.dot(by_slot[...], right[:, columns], preferred_element_type=jnp.float32)
        stage[:, columns] = out.astype(stage.dtype)
        for write in writes[4 * i : 4 * i + 4]:
            write.start()
    for write in writes:
        write.wait()


def stream_product(coef, right, size, rows):
    tokens, latents = coef.shape
    width = right.shape[1]
    part = latents // 4
    pieces, cuts = 4, 4
    anywhere = pl.BlockSpec(memory_space=pl.ANY)
    return pl.pallas_call(
        functools.partial(stream_kernel, size, rows),
        in_specs=[pl.BlockSpec(memory_space=pltpu.VMEM), anywhere],
        out_specs=[anywhere] * 4,
        out_shape=[jax.ShapeDtypeStruct((part, width), coef.dtype)] * 4,
        scratch_shapes=[
            pltpu.VMEM((tokens, width), coef.dtype),
            pltpu.VMEM((latents, tokens), coef.dtype),
            pltpu.VMEM((latents, tokens), coef.dtype),
            pltpu.VMEM((latents, width), coef.dtype),
            pltpu.SemaphoreType.DMA((pieces, cuts)),
            pltpu.SemaphoreType.DMA((pieces, 4)),
        ],
        compiler_params=params(50),
        cost_estimate=cost(
            2 * latents * tokens * width, 2 * (tokens * width + latents * (tokens + width))
        ),
        name="product",
    )(coef, right)


def select_kernel(size, rows, count, coef_ref, right_ref, picks_ref, *refs):
    pieces, refs = refs[:count], refs[count:]
    outs, own_code, (by_latent, by_slot, table, codes) = refs[:4], refs[4], refs[5:]

    @pl.when(pl.program_id(0) == 0)
    def _():
        height = size // count
        for i, piece in enumerate(pieces):
            table[i * height : (i + 1) * height] = piece[...]
        code = row_codes(size, rows, table[...], picks_ref)
        codes[...] = code
        own_code[...] = codes[pl.ds(pl.multiple_of(lax.axis_index("latent") * rows, rows), rows)]
        tokens = lax.broadcasted_iota(jnp.int32, by_latent.shape, 1)
        by_latent[...] = jnp.where(
            code == KEPT, coef_ref[...].T, (tokens == code).astype(by_latent.dtype)
        )
        ordered_rows(size, rows, by_latent, by_slot)

    multiply(by_slot, right_ref, outs)


def select_product(coef, right, size, rows, picks, table):
    tokens, latents = coef.shape
    width = right.shape[1]
    tile = 512
    part = latents // 4
    fixed = lambda j: (0, 0)
    operands = [coef, right, picks] + list(table)
    in_specs = [pl.BlockSpec(value.shape, fixed) for value in operands]
    in_specs[1] = pl.BlockSpec((tokens, tile), lambda j: (0, j))
    return pl.pallas_call(
        functools.partial(select_kernel, size, rows, len(table)),
        grid=(width // tile,),
        in_specs=in_specs,
        out_specs=[pl.BlockSpec((part, tile), lambda j: (0, j))] * 4
        + [pl.BlockSpec((rows, 1), fixed)],
        out_shape=[jax.ShapeDtypeStruct((part, width), coef.dtype)] * 4
        + [jax.ShapeDtypeStruct((rows, 1), jnp.int32)],
        scratch_shapes=[
            pltpu.VMEM((latents, tokens), coef.dtype),
            pltpu.VMEM((latents, tokens), coef.dtype),
            pltpu.VMEM((size, table[0].shape[1]), jnp.int32),
            pltpu.VMEM((latents, 1), jnp.int32),
        ],
        compiler_params=params(24),
        cost_estimate=cost(
            2 * latents * tokens * width, 2 * (tokens * width + latents * (tokens + width))
        ),
        name="select_product",
    )(*operands)


def term(kept, from_core, slot, rows):
    slots = kept[0].shape[0] // rows
    group, begin = slot // slots, slot % slots * rows
    pair = (kept[group], from_core[group])
    return sum(value[begin : begin + rows].astype(jnp.float32) for value in pair)


def updated(refs):
    code, states, terms = refs[0], refs[1:7], refs[7:15]
    reset = code[...] != KEPT
    enc_grad, dec_grad = (
        sum(ref[...].astype(jnp.float32) for ref in half) for half in (terms[:4], terms[4:])
    )
    enc = adam_update(*(ref[...] for ref in states[:3]), enc_grad)
    dec = adam_update(*(ref[...] for ref in states[3:]), dec_grad)
    enc_w = jnp.where(reset, reset_gain * enc_grad * inverse_rms(enc_grad), enc[0])
    dec_w = jnp.where(reset, enc_grad, dec[0])
    dec_w = dec_w * inverse_rms(dec_w)
    moments = [jnp.where(reset, 0.0, value) for value in enc[1:] + dec[1:]]
    return [enc_w] + moments[:2] + [dec_w] + moments[2:]


def blocks_kernel(*refs):
    results, blocks = updated(refs), refs[-1]
    blocks[0] = results[0].astype(blocks.dtype)
    blocks[1] = results[3].astype(blocks.dtype)


def states_kernel(*refs):
    for ref, value in zip(refs[-6:], updated(refs)):
        ref[...] = value


def update(code, states, enc_parts, dec_parts, blocks_only):
    rows, width = states[0].shape
    tile = 16

    def row_tile(value, skipped):
        return pl.BlockSpec((tile, value.shape[1]), lambda i: (i + skipped // tile, 0))

    operands = [(value, 0) for value in [code] + list(states)]
    operands += [(value, value.shape[0] - rows) for value in enc_parts + dec_parts]
    if blocks_only:
        out_shape = [jax.ShapeDtypeStruct((2, rows, width), jnp.bfloat16)]
        out_specs = [pl.BlockSpec((2, tile, width), lambda i: (0, i, 0))]
    else:
        out_shape = [jax.ShapeDtypeStruct((rows, width), jnp.float32)] * 6
        out_specs = [pl.BlockSpec((tile, width), lambda i: (i, 0))] * 6
    return pl.pallas_call(
        blocks_kernel if blocks_only else states_kernel,
        grid=(rows // tile,),
        in_specs=[row_tile(*operand) for operand in operands],
        out_specs=out_specs,
        out_shape=out_shape,
        cost_estimate=cost(10 * rows * width, 10 * rows * width),
        compiler_params=params(20),
        name="blocks" if blocks_only else "states",
    )(*(value for value, _ in operands))


def place_kernel(plan, size, rows, count, *refs):
    pieces, outs, sems = refs[:count], refs[-3:-1], refs[-1]
    copies = []
    for i, (offset, other_core, column) in enumerate(plan):
        start = pl.multiple_of(owner_at(offset, other_core, size) * rows, rows)
        for whole, out in enumerate(outs):
            source = pieces[i].at[pl.ds(whole * rows, rows)]
            target = out.at[pl.ds(start, rows), pl.ds(column, pieces[i].shape[1])]
            copies.append(pltpu.make_async_copy(source, target, sems.at[i, whole]))
    for copy in copies:
        copy.start()
    for copy in copies:
        copy.wait()


def place(pieces, wholes, size, rows, width):
    operands = [value for _, _, _, value in pieces]
    plan = [piece[:3] for piece in pieces]
    count = len(operands)
    first = wholes is None
    if not first:
        operands += list(wholes)
    anywhere = pl.BlockSpec(memory_space=pl.ANY)
    return pl.pallas_call(
        functools.partial(place_kernel, plan, size, rows, count),
        out_shape=[jax.ShapeDtypeStruct((size * rows, width), operands[0].dtype)] * 2,
        in_specs=[anywhere] * len(operands),
        out_specs=[anywhere] * 2,
        scratch_shapes=[pltpu.SemaphoreType.DMA((count, 2))],
        input_output_aliases={} if first else {count: 0, count + 1: 1},
        compiler_params=params(4),
        cost_estimate=cost(0, 8 * count * rows * width),
        name="place",
    )(*operands)


def gathered(block, order, size, rows):
    chips = size // 2
    width = block.shape[1]
    half = width // 2
    hops = chips // 2
    right = left = block
    near, far, wholes = [(0, 0, 0, after(block, order))], [], None
    for hop in range(1, hops + 1):
        if hop == hops:
            right, left = right[:, :half], left[:, half:]
        right, left = shift(right, 1, size), shift(left, -1, size)
        sent = [(offset, 1, column, swap(value, 1, size)) for offset, _, column, value in near]
        wholes = place(near + far, wholes, size, rows, width)
        far = sent
        right, wholes = tied(right, wholes)
        left = after(left, right)
        near = [(-hop, 0, 0, right), (hop, 0, half if hop == hops else 0, left)]
    sent = [(offset, 1, column, swap(value, 1, size)) for offset, _, column, value in near]
    wholes = place(near, wholes, size, rows, width)
    return place(far + sent, wholes, size, rows, width)


def shards(
    x_rows,
    out_grad,
    enc_coef,
    latent_act,
    enc_w,
    enc_m,
    enc_v,
    dec_w,
    dec_m,
    dec_v,
    dead_order,
    pick_rows,
    send_count,
):
    rows, width = enc_w.shape
    half = width // 2
    size = lax.axis_size("latent")
    chips = size // 2
    stages = gather_table(jnp.concatenate([send_count, dead_order], axis=1), size)
    table = stages[-1]
    def begin(kept, from_core):
        far = term(kept, from_core, 0, rows).astype(jnp.bfloat16)
        return [far[:, :half], far[:, half:]]

    def travel(moving):
        return [shift(moving[0], 1, size), shift(moving[1], -1, size)]

    def advance(came, kept, from_core, hop):
        moving = []
        for side, value in enumerate(came):
            value = value.astype(jnp.float32)
            if value.shape[1] < width:
                pads = ((0, 0, 0), (0, half, 0) if side == 0 else (half, 0, 0))
                value = lax.pad(value, jnp.float32(0), pads)
            value = value + term(kept, from_core, 2 * hop - side, rows)
            moving.append(value.astype(jnp.bfloat16))
        return moving

    dec = stream_product(latent_act, out_grad, size, rows)
    dec_far = after(dec[0], *stages[0])
    dec_kept, dec_core = [dec[1], dec[3]], [swap(dec_far, 1, size), swap(after(dec[2], table[0]), 1, size)]
    dec_moving = begin(dec_kept, after(dec_core, table[0]))
    *enc, code = select_product(
        after(enc_coef, *dec_moving), x_rows, size, rows, pick_rows[0].T, table
    )
    dec_came, enc_far = tied(travel(dec_moving), enc[0])
    enc_kept, enc_core = [enc[1], enc[3]], [swap(enc_far, 1, size), swap(enc[2], 1, size)]
    dec_moving = advance(dec_came, dec_kept, dec_core, 1)
    dec_came = travel(dec_moving)
    enc_moving = begin(enc_kept, after(enc_core, *dec_moving))
    enc_came = travel(enc_moving)
    dec_came = after(dec_came, *enc_moving)
    for hop in range(1, chips // 2):
        if hop + 1 < chips // 2:
            dec_moving = advance(dec_came, dec_kept, dec_core, hop + 1)
            dec_came = travel(dec_moving)
            enc_came = after(enc_came, *dec_moving)
        enc_moving = advance(enc_came, enc_kept, enc_core, hop)
        enc_came = travel(enc_moving)
        dec_came = after(dec_came, *enc_moving)
    states = (enc_w, enc_m, enc_v, dec_w, dec_m, dec_v)
    parts = ([enc_kept[1], enc_core[1]] + enc_came, [dec_kept[1], dec_core[1]] + dec_came)
    (blocks,) = update(code, states, *parts, True)
    results = update(code, after(states, blocks), *parts, False)
    enc_full, dec_full = gathered(blocks.reshape(2 * rows, width), results[0], size, rows)
    return (*results, enc_full, dec_full)


def solution(mesh):
    split = P(("groups", "latent"), None)
    placed = (split,) * 11 + (P(("groups", "latent"), None, None), split)
    return jax.shard_map(
        shards,
        mesh=mesh,
        in_specs=placed,
        out_specs=(split,) * 6 + (P("groups", None),) * 2,
        check_vma=False,
    )
```

```python
import functools

import jax
import jax.numpy as jnp
from jax import lax
from jax.experimental import pallas as pl
from jax.experimental.pallas import tpu as pltpu
from jax.sharding import PartitionSpec as P

beta_one = 0.9
beta_two = 0.99
first_fix = 1.0 - 0.9**4
second_fix = 1.0 - 0.99**4
learn_rate = 0.02
adam_eps = 1e-08
reset_gain = 0.01
norm_eps = 1e-06

KEPT = -1
ABSENT = -2


def adam_update(weight, moment, second, gradient):
    moment_new = beta_one * moment + (1.0 - beta_one) * gradient
    second_new = beta_two * second + (1.0 - beta_two) * gradient * gradient
    weight_new = weight - learn_rate * (moment_new / first_fix) / (
        jnp.sqrt(second_new / second_fix) + adam_eps
    )
    return (weight_new, moment_new, second_new)


def inverse_rms(value):
    return lax.rsqrt(jnp.mean(value * value, axis=1, keepdims=True) + norm_eps)


def swap(value, bits, size):
    return lax.ppermute(value, "latent", [(i, i ^ bits) for i in range(size)])


def after(value, *others):
    return lax.optimization_barrier((value,) + others)[0]


def tied(*values):
    return lax.optimization_barrier(values)


def params(mebibytes):
    return pltpu.CompilerParams(vmem_limit_bytes=mebibytes * 2**20)


def cost(flops, moved):
    return pl.CostEstimate(flops=int(flops), bytes_accessed=int(moved), transcendentals=0)


def chip_at(position, chips):
    return jnp.where(position < chips // 2, 2 * position, 2 * (chips - 1 - position) + 1)


def position_of(chip, chips):
    return jnp.where(chip % 2 == 0, chip // 2, chips - 1 - chip // 2)


def owner_at(offset, other_core, size):
    me = lax.axis_index("latent")
    chips = size // 2
    position = lax.rem(position_of(me // 2, chips) + offset + chips, chips)
    return 2 * chip_at(position, chips) + ((me % 2) ^ other_core)


def shift(value, step, size):
    chips = size // 2
    ring = [2 * q for q in range(chips // 2)] + [2 * q + 1 for q in reversed(range(chips // 2))]
    pairs = [
        (2 * ring[p] + core, 2 * ring[(p + step) % chips] + core)
        for p in range(chips)
        for core in range(2)
    ]
    return lax.ppermute(value, "latent", pairs)


def gather_table(row, size):
    stages, step = [], 1
    pieces = [row]
    while step < size:
        if step > 1:
            pieces = [jnp.concatenate(pieces, axis=0)]
        pieces += [swap(pieces[0], step * k, size) for k in range(1, min(4, size // step))]
        stages.append(pieces)
        step *= len(pieces)
    return stages


def ordered_rows(size, rows, by_latent, by_slot):
    chips = size // 2
    for block in range(size):
        group, inside = block // chips, block % chips
        slot = group * (chips // 2) + inside % (chips // 2)
        far = chips // 2 - slot // 2
        offset = far if slot % 2 == 0 else 1 - far
        owner = owner_at(offset, 1 - inside // (chips // 2), size)
        begin = pl.multiple_of(owner * rows, rows)
        by_slot[block * rows : (block + 1) * rows] = by_latent[pl.ds(begin, rows)]


def row_codes(size, rows, table, picks_ref):
    me = lax.axis_index("latent")
    counts = table[:, :size]
    order = table[:, size:]
    source = me ^ lax.broadcasted_iota(jnp.int32, (size, 1), 0)
    before = jnp.sum(jnp.where(source < me, counts, 0), axis=0, keepdims=True)
    total = jnp.sum(counts, axis=0, keepdims=True)
    owners = lax.broadcasted_iota(jnp.int32, (size, size), 1) == source

    def by_key(row):
        return jnp.sum(jnp.where(owners, row, 0), axis=1, keepdims=True)

    begin, here = by_key(before), by_key(counts[:1])
    place = lax.broadcasted_iota(jnp.int32, (size, rows), 1)
    token = jnp.full((size, rows), ABSENT, jnp.int32)
    for c in range(picks_ref.shape[0]):
        own = (place == begin + c) & (here > c)
        token = jnp.where(own, by_key(picks_ref[c : c + 1]), token)
    token = jnp.where(place < by_key(total), token, KEPT)
    latent = lax.broadcasted_iota(jnp.int32, (size * rows, 1), 0)
    keys = lax.broadcasted_iota(jnp.int32, (size * rows, size), 1)
    spread = (keys == (me ^ (latent // rows))).astype(jnp.float32)

    def by_row(values):
        return jnp.dot(spread, values.astype(jnp.float32), precision=lax.Precision.HIGHEST)

    is_latent = by_row(order) == (latent % rows).astype(jnp.float32)
    code = jnp.sum(jnp.where(is_latent, by_row(token), 0.0), axis=1, keepdims=True)
    return (code + jnp.where(code < 0, -0.5, 0.5)).astype(jnp.int32)


def multiply(by_slot, right_ref, outs):
    out = jnp.dot(by_slot[...], right_ref[...], preferred_element_type=jnp.float32)
    part = outs[0].shape[0]
    for i, ref in enumerate(outs):
        ref[...] = out[i * part : (i + 1) * part].astype(ref.dtype)


def stream_kernel(size, rows, coef_ref, right_hbm, *refs):
    outs, (right, by_latent, by_slot, stage, sems_in, sems_out) = refs[:4], refs[4:]
    tokens, width = right.shape
    part = outs[0].shape[0]
    pieces, cuts = sems_in.shape
    tile, height = width // pieces, tokens // cuts
    reads, writes = [], []
    for i in range(pieces):
        columns = pl.ds(i * tile, tile)
        reads.append([])
        for cut in range(cuts):
            span = pl.ds(cut * height, height)
            reads[i].append(
                pltpu.make_async_copy(
                    right_hbm.at[span, columns], right.at[span, columns], sems_in.at[i, cut]
                )
            )
        for group, out in enumerate(outs):
            source = stage.at[pl.ds(group * part, part), columns]
            writes.append(pltpu.make_async_copy(source, out.at[:, columns], sems_out.at[i, group]))
    for read in sum(reads, []):
        read.start()
    by_latent[...] = coef_ref[...].T
    ordered_rows(size, rows, by_latent, by_slot)
    for i in range(pieces):
        for read in reads[i]:
            read.wait()
        columns = slice(i * tile, (i + 1) * tile)
        out = jnp.dot(by_slot[...], right[:, columns], preferred_element_type=jnp.float32)
        stage[:, columns] = out.astype(stage.dtype)
        for write in writes[4 * i : 4 * i + 4]:
            write.start()
    for write in writes:
        write.wait()


def stream_product(coef, right, size, rows):
    tokens, latents = coef.shape
    width = right.shape[1]
    part = latents // 4
    pieces, cuts = 4, 4
    anywhere = pl.BlockSpec(memory_space=pl.ANY)
    return pl.pallas_call(
        functools.partial(stream_kernel, size, rows),
        in_specs=[pl.BlockSpec(memory_space=pltpu.VMEM), anywhere],
        out_specs=[anywhere] * 4,
        out_shape=[jax.ShapeDtypeStruct((part, width), coef.dtype)] * 4,
        scratch_shapes=[
            pltpu.VMEM((tokens, width), coef.dtype),
            pltpu.VMEM((latents, tokens), coef.dtype),
            pltpu.VMEM((latents, tokens), coef.dtype),
            pltpu.VMEM((latents, width), coef.dtype),
            pltpu.SemaphoreType.DMA((pieces, cuts)),
            pltpu.SemaphoreType.DMA((pieces, 4)),
        ],
        compiler_params=params(50),
        cost_estimate=cost(
            2 * latents * tokens * width, 2 * (tokens * width + latents * (tokens + width))
        ),
        name="product",
    )(coef, right)


def select_kernel(size, rows, count, coef_ref, right_ref, picks_ref, *refs):
    pieces, refs = refs[:count], refs[count:]
    outs, own_code, (by_latent, by_slot, table, codes) = refs[:4], refs[4], refs[5:]

    @pl.when(pl.program_id(0) == 0)
    def _():
        height = size // count
        for i, piece in enumerate(pieces):
            table[i * height : (i + 1) * height] = piece[...]
        code = row_codes(size, rows, table[...], picks_ref)
        codes[...] = code
        own_code[...] = codes[pl.ds(pl.multiple_of(lax.axis_index("latent") * rows, rows), rows)]
        tokens = lax.broadcasted_iota(jnp.int32, by_latent.shape, 1)
        by_latent[...] = jnp.where(
            code == KEPT, coef_ref[...].T, (tokens == code).astype(by_latent.dtype)
        )
        ordered_rows(size, rows, by_latent, by_slot)

    multiply(by_slot, right_ref, outs)


def select_product(coef, right, size, rows, picks, table):
    tokens, latents = coef.shape
    width = right.shape[1]
    tile = 512
    part = latents // 4
    fixed = lambda j: (0, 0)
    operands = [coef, right, picks] + list(table)
    in_specs = [pl.BlockSpec(value.shape, fixed) for value in operands]
    in_specs[1] = pl.BlockSpec((tokens, tile), lambda j: (0, j))
    return pl.pallas_call(
        functools.partial(select_kernel, size, rows, len(table)),
        grid=(width // tile,),
        in_specs=in_specs,
        out_specs=[pl.BlockSpec((part, tile), lambda j: (0, j))] * 4
        + [pl.BlockSpec((rows, 1), fixed)],
        out_shape=[jax.ShapeDtypeStruct((part, width), coef.dtype)] * 4
        + [jax.ShapeDtypeStruct((rows, 1), jnp.int32)],
        scratch_shapes=[
            pltpu.VMEM((latents, tokens), coef.dtype),
            pltpu.VMEM((latents, tokens), coef.dtype),
            pltpu.VMEM((size, table[0].shape[1]), jnp.int32),
            pltpu.VMEM((latents, 1), jnp.int32),
        ],
        compiler_params=params(24),
        cost_estimate=cost(
            2 * latents * tokens * width, 2 * (tokens * width + latents * (tokens + width))
        ),
        name="select_product",
    )(*operands)


def term(kept, from_core, slot, rows):
    slots = kept[0].shape[0] // rows
    group, begin = slot // slots, slot % slots * rows
    pair = (kept[group], from_core[group])
    return sum(value[begin : begin + rows].astype(jnp.float32) for value in pair)


def updated(refs):
    code, states, terms = refs[0], refs[1:7], refs[7:15]
    reset = code[...] != KEPT
    enc_grad, dec_grad = (
        sum(ref[...].astype(jnp.float32) for ref in half) for half in (terms[:4], terms[4:])
    )
    enc = adam_update(*(ref[...] for ref in states[:3]), enc_grad)
    dec = adam_update(*(ref[...] for ref in states[3:]), dec_grad)
    enc_w = jnp.where(reset, reset_gain * enc_grad * inverse_rms(enc_grad), enc[0])
    dec_w = jnp.where(reset, enc_grad, dec[0])
    dec_w = dec_w * inverse_rms(dec_w)
    moments = [jnp.where(reset, 0.0, value) for value in enc[1:] + dec[1:]]
    return [enc_w] + moments[:2] + [dec_w] + moments[2:]


def blocks_kernel(*refs):
    results, blocks = updated(refs), refs[-1]
    blocks[0] = results[0].astype(blocks.dtype)
    blocks[1] = results[3].astype(blocks.dtype)


def states_kernel(*refs):
    for ref, value in zip(refs[-6:], updated(refs)):
        ref[...] = value


def update(code, states, enc_parts, dec_parts, blocks_only):
    rows, width = states[0].shape
    tile = 16

    def row_tile(value, skipped):
        return pl.BlockSpec((tile, value.shape[1]), lambda i: (i + skipped // tile, 0))

    operands = [(value, 0) for value in [code] + list(states)]
    operands += [(value, value.shape[0] - rows) for value in enc_parts + dec_parts]
    if blocks_only:
        out_shape = [jax.ShapeDtypeStruct((2, rows, width), jnp.bfloat16)]
        out_specs = [pl.BlockSpec((2, tile, width), lambda i: (0, i, 0))]
    else:
        out_shape = [jax.ShapeDtypeStruct((rows, width), jnp.float32)] * 6
        out_specs = [pl.BlockSpec((tile, width), lambda i: (i, 0))] * 6
    return pl.pallas_call(
        blocks_kernel if blocks_only else states_kernel,
        grid=(rows // tile,),
        in_specs=[row_tile(*operand) for operand in operands],
        out_specs=out_specs,
        out_shape=out_shape,
        cost_estimate=cost(10 * rows * width, 10 * rows * width),
        compiler_params=params(20),
        name="blocks" if blocks_only else "states",
    )(*(value for value, _ in operands))


def place_kernel(plan, size, rows, count, *refs):
    pieces, outs, sems = refs[:count], refs[-3:-1], refs[-1]
    copies = []
    for i, (offset, other_core, column) in enumerate(plan):
        start = pl.multiple_of(owner_at(offset, other_core, size) * rows, rows)
        for whole, out in enumerate(outs):
            source = pieces[i].at[pl.ds(whole * rows, rows)]
            target = out.at[pl.ds(start, rows), pl.ds(column, pieces[i].shape[1])]
            copies.append(pltpu.make_async_copy(source, target, sems.at[i, whole]))
    for copy in copies:
        copy.start()
    for copy in copies:
        copy.wait()


def place(pieces, wholes, size, rows, width):
    operands = [value for _, _, _, value in pieces]
    plan = [piece[:3] for piece in pieces]
    count = len(operands)
    first = wholes is None
    if not first:
        operands += list(wholes)
    anywhere = pl.BlockSpec(memory_space=pl.ANY)
    return pl.pallas_call(
        functools.partial(place_kernel, plan, size, rows, count),
        out_shape=[jax.ShapeDtypeStruct((size * rows, width), operands[0].dtype)] * 2,
        in_specs=[anywhere] * len(operands),
        out_specs=[anywhere] * 2,
        scratch_shapes=[pltpu.SemaphoreType.DMA((count, 2))],
        input_output_aliases={} if first else {count: 0, count + 1: 1},
        compiler_params=params(4),
        cost_estimate=cost(0, 8 * count * rows * width),
        name="place",
    )(*operands)


def gathered(block, order, size, rows):
    chips = size // 2
    width = block.shape[1]
    half = width // 2
    hops = chips // 2
    right = left = block
    near, far, wholes = [(0, 0, 0, after(block, order))], [], None
    for hop in range(1, hops + 1):
        if hop == hops:
            right, left = right[:, :half], left[:, half:]
        right, left = shift(right, 1, size), shift(left, -1, size)
        sent = [(offset, 1, column, swap(value, 1, size)) for offset, _, column, value in near]
        wholes = place(near + far, wholes, size, rows, width)
        far = sent
        right, wholes = tied(right, wholes)
        left = after(left, right)
        near = [(-hop, 0, 0, right), (hop, 0, half if hop == hops else 0, left)]
    sent = [(offset, 1, column, swap(value, 1, size)) for offset, _, column, value in near]
    wholes = place(near, wholes, size, rows, width)
    return place(far + sent, wholes, size, rows, width)


def shards(
    x_rows,
    out_grad,
    enc_coef,
    latent_act,
    enc_w,
    enc_m,
    enc_v,
    dec_w,
    dec_m,
    dec_v,
    dead_order,
    pick_rows,
    send_count,
):
    rows, width = enc_w.shape
    half = width // 2
    size = lax.axis_size("latent")
    chips = size // 2
    stages = gather_table(jnp.concatenate([send_count, dead_order], axis=1), size)
    table = stages[-1]
    def begin(kept, from_core):
        far = term(kept, from_core, 0, rows).astype(jnp.bfloat16)
        return [far[:, :half], far[:, half:]]

    def travel(moving):
        return [shift(moving[0], 1, size), shift(moving[1], -1, size)]

    def advance(came, kept, from_core, hop):
        moving = []
        for side, value in enumerate(came):
            value = value.astype(jnp.float32)
            if value.shape[1] < width:
                pads = ((0, 0, 0), (0, half, 0) if side == 0 else (half, 0, 0))
                value = lax.pad(value, jnp.float32(0), pads)
            value = value + term(kept, from_core, 2 * hop - side, rows)
            moving.append(value.astype(jnp.bfloat16))
        return moving

    dec = stream_product(latent_act, out_grad, size, rows)
    dec_far = after(dec[0], *stages[0])
    dec_kept, dec_core = [dec[1], dec[3]], [swap(dec_far, 1, size), swap(after(dec[2], table[0]), 1, size)]
    dec_moving = begin(dec_kept, after(dec_core, table[0]))
    *enc, code = select_product(
        after(enc_coef, *dec_moving), x_rows, size, rows, pick_rows[0].T, table
    )
    dec_came, enc_far = tied(travel(dec_moving), enc[0])
    enc_kept, enc_core = [enc[1], enc[3]], [swap(enc_far, 1, size), swap(enc[2], 1, size)]
    dec_moving = advance(dec_came, dec_kept, dec_core, 1)
    dec_came = travel(dec_moving)
    enc_moving = begin(enc_kept, after(enc_core, *dec_moving))
    enc_came = travel(enc_moving)
    dec_came = after(dec_came, *enc_moving)
    for hop in range(1, chips // 2):
        if hop + 1 < chips // 2:
            dec_moving = advance(dec_came, dec_kept, dec_core, hop + 1)
            dec_came = dec_arrived = travel(dec_moving)
            enc_came = after(enc_came, *dec_moving)
        else:
            enc_came = after(enc_came, *dec_arrived)
        enc_moving = advance(enc_came, enc_kept, enc_core, hop)
        enc_came = travel(enc_moving)
        dec_came = after(dec_came, *enc_moving)
    states = (enc_w, enc_m, enc_v, dec_w, dec_m, dec_v)
    parts = ([enc_kept[1], enc_core[1]] + enc_came, [dec_kept[1], dec_core[1]] + dec_came)
    (blocks,) = update(code, states, *parts, True)
    results = update(code, after(states, blocks), *parts, False)
    enc_full, dec_full = gathered(blocks.reshape(2 * rows, width), results[0], size, rows)
    return (*results, enc_full, dec_full)


def solution(mesh):
    split = P(("groups", "latent"), None)
    placed = (split,) * 11 + (P(("groups", "latent"), None, None), split)
    return jax.shard_map(
        shards,
        mesh=mesh,
        in_specs=placed,
        out_specs=(split,) * 6 + (P("groups", None),) * 2,
        check_vma=False,
    )
```

```python
import functools

import jax
import jax.numpy as jnp
from jax import lax
from jax.experimental import pallas as pl
from jax.experimental.pallas import tpu as pltpu
from jax.sharding import PartitionSpec as P

beta_one = 0.9
beta_two = 0.99
first_fix = 1.0 - 0.9**4
second_fix = 1.0 - 0.99**4
learn_rate = 0.02
adam_eps = 1e-08
reset_gain = 0.01
norm_eps = 1e-06

KEPT = -1
ABSENT = -2


def adam_update(weight, moment, second, gradient):
    moment_new = beta_one * moment + (1.0 - beta_one) * gradient
    second_new = beta_two * second + (1.0 - beta_two) * gradient * gradient
    weight_new = weight - learn_rate * (moment_new / first_fix) / (
        jnp.sqrt(second_new / second_fix) + adam_eps
    )
    return (weight_new, moment_new, second_new)


def inverse_rms(value):
    return lax.rsqrt(jnp.mean(value * value, axis=1, keepdims=True) + norm_eps)


def swap(value, bits, size):
    return lax.ppermute(value, "latent", [(i, i ^ bits) for i in range(size)])


def after(value, *others):
    return lax.optimization_barrier((value,) + others)[0]


def tied(*values):
    return lax.optimization_barrier(values)


def params(mebibytes):
    return pltpu.CompilerParams(vmem_limit_bytes=mebibytes * 2**20)


def cost(flops, moved):
    return pl.CostEstimate(flops=int(flops), bytes_accessed=int(moved), transcendentals=0)


def chip_at(position, chips):
    return jnp.where(position < chips // 2, 2 * position, 2 * (chips - 1 - position) + 1)


def position_of(chip, chips):
    return jnp.where(chip % 2 == 0, chip // 2, chips - 1 - chip // 2)


def owner_at(offset, other_core, size):
    me = lax.axis_index("latent")
    chips = size // 2
    position = lax.rem(position_of(me // 2, chips) + offset + chips, chips)
    return 2 * chip_at(position, chips) + ((me % 2) ^ other_core)


def shift(value, step, size):
    chips = size // 2
    ring = [2 * q for q in range(chips // 2)] + [2 * q + 1 for q in reversed(range(chips // 2))]
    pairs = [
        (2 * ring[p] + core, 2 * ring[(p + step) % chips] + core)
        for p in range(chips)
        for core in range(2)
    ]
    return lax.ppermute(value, "latent", pairs)


def gather_table(row, size):
    stages, step = [], 1
    pieces = [row]
    while step < size:
        if step > 1:
            pieces = [jnp.concatenate(pieces, axis=0)]
        pieces += [swap(pieces[0], step * k, size) for k in range(1, min(4, size // step))]
        stages.append(pieces)
        step *= len(pieces)
    return stages


def ordered_rows(size, rows, by_latent, by_slot):
    chips = size // 2
    for block in range(size):
        group, inside = block // chips, block % chips
        slot = group * (chips // 2) + inside % (chips // 2)
        far = chips // 2 - slot // 2
        offset = far if slot % 2 == 0 else 1 - far
        owner = owner_at(offset, 1 - inside // (chips // 2), size)
        begin = pl.multiple_of(owner * rows, rows)
        by_slot[block * rows : (block + 1) * rows] = by_latent[pl.ds(begin, rows)]


def row_codes(size, rows, table, picks_ref):
    me = lax.axis_index("latent")
    counts = table[:, :size]
    order = table[:, size:]
    source = me ^ lax.broadcasted_iota(jnp.int32, (size, 1), 0)
    before = jnp.sum(jnp.where(source < me, counts, 0), axis=0, keepdims=True)
    total = jnp.sum(counts, axis=0, keepdims=True)
    owners = lax.broadcasted_iota(jnp.int32, (size, size), 1) == source

    def by_key(row):
        return jnp.sum(jnp.where(owners, row, 0), axis=1, keepdims=True)

    begin, here = by_key(before), by_key(counts[:1])
    place = lax.broadcasted_iota(jnp.int32, (size, rows), 1)
    token = jnp.full((size, rows), ABSENT, jnp.int32)
    for c in range(picks_ref.shape[0]):
        own = (place == begin + c) & (here > c)
        token = jnp.where(own, by_key(picks_ref[c : c + 1]), token)
    token = jnp.where(place < by_key(total), token, KEPT)
    latent = lax.broadcasted_iota(jnp.int32, (size * rows, 1), 0)
    keys = lax.broadcasted_iota(jnp.int32, (size * rows, size), 1)
    spread = (keys == (me ^ (latent // rows))).astype(jnp.float32)

    def by_row(values):
        return jnp.dot(spread, values.astype(jnp.float32), precision=lax.Precision.HIGHEST)

    is_latent = by_row(order) == (latent % rows).astype(jnp.float32)
    code = jnp.sum(jnp.where(is_latent, by_row(token), 0.0), axis=1, keepdims=True)
    return (code + jnp.where(code < 0, -0.5, 0.5)).astype(jnp.int32)


def multiply(by_slot, right_ref, outs):
    out = jnp.dot(by_slot[...], right_ref[...], preferred_element_type=jnp.float32)
    part = outs[0].shape[0]
    for i, ref in enumerate(outs):
        ref[...] = out[i * part : (i + 1) * part].astype(ref.dtype)


def stream_kernel(size, rows, coef_ref, right_hbm, *refs):
    outs, (right, by_latent, by_slot, stage, sems_in, sems_out) = refs[:4], refs[4:]
    tokens, width = right.shape
    part = outs[0].shape[0]
    pieces, cuts = sems_in.shape
    tile, height = width // pieces, tokens // cuts
    reads, writes = [], []
    for i in range(pieces):
        columns = pl.ds(i * tile, tile)
        reads.append([])
        for cut in range(cuts):
            span = pl.ds(cut * height, height)
            reads[i].append(
                pltpu.make_async_copy(
                    right_hbm.at[span, columns], right.at[span, columns], sems_in.at[i, cut]
                )
            )
        for group, out in enumerate(outs):
            source = stage.at[pl.ds(group * part, part), columns]
            writes.append(pltpu.make_async_copy(source, out.at[:, columns], sems_out.at[i, group]))
    for read in sum(reads, []):
        read.start()
    by_latent[...] = coef_ref[...].T
    ordered_rows(size, rows, by_latent, by_slot)
    for i in range(pieces):
        for read in reads[i]:
            read.wait()
        columns = slice(i * tile, (i + 1) * tile)
        out = jnp.dot(by_slot[...], right[:, columns], preferred_element_type=jnp.float32)
        stage[:, columns] = out.astype(stage.dtype)
        for write in writes[4 * i : 4 * i + 4]:
            write.start()
    for write in writes:
        write.wait()


def stream_product(coef, right, size, rows):
    tokens, latents = coef.shape
    width = right.shape[1]
    part = latents // 4
    pieces, cuts = 2, 8
    anywhere = pl.BlockSpec(memory_space=pl.ANY)
    return pl.pallas_call(
        functools.partial(stream_kernel, size, rows),
        in_specs=[pl.BlockSpec(memory_space=pltpu.VMEM), anywhere],
        out_specs=[anywhere] * 4,
        out_shape=[jax.ShapeDtypeStruct((part, width), coef.dtype)] * 4,
        scratch_shapes=[
            pltpu.VMEM((tokens, width), coef.dtype),
            pltpu.VMEM((latents, tokens), coef.dtype),
            pltpu.VMEM((latents, tokens), coef.dtype),
            pltpu.VMEM((latents, width), coef.dtype),
            pltpu.SemaphoreType.DMA((pieces, cuts)),
            pltpu.SemaphoreType.DMA((pieces, 4)),
        ],
        compiler_params=params(50),
        cost_estimate=cost(
            2 * latents * tokens * width, 2 * (tokens * width + latents * (tokens + width))
        ),
        name="product",
    )(coef, right)


def select_kernel(size, rows, count, coef_ref, right_ref, picks_ref, *refs):
    pieces, refs = refs[:count], refs[count:]
    outs, own_code, (by_latent, by_slot, table, codes) = refs[:4], refs[4], refs[5:]

    @pl.when(pl.program_id(0) == 0)
    def _():
        height = size // count
        for i, piece in enumerate(pieces):
            table[i * height : (i + 1) * height] = piece[...]
        code = row_codes(size, rows, table[...], picks_ref)
        codes[...] = code
        own_code[...] = codes[pl.ds(pl.multiple_of(lax.axis_index("latent") * rows, rows), rows)]
        tokens = lax.broadcasted_iota(jnp.int32, by_latent.shape, 1)
        by_latent[...] = jnp.where(
            code == KEPT, coef_ref[...].T, (tokens == code).astype(by_latent.dtype)
        )
        ordered_rows(size, rows, by_latent, by_slot)

    multiply(by_slot, right_ref, outs)


def select_product(coef, right, size, rows, picks, table):
    tokens, latents = coef.shape
    width = right.shape[1]
    tile = 512
    part = latents // 4
    fixed = lambda j: (0, 0)
    operands = [coef, right, picks] + list(table)
    in_specs = [pl.BlockSpec(value.shape, fixed) for value in operands]
    in_specs[1] = pl.BlockSpec((tokens, tile), lambda j: (0, j))
    return pl.pallas_call(
        functools.partial(select_kernel, size, rows, len(table)),
        grid=(width // tile,),
        in_specs=in_specs,
        out_specs=[pl.BlockSpec((part, tile), lambda j: (0, j))] * 4
        + [pl.BlockSpec((rows, 1), fixed)],
        out_shape=[jax.ShapeDtypeStruct((part, width), coef.dtype)] * 4
        + [jax.ShapeDtypeStruct((rows, 1), jnp.int32)],
        scratch_shapes=[
            pltpu.VMEM((latents, tokens), coef.dtype),
            pltpu.VMEM((latents, tokens), coef.dtype),
            pltpu.VMEM((size, table[0].shape[1]), jnp.int32),
            pltpu.VMEM((latents, 1), jnp.int32),
        ],
        compiler_params=params(24),
        cost_estimate=cost(
            2 * latents * tokens * width, 2 * (tokens * width + latents * (tokens + width))
        ),
        name="select_product",
    )(*operands)


def term(kept, from_core, slot, rows):
    slots = kept[0].shape[0] // rows
    group, begin = slot // slots, slot % slots * rows
    pair = (kept[group], from_core[group])
    return sum(value[begin : begin + rows].astype(jnp.float32) for value in pair)


def updated(refs):
    code, states, terms = refs[0], refs[1:7], refs[7:15]
    reset = code[...] != KEPT
    enc_grad, dec_grad = (
        sum(ref[...].astype(jnp.float32) for ref in half) for half in (terms[:4], terms[4:])
    )
    enc = adam_update(*(ref[...] for ref in states[:3]), enc_grad)
    dec = adam_update(*(ref[...] for ref in states[3:]), dec_grad)
    enc_w = jnp.where(reset, reset_gain * enc_grad * inverse_rms(enc_grad), enc[0])
    dec_w = jnp.where(reset, enc_grad, dec[0])
    dec_w = dec_w * inverse_rms(dec_w)
    moments = [jnp.where(reset, 0.0, value) for value in enc[1:] + dec[1:]]
    return [enc_w] + moments[:2] + [dec_w] + moments[2:]


def blocks_kernel(*refs):
    results, blocks = updated(refs), refs[-1]
    blocks[0] = results[0].astype(blocks.dtype)
    blocks[1] = results[3].astype(blocks.dtype)


def states_kernel(*refs):
    for ref, value in zip(refs[-6:], updated(refs)):
        ref[...] = value


def update(code, states, enc_parts, dec_parts, blocks_only):
    rows, width = states[0].shape
    tile = 16

    def row_tile(value, skipped):
        return pl.BlockSpec((tile, value.shape[1]), lambda i: (i + skipped // tile, 0))

    operands = [(value, 0) for value in [code] + list(states)]
    operands += [(value, value.shape[0] - rows) for value in enc_parts + dec_parts]
    if blocks_only:
        out_shape = [jax.ShapeDtypeStruct((2, rows, width), jnp.bfloat16)]
        out_specs = [pl.BlockSpec((2, tile, width), lambda i: (0, i, 0))]
    else:
        out_shape = [jax.ShapeDtypeStruct((rows, width), jnp.float32)] * 6
        out_specs = [pl.BlockSpec((tile, width), lambda i: (i, 0))] * 6
    return pl.pallas_call(
        blocks_kernel if blocks_only else states_kernel,
        grid=(rows // tile,),
        in_specs=[row_tile(*operand) for operand in operands],
        out_specs=out_specs,
        out_shape=out_shape,
        cost_estimate=cost(10 * rows * width, 10 * rows * width),
        compiler_params=params(20),
        name="blocks" if blocks_only else "states",
    )(*(value for value, _ in operands))


def place_kernel(plan, size, rows, count, *refs):
    pieces, outs, sems = refs[:count], refs[-3:-1], refs[-1]
    copies = []
    for i, (offset, other_core, column) in enumerate(plan):
        start = pl.multiple_of(owner_at(offset, other_core, size) * rows, rows)
        for whole, out in enumerate(outs):
            source = pieces[i].at[pl.ds(whole * rows, rows)]
            target = out.at[pl.ds(start, rows), pl.ds(column, pieces[i].shape[1])]
            copies.append(pltpu.make_async_copy(source, target, sems.at[i, whole]))
    for copy in copies:
        copy.start()
    for copy in copies:
        copy.wait()


def place(pieces, wholes, size, rows, width):
    operands = [value for _, _, _, value in pieces]
    plan = [piece[:3] for piece in pieces]
    count = len(operands)
    first = wholes is None
    if not first:
        operands += list(wholes)
    anywhere = pl.BlockSpec(memory_space=pl.ANY)
    return pl.pallas_call(
        functools.partial(place_kernel, plan, size, rows, count),
        out_shape=[jax.ShapeDtypeStruct((size * rows, width), operands[0].dtype)] * 2,
        in_specs=[anywhere] * len(operands),
        out_specs=[anywhere] * 2,
        scratch_shapes=[pltpu.SemaphoreType.DMA((count, 2))],
        input_output_aliases={} if first else {count: 0, count + 1: 1},
        compiler_params=params(4),
        cost_estimate=cost(0, 8 * count * rows * width),
        name="place",
    )(*operands)


def gathered(block, order, size, rows):
    chips = size // 2
    width = block.shape[1]
    half = width // 2
    hops = chips // 2
    right = left = block
    near, far, wholes = [(0, 0, 0, after(block, order))], [], None
    for hop in range(1, hops + 1):
        if hop == hops:
            right, left = right[:, :half], left[:, half:]
        right, left = shift(right, 1, size), shift(left, -1, size)
        sent = [(offset, 1, column, swap(value, 1, size)) for offset, _, column, value in near]
        wholes = place(near + far, wholes, size, rows, width)
        far = sent
        right, wholes = tied(right, wholes)
        left = after(left, right)
        near = [(-hop, 0, 0, right), (hop, 0, half if hop == hops else 0, left)]
    sent = [(offset, 1, column, swap(value, 1, size)) for offset, _, column, value in near]
    wholes = place(near, wholes, size, rows, width)
    return place(far + sent, wholes, size, rows, width)


def shards(
    x_rows,
    out_grad,
    enc_coef,
    latent_act,
    enc_w,
    enc_m,
    enc_v,
    dec_w,
    dec_m,
    dec_v,
    dead_order,
    pick_rows,
    send_count,
):
    rows, width = enc_w.shape
    half = width // 2
    size = lax.axis_size("latent")
    chips = size // 2
    stages = gather_table(jnp.concatenate([send_count, dead_order], axis=1), size)
    table = stages[-1]
    def begin(kept, from_core):
        far = term(kept, from_core, 0, rows).astype(jnp.bfloat16)
        return [far[:, :half], far[:, half:]]

    def travel(moving):
        return [shift(moving[0], 1, size), shift(moving[1], -1, size)]

    def advance(came, kept, from_core, hop):
        moving = []
        for side, value in enumerate(came):
            value = value.astype(jnp.float32)
            if value.shape[1] < width:
                pads = ((0, 0, 0), (0, half, 0) if side == 0 else (half, 0, 0))
                value = lax.pad(value, jnp.float32(0), pads)
            value = value + term(kept, from_core, 2 * hop - side, rows)
            moving.append(value.astype(jnp.bfloat16))
        return moving

    dec = stream_product(latent_act, out_grad, size, rows)
    dec_far = after(dec[0], *stages[0])
    dec_kept, dec_core = [dec[1], dec[3]], [swap(dec_far, 1, size), swap(after(dec[2], table[0]), 1, size)]
    dec_moving = begin(dec_kept, after(dec_core, table[0]))
    *enc, code = select_product(
        after(enc_coef, *dec_moving), x_rows, size, rows, pick_rows[0].T, table
    )
    dec_came, enc_far = tied(travel(dec_moving), enc[0])
    enc_kept, enc_core = [enc[1], enc[3]], [swap(enc_far, 1, size), swap(enc[2], 1, size)]
    dec_moving = advance(dec_came, dec_kept, dec_core, 1)
    dec_came = travel(dec_moving)
    enc_moving = begin(enc_kept, after(enc_core, *dec_moving))
    enc_came = travel(enc_moving)
    dec_came = after(dec_came, *enc_moving)
    for hop in range(1, chips // 2):
        if hop + 1 < chips // 2:
            dec_moving = advance(dec_came, dec_kept, dec_core, hop + 1)
            dec_came = travel(dec_moving)
            enc_came = after(enc_came, *dec_moving)
        enc_moving = advance(enc_came, enc_kept, enc_core, hop)
        enc_came = travel(enc_moving)
        dec_came = after(dec_came, *enc_moving)
    states = (enc_w, enc_m, enc_v, dec_w, dec_m, dec_v)
    parts = ([enc_kept[1], enc_core[1]] + enc_came, [dec_kept[1], dec_core[1]] + dec_came)
    (blocks,) = update(code, states, *parts, True)
    results = update(code, after(states, blocks), *parts, False)
    enc_full, dec_full = gathered(blocks.reshape(2 * rows, width), results[0], size, rows)
    return (*results, enc_full, dec_full)


def solution(mesh):
    split = P(("groups", "latent"), None)
    placed = (split,) * 11 + (P(("groups", "latent"), None, None), split)
    return jax.shard_map(
        shards,
        mesh=mesh,
        in_specs=placed,
        out_specs=(split,) * 6 + (P("groups", None),) * 2,
        check_vma=False,
    )
```
